128 devices in a mesh: fsdp: 32 (over z, x_hi, y), cp: 4 (over x_lo, core).
Axes of the slice: x: 4 (x_hi: 2, x_lo: 2; x = x_hi * 2 + x_lo), y: 4, z: 4, core: 2. Of those that a mesh axis runs over, the one named last changes fastest.
Arguments:
- video: bfloat16 [384, 4, 96, 512], P('fsdp', None, 'cp'), may hold values from -6 to 6
- conv_weight: bfloat16 [3, 3, 512, 512], replicated, may hold values from -0.09375 to 0.09375
- conv_bias: float32 [512], replicated, may hold values from -3 to 3
- time_weight: bfloat16 [3, 512, 512], replicated, may hold values from -0.15625 to 0.15625
- time_bias: float32 [512], replicated, may hold values from -3 to 3
- latent_weight: bfloat16 [512, 16], replicated, may hold values from -0.25 to 0.25
- latent_bias: float32 [16], replicated, may hold values from -3 to 3
- patch_weight: bfloat16 [64, 6144], replicated, may hold values from -0.75 to 0.75
- patch_bias: float32 [6144], replicated, may hold values from -3 to 3
- frame_pos: bfloat16 [8, 6144], replicated, may hold values from -3 to 3
- row_pos: bfloat16 [48, 6144], replicated, may hold values from -3 to 3
- col_pos: bfloat16 [48, 6144], replicated, may hold values from -3 to 3
- modulation: float32 [2, 6144], replicated, may hold values from -2 to 2
- qkv_weight: bfloat16 [3, 6144, 3072], P(None, 'fsdp', 'cp'), may hold values from -0.078125 to 0.078125
- qk_gain: float32 [2, 3072], P(None, 'cp'), may hold values from 0.1 to 1.9
Outputs:
- query: bfloat16 [18432, 3072], P('fsdp', 'cp')
- keys: bfloat16 [18432, 3072], P('fsdp', 'cp')
- values: bfloat16 [18432, 3072], P('fsdp', 'cp')
The draws below stay inside these ranges and needn't reach their ends.
All inputs are finite; a program needn't handle non-finite values.
Results may differ from the reference program's by a relative error of at most 0.008.
Values may be sent and summed in bfloat16 or wider, within the bound.
A program may use at most 256 MiB of HBM per device.

```python
import jax
import jax.numpy as jnp
from jax import lax

D = 6144
HEADS = 24
HD = 128
C = 512
LAT = 16
FR = 4
H = 96
W = 96
ROW_SPLIT = 2
COL_SPLIT = 4
WIN_SETS = 1
WINDOWS = 4
LF = 2
PH = 48
PW = 48
ROW_BLOCKS = 8
PATCH_ROWS = 3
PATCH_COLS = 3
TOKENS = 18432
N_CP = 4


def block_scale(stream_key, extent, split, smallest, top_value):
    level, own = 1.0, jax.random.fold_in(stream_key, 6)
    for axis_at, shards_of in split:
        heights = jnp.exp(jax.random.uniform(jax.random.fold_in(own, axis_at), (shards_of,), jnp.float32, smallest / len(split), top_value / len(split)))
        level = level * jnp.repeat(heights, extent[axis_at] // shards_of).reshape([-1 if axis == axis_at else 1 for axis in range(len(extent))])
    return level


def noise(stream_key, shape, scale, reach, split=(), kind=jnp.bfloat16):
    entries = scale * jax.random.normal(stream_key, shape, jnp.float32)
    if split:
        entries = entries * block_scale(stream_key, shape, split, -0.22, 0.18)
    return jnp.clip(entries, -reach, reach).astype(kind)


def setup_inputs(seed: int = 0) -> dict:
    splits = jax.random.split(jax.random.key(seed), 16)
    video = noise(splits[0], (FR * H, WINDOWS, W, C), 1.0, 6.0, ((0, 32), (2, 4)))
    conv_weight = noise(splits[1], (3, 3, C, C), (9 * C) ** -0.5, 0.09375)
    conv_bias = noise(splits[2], (C,), 0.5, 3.0, (), jnp.float32)
    time_weight = noise(splits[3], (3, C, C), (3 * C) ** -0.5, 0.15625)
    time_bias = noise(splits[4], (C,), 0.5, 3.0, (), jnp.float32)
    latent_weight = noise(splits[5], (C, LAT), C ** -0.5, 0.25)
    latent_bias = noise(splits[6], (LAT,), 0.5, 3.0, (), jnp.float32)
    patch_weight = noise(splits[7], (4 * LAT, D), (4 * LAT) ** -0.5, 0.75)
    patch_bias = noise(splits[8], (D,), 0.5, 3.0, (), jnp.float32)
    frame_pos = noise(splits[9], (WINDOWS * LF, D), 0.5, 3.0)
    row_pos = noise(splits[10], (PH, D), 0.5, 3.0)
    col_pos = noise(splits[11], (PW, D), 0.5, 3.0)
    modulation = noise(splits[12], (2, D), 0.3, 2.0, (), jnp.float32)
    qkv_weight = noise(splits[13], (3, D, HEADS * HD), D ** -0.5, 0.078125, ((1, 32), (2, 4)))
    qk_gain = jnp.clip(1.0 + 0.18 * jax.random.normal(splits[14], (2, HEADS * HD), jnp.float32), 0.1, 1.9)
    return {"video": video, "conv_weight": conv_weight, "conv_bias": conv_bias, "time_weight": time_weight, "time_bias": time_bias, "latent_weight": latent_weight, "latent_bias": latent_bias, "patch_weight": patch_weight, "patch_bias": patch_bias, "frame_pos": frame_pos, "row_pos": row_pos, "col_pos": col_pos, "modulation": modulation, "qkv_weight": qkv_weight, "qk_gain": qk_gain}


def head_norm(projected_part, gain_row):
    count = projected_part.shape[0]
    shaped = projected_part.reshape(count, HEADS, HD)
    scale = lax.rsqrt(lax.optimization_barrier(jnp.mean(shaped * shaped, axis=-1, keepdims=True)) + 1e-06)
    return ((shaped * scale).reshape(count, HEADS * HD) * gain_row).astype(jnp.bfloat16)

def reference(video, conv_weight, conv_bias, time_weight, time_bias, latent_weight, latent_bias, patch_weight, patch_bias, frame_pos, row_pos, col_pos, modulation, qkv_weight, qk_gain):
    frames = jnp.roll(video, -(H // 2), axis=0).reshape(FR, H, WINDOWS, W, C)
    active = jax.nn.silu(frames.astype(jnp.float32)).astype(jnp.bfloat16)
    padded = jnp.pad(active, ((0, 0), (1, 1), (0, 0), (1, 1), (0, 0)))
    running = frames.astype(jnp.float32) + conv_bias
    for row_shift in range(3):
        for col_shift in range(3):
            region = padded[:, row_shift:row_shift + H, :, col_shift:col_shift + W, :]
            running = running + jnp.dot(region, conv_weight[row_shift, col_shift], preferred_element_type=jnp.float32)
    spatial = running.astype(jnp.bfloat16)
    latents = []
    for latent_frame in range(LF):
        mixed = jnp.zeros((H, WINDOWS, W, C), jnp.float32) + time_bias
        for offset in range(3):
            source = 2 * latent_frame + offset - 1
            if 0 <= source < FR:
                mixed = mixed + jnp.dot(spatial[source], time_weight[offset], preferred_element_type=jnp.float32)
        mixed = mixed.astype(jnp.bfloat16)
        latents.append(jnp.dot(mixed, latent_weight, preferred_element_type=jnp.float32) + latent_bias)
    latent = jnp.stack(latents, axis=0)
    patch = latent.reshape(LF, PH, 2, WINDOWS, PW, 2, LAT).transpose(3, 0, 1, 4, 2, 5, 6)
    patch = patch.reshape(WINDOWS, LF, PH, PW, 4 * LAT).astype(jnp.bfloat16)
    embedded = jnp.dot(patch, patch_weight, preferred_element_type=jnp.float32) + patch_bias
    embedded = embedded + frame_pos.astype(jnp.float32).reshape(WINDOWS, LF, D)[:, :, None, None, :]
    embedded = embedded + row_pos.astype(jnp.float32)[None, None, :, None, :]
    embedded = embedded + col_pos.astype(jnp.float32)[None, None, None, :, :]
    center = lax.optimization_barrier(jnp.mean(embedded, axis=-1, keepdims=True))
    spread = lax.optimization_barrier(jnp.mean((embedded - center) ** 2, axis=-1, keepdims=True))
    scale_part = 1.0 + modulation[0]
    shift_part = modulation[1]
    normed = ((embedded - center) * lax.rsqrt(spread + 1e-06) * scale_part + shift_part).astype(jnp.bfloat16)
    groups = WINDOWS // WIN_SETS
    normed = normed.reshape(groups, WIN_SETS, LF, ROW_BLOCKS, ROW_SPLIT, PATCH_ROWS, N_CP, COL_SPLIT, PATCH_COLS, D)
    rows = normed.transpose(0, 4, 7, 6, 1, 2, 3, 5, 8, 9).reshape(TOKENS, D)
    outputs = []
    for which in range(3):
        projected = jnp.dot(rows, qkv_weight[which], preferred_element_type=jnp.float32)
        if which < 2:
            outputs.append(head_norm(projected, qk_gain[which]))
        else:
            outputs.append(projected.astype(jnp.bfloat16))
    return (outputs[0], outputs[1], outputs[2])
```

```python
import jax
import jax.numpy as jnp
from jax import lax
from jax.sharding import PartitionSpec as P

D = 6144
HD = 128
C = 512
LAT = 16
FR = 4
H = 96
ROW_SPLIT = 2
COL_SPLIT = 4
HIGHEST = lax.Precision.HIGHEST


def padded_2(cells, sides, width):
    for axis, dim in sides:
        count = lax.axis_size(axis)
        head = lax.slice_in_dim(cells, 0, width, axis=dim)
        tail = lax.slice_in_dim(cells, cells.shape[dim] - width, cells.shape[dim], axis=dim)
        cells = jnp.concatenate(
            [
                lax.ppermute(tail, axis, [(i, (i + 1) % count) for i in range(count)]),
                cells,
                lax.ppermute(head, axis, [((i + 1) % count, i) for i in range(count)]),
            ],
            axis=dim,
        )
    return cells


def head_norm(projected_part, gain_row):
    count = projected_part.shape[0]
    shaped = projected_part.reshape(count, -1, HD)
    scale = lax.rsqrt(jnp.mean(shaped * shaped, axis=-1, keepdims=True) + 1e-06)
    return ((shaped * scale).reshape(count, -1) * gain_row).astype(jnp.bfloat16)


def halves(values):
    high = values.astype(jnp.bfloat16)
    low = (values - high.astype(jnp.float32)).astype(jnp.bfloat16)
    return high, low


def body(
    video,
    conv_weight,
    conv_bias,
    time_weight,
    time_bias,
    latent_weight,
    latent_bias,
    patch_weight,
    patch_bias,
    frame_pos,
    row_pos,
    col_pos,
    modulation,
    qkv_weight,
    qk_gain,
):
    f32 = jnp.float32
    fsdp_count = lax.axis_size("fsdp")
    cp_count = lax.axis_size("cp")
    position = lax.axis_index("fsdp")
    column = lax.axis_index("cp")
    block_rows = video.shape[0]
    window_count = video.shape[1]
    col_block = video.shape[2]
    row_blocks = H // block_rows
    half_blocks = row_blocks // 2
    block_index = (position + row_blocks - half_blocks) % row_blocks
    frame = ((position + fsdp_count - half_blocks) % fsdp_count) // row_blocks
    tables = jnp.concatenate(
        [
            patch_weight.astype(f32),
            frame_pos.astype(f32) + patch_bias,
            row_pos.astype(f32),
            col_pos.astype(f32),
        ],
        axis=0,
    )
    centered = (tables - jnp.mean(tables, axis=1, keepdims=True)) * (1.0 + modulation[0])
    centered = jnp.concatenate([centered, modulation[1:2]], axis=0)
    own_rows = qkv_weight.shape[1]
    own = lax.dynamic_slice_in_dim(centered, position * own_rows, own_rows, 1)
    own_high, own_low = halves(own)
    parts = jnp.einsum(
        "tr,krh->tkh",
        jnp.concatenate([own_high, own_low], axis=0),
        qkv_weight,
        preferred_element_type=f32,
    )
    count = own.shape[0]
    panel = lax.psum(parts[:count] + parts[count:], "fsdp")
    folded = jnp.einsum(
        "jco,ol->jcl", time_weight, latent_weight, preferred_element_type=f32
    )
    zeros = jnp.zeros_like(folded[0])
    early = jnp.stack([folded[1], folded[2], zeros, zeros])
    late = jnp.stack([zeros, folded[0], folded[1], folded[2]])
    both = jnp.concatenate(
        [
            lax.dynamic_index_in_dim(early, frame, 0, False),
            lax.dynamic_index_in_dim(late, frame, 0, False),
        ],
        axis=1,
    )
    high, low = halves(both)
    wide = jnp.concatenate([high, low], axis=1)
    kernel = jnp.einsum("abco,ol->abcl", conv_weight, wide, preferred_element_type=f32)
    kernel = kernel[..., : 2 * LAT] + kernel[..., 2 * LAT :]
    kernel_high, kernel_low = halves(kernel)
    active = jax.nn.silu(video.astype(f32)).astype(jnp.bfloat16)
    padded = padded_2(active, (("fsdp", 0), ("cp", 2)), 1)
    row_ids = lax.broadcasted_iota(jnp.int32, (block_rows + 2, 1, 1, 1), 0)
    col_ids = lax.broadcasted_iota(jnp.int32, (1, 1, col_block + 2, 1), 2)
    dropped_rows = (row_ids == 0) & (block_index == 0) | (row_ids == block_rows + 1) & (
        block_index == row_blocks - 1
    )
    dropped_cols = (col_ids == 0) & (column == 0) | (col_ids == col_block + 1) & (
        column == cp_count - 1
    )
    padded = jnp.where(dropped_rows | dropped_cols, jnp.zeros((), jnp.bfloat16), padded)
    kernels = jnp.concatenate([kernel_high, kernel_low], axis=-1)
    kernels = kernels.transpose(2, 0, 1, 3).reshape(C, -1)
    through = jnp.dot(padded, kernels, preferred_element_type=f32)
    through = through.reshape(*padded.shape[:3], 3, 3, 2, 2 * LAT).sum(axis=5)
    direct = jnp.dot(video, wide, preferred_element_type=f32)
    running = direct[..., : 2 * LAT] + direct[..., 2 * LAT :]
    running = running + jnp.dot(conv_bias, both, precision=HIGHEST)
    for row_shift in range(3):
        for col_shift in range(3):
            running = running + through[
                row_shift : row_shift + block_rows,
                :,
                col_shift : col_shift + col_block,
                row_shift,
                col_shift,
            ]
    sub_rows = block_rows // ROW_SPLIT
    sub_cols = col_block // COL_SPLIT
    outgoing = running.reshape(ROW_SPLIT, sub_rows, window_count, COL_SPLIT, sub_cols, 2 * LAT)
    outgoing = outgoing.transpose(2, 0, 3, 1, 4, 5).reshape(fsdp_count, -1)
    tiles = lax.all_to_all(outgoing, "fsdp", split_axis=0, concat_axis=0, tiled=True)
    tiles = jnp.roll(tiles, -half_blocks, axis=0)
    half_rows = sub_rows // 2
    half_cols = sub_cols // 2
    tiles = tiles.reshape(FR, row_blocks, half_rows, 2, half_cols, 2, 2, LAT).sum(axis=0)
    offset = jnp.dot(time_bias, latent_weight.astype(f32), precision=HIGHEST) + latent_bias
    tiles = tiles + offset
    patches = tiles.transpose(5, 0, 1, 3, 2, 4, 6).reshape(-1, 4 * LAT).astype(jnp.bfloat16)
    row_part = position // COL_SPLIT % ROW_SPLIT
    col_part = position % COL_SPLIT
    group_index = position // (ROW_SPLIT * COL_SPLIT)

    def select(frames, rows, cols):
        width = frames.shape[-1]
        frames = lax.dynamic_slice_in_dim(frames, group_index * 2, 2, 0)
        rows = lax.dynamic_index_in_dim(
            rows.reshape(row_blocks, ROW_SPLIT, half_rows, width), row_part, 1, False
        )
        cols = lax.dynamic_index_in_dim(
            cols.reshape(cp_count, COL_SPLIT, half_cols, width), col_part, 1, False
        )
        return frames, rows, cols

    def embed(values, weight, frames, rows, cols):
        base = jnp.dot(values, weight, preferred_element_type=f32, precision=HIGHEST)
        shaped = base.reshape(cols.shape[0], 2, row_blocks, half_rows, half_cols, -1)
        shaped = shaped + frames[None, :, None, None, None, :]
        shaped = shaped + rows[None, None, :, :, None, :]
        shaped = shaped + cols[:, None, None, None, :, :]
        return shaped.reshape(base.shape)

    frames, rows, cols = select(frame_pos.astype(f32) + patch_bias, row_pos, col_pos)
    own_cols = lax.dynamic_slice_in_dim(cols, column, 1, 0)
    embedded = embed(patches, patch_weight, frames, rows.astype(f32), own_cols.astype(f32))
    center = jnp.mean(embedded, axis=-1, keepdims=True)
    spread = jnp.mean((embedded - center) ** 2, axis=-1, keepdims=True)
    scale = lax.rsqrt(spread + 1e-06)
    packed = jnp.concatenate([patches.astype(f32), scale], axis=1)
    packed = lax.all_gather(packed, "cp", axis=0, tiled=True)
    panel = panel.reshape(count, -1)
    heads = qkv_weight.shape[2]
    frames, rows, cols = select(panel[64:72], panel[72:120], panel[120:168])
    projected = embed(packed[:, :64], panel[:64], frames, rows, cols)
    projected = projected * packed[:, 64:65] + panel[168]
    query = head_norm(projected[:, :heads], qk_gain[0])
    keys = head_norm(projected[:, heads : 2 * heads], qk_gain[1])
    values = projected[:, 2 * heads :].astype(jnp.bfloat16)
    return (query, keys, values)


def solution(mesh):
    return jax.shard_map(
        body,
        mesh=mesh,
        in_specs=(
            P("fsdp", None, "cp", None),
            P(),
            P(),
            P(),
            P(),
            P(),
            P(),
            P(),
            P(),
            P(),
            P(),
            P(),
            P(),
            P(None, "fsdp", "cp"),
            P(None, "cp"),
        ),
        out_specs=(P("fsdp", "cp"), P("fsdp", "cp"), P("fsdp", "cp")),
        check_vma=False,
    )
```

```python
import functools

import jax
import jax.numpy as jnp
from jax import lax
from jax.experimental import pallas as pl
from jax.experimental.pallas import tpu as pltpu
from jax.sharding import PartitionSpec as P

MESH = pl.DeviceIdType.MESH
F32 = jnp.float32
BF16 = jnp.bfloat16
HIGHEST = lax.Precision.HIGHEST

D = 6144
HD = 128
C = 512
LAT = 16
FR = 4
LANES = 128
GROUP = 16
N_FSDP = 32
N_CP = 4
WINDOWS = 4
ROWS = 12
COLS = 24
ROW_BLOCKS = 8
ROW_SPLIT = 2
COL_SPLIT = 4
PATCH = 3
CELLS = ROW_BLOCKS * PATCH * PATCH
WIDE = WINDOWS * COLS
PW_ROWS = 64
POS_ROWS = 48
TABLE_ROWS = PW_ROWS + 2 * POS_ROWS + GROUP
KEPT = PW_ROWS + TABLE_ROWS
GROUPS = TABLE_ROWS // GROUP
SHIFT_ROW = 11
HEAD_TILES = 18
PIECE = 7
TILES = N_FSDP * PIECE
OWN = D // N_FSDP


def split_2(values):
    high = values.astype(BF16)
    low = (values - high.astype(F32)).astype(BF16)
    return high, low


def place(shape):
    return [lax.broadcasted_iota(jnp.int32, shape, axis) for axis in range(len(shape))]


def token_coefs(cells, fsdp, column):
    group, row_part, col_part = fsdp // 8, fsdp // 4 % 2, fsdp % 4
    cell, lane = place((CELLS, LANES))
    block, inner = cell // 9, cell % 9
    row = block * 6 + row_part * PATCH + inner // PATCH
    col = column * 12 + col_part * PATCH + inner % PATCH
    base = (lane == row) | (lane == POS_ROWS + col)
    base = base | ((lane >= 2 * POS_ROWS + 8) & (lane < 2 * POS_ROWS + SHIFT_ROW))
    coefs = []
    for late in range(2):
        hot = base | (lane == 2 * POS_ROWS + group * 2 + late)
        kept = (lane // PW_ROWS) == late
        coefs.append(
            jnp.concatenate(
                [jnp.where(kept, cells, 0.0), jnp.where(hot, 1.0, 0.0)[:, : KEPT - LANES]],
                axis=1,
            )
        )
    return jnp.concatenate(coefs, axis=0).astype(BF16)


def exchange_kernel(
    video,
    conv_weight,
    conv_bias,
    time_weight,
    time_bias,
    latent_weight,
    latent_bias,
    patch_weight,
    patch_bias,
    frame_pos,
    row_pos,
    col_pos,
    modulation,
    weight,
    panel_out,
    cells_out,
    tables,
    video_in,
    conv_in,
    time_in,
    left_side,
    parts,
    arrived,
    piece,
    folded,
    kernels,
    q0,
    q1,
    q2,
    direct,
    edge_out,
    edge_in,
    padded,
    spread_out,
    messages,
    latents_in,
    sums,
    cells,
    embedded,
    token_out,
    local_sems,
    sums_sems,
    panel_sems,
    edge_send,
    edge_recv,
    tile_sems,
    cell_sems,
):
    me = lax.axis_index("fsdp")
    column = lax.axis_index("cp")
    barrier = pltpu.get_barrier_semaphore()

    def greet(step, carry):
        pl.semaphore_signal(
            barrier, inc=1, device_id={"fsdp": (me + step) % N_FSDP}, device_id_type=MESH
        )
        return carry

    lax.fori_loop(1, N_FSDP, greet, 0)
    for step in range(1, N_CP):
        pl.semaphore_signal(
            barrier, inc=1, device_id={"cp": (column + step) % N_CP}, device_id_type=MESH
        )
    loads = [
        pltpu.make_async_copy(source, target, local_sems.at[at])
        for at, (source, target) in enumerate(
            [
                (patch_weight, tables.at[pl.ds(PW_ROWS, PW_ROWS)]),
                (row_pos, tables.at[pl.ds(2 * PW_ROWS, POS_ROWS)]),
                (col_pos, tables.at[pl.ds(2 * PW_ROWS + POS_ROWS, POS_ROWS)]),
                (time_weight, time_in),
                (conv_weight, conv_in),
                (video, video_in),
                (patch_weight, tables.at[pl.ds(0, PW_ROWS)]),
            ]
        )
    ]
    for load in loads:
        load.start()

    bias = patch_bias[...]
    bias_high = bias.astype(BF16).astype(F32)
    bias_mid = (bias - bias_high).astype(BF16).astype(F32)
    bias_low = bias - bias_high - bias_mid
    eight = lax.broadcasted_iota(jnp.int32, (8, D), 0)
    tail = jnp.where(
        eight == 0,
        bias_high,
        jnp.where(eight == 1, bias_mid, jnp.where(eight == 2, bias_low, 0.0)),
    )
    tables[pl.ds(KEPT - GROUP, GROUP), :] = jnp.concatenate(
        [frame_pos[...].astype(F32), tail], axis=0
    ).astype(BF16)
    for load in loads[:3]:
        load.wait()
    start = pl.multiple_of((me // 2) * (2 * OWN), 2 * OWN)
    odd = me % 2 == 1
    own_mod = modulation[:, pl.ds(start, 2 * OWN)]
    own_scale = 1.0 + own_mod[0:1]
    own_shift = own_mod[1:2]

    def scaled(group, carry):
        at = pl.multiple_of(PW_ROWS + group * GROUP, GROUP)
        whole = tables[pl.ds(at, GROUP), :].astype(F32)
        center = jnp.sum(whole, axis=1, keepdims=True) * (1.0 / D)
        block = tables[pl.ds(at, GROUP), pl.ds(start, 2 * OWN)].astype(F32)
        block = (block - center) * own_scale
        row = lax.broadcasted_iota(jnp.int32, block.shape, 0)
        block = jnp.where((row == SHIFT_ROW) & (group == GROUPS - 1), own_shift, block)
        block = jnp.where(odd, block[:, OWN:], block[:, :OWN])
        high, low = split_2(block)
        to = pl.multiple_of(group * GROUP, GROUP)
        left_side[pl.ds(to, GROUP), :] = high
        left_side[pl.ds(TABLE_ROWS + to, GROUP), :] = low
        return carry

    lax.fori_loop(0, GROUPS, scaled, 0)
    for which in range(3):
        for pair in range(3):
            part = jnp.dot(
                left_side[...],
                weight[which, :, pair * 256 : (pair + 1) * 256],
                preferred_element_type=F32,
            )
            part = part[:TABLE_ROWS] + part[TABLE_ROWS:]
            for half in range(2):
                tile = which * 6 + pair * 2 + half
                parts[pl.ds(tile * GROUPS, GROUPS)] = (
                    part[:, half * LANES : (half + 1) * LANES]
                    .astype(BF16)
                    .reshape(GROUPS, GROUP, LANES)
                )
    spare = TILES - HEAD_TILES * GROUPS
    parts[pl.ds(HEAD_TILES * GROUPS, spare)] = jnp.zeros((spare, GROUP, LANES), BF16)
    pl.semaphore_wait(barrier, N_FSDP - 1 + N_CP - 1)

    def part_copy(step):
        target = (me + step) % N_FSDP
        return pltpu.make_async_remote_copy(
            src_ref=parts.at[pl.ds(target * PIECE, PIECE)],
            dst_ref=arrived.at[N_FSDP - 1 - step],
            send_sem=sums_sems.at[0],
            recv_sem=sums_sems.at[1],
            device_id={"fsdp": target},
            device_id_type=MESH,
        )

    def send_part(step, carry):
        part_copy(step).start()
        return carry

    lax.fori_loop(1, N_FSDP, send_part, 0)

    frame = (me + N_FSDP - 4) % N_FSDP // ROW_BLOCKS
    channel, lane = place((LAT, LANES))
    latent_in = latent_weight[...]

    def spread(keep):
        return jnp.dot(
            latent_in, jnp.where(keep, 1.0, 0.0).astype(BF16), preferred_element_type=F32
        ).astype(BF16)

    early_index = jnp.minimum(frame + 1, 2)
    late_index = jnp.maximum(frame - 1, 0)
    early_keep = (frame <= 1) & (lane == channel)
    late_keep = (frame >= 1) & (lane == PW_ROWS + channel)
    loads[3].wait()
    both = jnp.dot(time_in[early_index], spread(early_keep), preferred_element_type=F32)
    both = both + jnp.dot(time_in[late_index], spread(late_keep), preferred_element_type=F32)
    high, low = split_2(both)
    folded[:, :LANES] = high
    folded[:, LANES:] = low
    bias_row = jnp.dot(conv_bias[...], both, precision=HIGHEST, preferred_element_type=F32)
    loads[4].wait()

    def fold(col_shift, carry):
        total = None
        for row_shift in range(3):
            through = jnp.dot(
                conv_in[row_shift, col_shift], folded[...], preferred_element_type=F32
            )
            through = through[:, :LANES] + through[:, LANES:]
            if row_shift:
                through = pltpu.roll(through, row_shift * LAT, 1)
            total = through if total is None else total + through
        high, low = split_2(total)
        kernels[col_shift, :, :LANES] = high
        kernels[col_shift, :, LANES:] = low
        return carry

    lax.fori_loop(0, 3, fold, 0)
    loads[5].wait()

    def convolve(row, carry):
        at = pl.multiple_of(row * WIDE, WIDE)
        raw = video_in[pl.ds(at, WIDE), :]
        wide = raw.astype(F32)
        active = (wide / (1.0 + jnp.exp(-wide))).astype(BF16)
        for col_shift, kept in enumerate((q0, q1, q2)):
            through = jnp.dot(active, kernels[col_shift], preferred_element_type=F32)
            kept[pl.ds(at, WIDE), :] = through[:, :LANES] + through[:, LANES:]
        plain = jnp.dot(raw, folded[...], preferred_element_type=F32)
        direct[pl.ds(at, WIDE), :] = plain[:, :LANES] + plain[:, LANES:] + bias_row
        return carry

    lax.fori_loop(0, ROWS, convolve, 0)
    lines = ROWS * WINDOWS
    edge_out[0] = q0[pl.ds(COLS - 1, lines, stride=COLS), :]
    edge_out[1] = q2[pl.ds(0, lines, stride=COLS), :]
    edges = [
        pltpu.make_async_remote_copy(
            src_ref=edge_out.at[side],
            dst_ref=edge_in.at[side],
            send_sem=edge_send.at[side],
            recv_sem=edge_recv.at[side],
            device_id={"cp": (column + step) % N_CP},
            device_id_type=MESH,
        )
        for side, step in ((0, 1), (1, N_CP - 1))
    ]
    for edge in edges:
        edge.start()
    empty = jnp.zeros((2 * WIDE, LANES), F32)
    padded[pl.ds(0, 2 * WIDE), :] = empty
    padded[pl.ds((ROWS + 2) * WIDE, 2 * WIDE), :] = empty
    pixel = lax.broadcasted_iota(jnp.int32, (WIDE, LANES), 0) % COLS

    def columns(row, carry):
        at = pl.multiple_of(row * WIDE, WIDE)
        here = pl.ds(at, WIDE)
        total = q1[here, :]
        total = total + jnp.where(pixel == 0, 0.0, pltpu.roll(q0[here, :], 1, 0))
        total = total + jnp.where(pixel == COLS - 1, 0.0, pltpu.roll(q2[here, :], WIDE - 1, 0))
        padded[pl.ds(pl.multiple_of(at + 2 * WIDE, WIDE), WIDE), :] = total
        return carry

    lax.fori_loop(0, ROWS, columns, 0)
    for edge in edges:
        edge.wait()
    first = pl.ds(2 * WIDE, lines, stride=COLS)
    last = pl.ds(2 * WIDE + COLS - 1, lines, stride=COLS)
    padded[first, :] = padded[first, :] + jnp.where(column > 0, edge_in[0], 0.0)
    padded[last, :] = padded[last, :] + jnp.where(column < N_CP - 1, edge_in[1], 0.0)
    own_lanes = lax.broadcasted_iota(jnp.int32, (WIDE, LANES), 1) % PW_ROWS < LAT

    def packed(row, parity):
        total = padded[pl.ds((row + 1) * WIDE, WIDE), :]
        total = total + pltpu.roll(
            padded[pl.ds((row + 2) * WIDE, WIDE), :], LANES - LAT, 1
        )
        total = total + pltpu.roll(
            padded[pl.ds((row + 3) * WIDE, WIDE), :], LANES - 2 * LAT, 1
        )
        if 0 <= row < ROWS:
            total = total + direct[pl.ds(row * WIDE, WIDE), :]
        spread_out[...] = jnp.where(own_lanes, total, 0.0)
        result = None
        for side in range(2):
            taken = spread_out[pl.ds(side, WIDE // 2, stride=2), :]
            shift = 2 * LAT * parity + LAT * side
            taken = pltpu.roll(taken, shift, 1) if shift else taken
            result = taken if result is None else result + taken
        return result

    def post(values, row_part, at):
        for window in range(WINDOWS):
            for part in range(COL_SPLIT):
                begin = window * COLS // 2 + part * PATCH
                messages[window * 8 + row_part * 4 + part, at : at + PATCH, :] = values[
                    begin : begin + PATCH
                ]

    messages[...] = jnp.zeros(messages.shape, F32)
    for pair in range(ROWS // 2):
        values = packed(2 * pair, 0) + packed(2 * pair + 1, 1)
        post(values, pair // PATCH, pair % PATCH * PATCH)
    post(packed(ROWS, 0), 0, PATCH * PATCH)
    post(packed(-1, 1), 1, PATCH * PATCH)
    slot = (me + N_FSDP - 4) % N_FSDP

    def tile_copy(step):
        target = (me + step) % N_FSDP
        return pltpu.make_async_remote_copy(
            src_ref=messages.at[target],
            dst_ref=latents_in.at[slot],
            send_sem=tile_sems.at[0],
            recv_sem=tile_sems.at[1],
            device_id={"fsdp": target},
            device_id_type=MESH,
        )

    def send_tile(step, carry):
        tile_copy(step).start()
        return carry

    lax.fori_loop(1, N_FSDP, send_tile, 0)
    latents_in[slot] = messages[me]

    def wait_all(ref, sem):
        view = ref.at[pl.ds(0, N_FSDP - 1)]
        pltpu.make_async_copy(view, view, sem).wait()

    wait_all(arrived, sums_sems.at[1])

    def add(step, total):
        return total + arrived[step].astype(F32)

    own = parts[pl.ds(me * PIECE, PIECE)].astype(F32)
    piece[...] = lax.fori_loop(0, N_FSDP - 1, add, own).astype(BF16)

    def panel_copy(step):
        return pltpu.make_async_remote_copy(
            src_ref=piece,
            dst_ref=panel_out.at[me],
            send_sem=panel_sems.at[0],
            recv_sem=panel_sems.at[1],
            device_id={"fsdp": (me + step) % N_FSDP},
            device_id_type=MESH,
        )

    def send_panel(step, carry):
        panel_copy(step).start()
        return carry

    lax.fori_loop(1, N_FSDP, send_panel, 0)
    panel_out[me] = piece[...]

    spread_all = spread(lane % LAT == channel).astype(F32)
    offset = jnp.dot(time_bias[...], spread_all, precision=HIGHEST, preferred_element_type=F32)
    offset = offset + jnp.dot(
        latent_bias[...],
        jnp.where(lane % LAT == channel, 1.0, 0.0),
        precision=HIGHEST,
        preferred_element_type=F32,
    )
    wait_all(latents_in, tile_sems.at[1])
    for block in range(ROW_BLOCKS):
        total = latents_in[block]
        for other in range(1, FR):
            total = total + latents_in[other * ROW_BLOCKS + block]
        sums[block] = total
    row_part = me // 4 % 2
    upper = jnp.where(row_part == 0, 1.0, 0.0)
    lower = 1.0 - upper
    nine = PATCH * PATCH
    for block in range(ROW_BLOCKS):
        cells[pl.ds(block * nine, nine), :] = sums[block, 0:nine, :]
        if block > 0:
            here = pl.ds(block * nine, PATCH)
            cells[here, :] = cells[here, :] + sums[block - 1, nine : nine + PATCH, :] * upper
        if block < ROW_BLOCKS - 1:
            here = pl.ds(block * nine + 2 * PATCH, PATCH)
            cells[here, :] = cells[here, :] + sums[block + 1, nine : nine + PATCH, :] * lower
    patches = (cells[...] + offset).astype(BF16).astype(F32)
    loads[6].wait()
    coefs = token_coefs(patches, me, column)
    wide = 512
    count = 2 * CELLS

    def embed(step, total):
        here = pl.ds(pl.multiple_of(step * wide, wide), wide)
        values = jnp.dot(coefs, tables[:, here], preferred_element_type=F32)
        embedded[:, here] = values
        return total + jnp.sum(values, axis=1, keepdims=True)

    center = lax.fori_loop(0, D // wide, embed, jnp.zeros((count, 1), F32)) * (1.0 / D)

    def deviate(step, total):
        here = pl.ds(pl.multiple_of(step * wide, wide), wide)
        values = embedded[:, here] - center
        return total + jnp.sum(values * values, axis=1, keepdims=True)

    spread_sum = lax.fori_loop(0, D // wide, deviate, jnp.zeros((count, 1), F32))
    scale = lax.rsqrt(spread_sum * (1.0 / D) + 1e-06)
    cell_lane = lax.broadcasted_iota(jnp.int32, (CELLS, LANES), 1)
    token_out[pl.ds(0, CELLS), :] = patches
    token_out[pl.ds(CELLS, CELLS), :] = jnp.where(
        cell_lane < PW_ROWS, scale[:CELLS], scale[CELLS:]
    )
    copies = [
        pltpu.make_async_remote_copy(
            src_ref=token_out,
            dst_ref=cells_out.at[column],
            send_sem=cell_sems.at[0],
            recv_sem=cell_sems.at[1],
            device_id={"cp": (column + step) % N_CP},
            device_id_type=MESH,
        )
        for step in range(1, N_CP)
    ]
    for copy in copies:
        copy.start()
    cells_out[column] = token_out[...]
    others = cells_out.at[pl.ds(0, N_CP - 1)]
    pltpu.make_async_copy(others, others, cell_sems.at[1]).wait()
    pltpu.make_async_copy(others, others, cell_sems.at[0]).wait()
    wait_all(arrived, sums_sems.at[0])
    wait_all(latents_in, tile_sems.at[0])
    wait_all(panel_out, panel_sems.at[0])
    wait_all(panel_out, panel_sems.at[1])


def exchange(*args):
    whole = pl.BlockSpec(memory_space=pltpu.VMEM)
    apart = pl.BlockSpec(memory_space=pl.ANY)
    in_specs = [
        apart,
        apart,
        whole,
        apart,
        whole,
        whole,
        whole,
        apart,
        whole,
        whole,
        apart,
        apart,
        whole,
        whole,
    ]
    pixels = ROWS * WIDE
    return pl.pallas_call(
        exchange_kernel,
        out_shape=(
            jax.ShapeDtypeStruct((N_FSDP, PIECE, GROUP, LANES), BF16),
            jax.ShapeDtypeStruct((N_CP, 2 * CELLS, LANES), F32),
        ),
        in_specs=in_specs,
        out_specs=(whole, whole),
        scratch_shapes=[
            pltpu.VMEM((KEPT, D), BF16),
            pltpu.VMEM((pixels, C), BF16),
            pltpu.VMEM((3, 3, C, C), BF16),
            pltpu.VMEM((3, C, C), BF16),
            pltpu.VMEM((2 * TABLE_ROWS, OWN), BF16),
            pltpu.VMEM((TILES, GROUP, LANES), BF16),
            pltpu.VMEM((N_FSDP - 1, PIECE, GROUP, LANES), BF16),
            pltpu.VMEM((PIECE, GROUP, LANES), BF16),
            pltpu.VMEM((C, 2 * LANES), BF16),
            pltpu.VMEM((3, C, 2 * LANES), BF16),
            pltpu.VMEM((pixels, LANES), F32),
            pltpu.VMEM((pixels, LANES), F32),
            pltpu.VMEM((pixels, LANES), F32),
            pltpu.VMEM((pixels, LANES), F32),
            pltpu.VMEM((2, ROWS * WINDOWS, LANES), F32),
            pltpu.VMEM((2, ROWS * WINDOWS, LANES), F32),
            pltpu.VMEM(((ROWS + 4) * WIDE, LANES), F32),
            pltpu.VMEM((WIDE, LANES), F32),
            pltpu.VMEM((N_FSDP, GROUP, LANES), F32),
            pltpu.VMEM((N_FSDP, GROUP, LANES), F32),
            pltpu.VMEM((ROW_BLOCKS, GROUP, LANES), F32),
            pltpu.VMEM((CELLS, LANES), F32),
            pltpu.VMEM((2 * CELLS, D), F32),
            pltpu.VMEM((2 * CELLS, LANES), F32),
            pltpu.SemaphoreType.DMA((7,)),
            pltpu.SemaphoreType.DMA((2,)),
            pltpu.SemaphoreType.DMA((2,)),
            pltpu.SemaphoreType.DMA((2,)),
            pltpu.SemaphoreType.DMA((2,)),
            pltpu.SemaphoreType.DMA((2,)),
            pltpu.SemaphoreType.DMA((2,)),
        ],
        compiler_params=pltpu.CompilerParams(
            collective_id=0, has_side_effects=True, vmem_limit_bytes=48 * 1024 * 1024
        ),
    )(*args)


def project_kernel(cells, panel, gain, query, keys, values, coefs, scales):
    me = lax.axis_index("fsdp")
    step = pl.program_id(0)
    count = 2 * CELLS

    @pl.when(step == 0)
    def _():
        for column in range(N_CP):
            both = cells[column]
            coefs[pl.ds(column * count, count), :] = token_coefs(both[:CELLS], me, column)
            scale = both[CELLS:]
            lane = lax.broadcasted_iota(jnp.int32, scale.shape, 1)
            turned = pltpu.roll(scale, PW_ROWS, 1)
            scales[pl.ds(column * count, CELLS), :] = jnp.where(lane < PW_ROWS, scale, turned)
            scales[pl.ds(column * count + CELLS, CELLS), :] = jnp.where(
                lane < PW_ROWS, turned, scale
            )

    for which, out in enumerate((query, keys, values)):
        sides = []
        for half in range(2):
            tile = which * 6 + step * 2 + half
            rows = panel[pl.ds(pl.multiple_of(tile * TABLE_ROWS, GROUP), TABLE_ROWS), :]
            sides.append(rows)
        both = jnp.concatenate(sides, axis=1)
        stacked = jnp.concatenate([both[:PW_ROWS], both], axis=0)
        shift_at = TABLE_ROWS - GROUP
        shift = both[shift_at:].astype(F32)[SHIFT_ROW : SHIFT_ROW + 1]
        for column in range(N_CP):
            here = pl.ds(column * count, count)
            projected = jnp.dot(coefs[here, :], stacked, preferred_element_type=F32)
            scale = scales[here, :]
            for half in range(2):
                side = slice(half * LANES, (half + 1) * LANES)
                part = projected[:, side] * scale + shift[:, side]
                if which < 2:
                    power = jnp.sum(part * part, axis=1, keepdims=True) * (1.0 / HD)
                    part = part * lax.rsqrt(power + 1e-06) * gain[which : which + 1, side]
                out[here, side] = part.astype(BF16)


def project(cells, panel, gain, tokens):
    width = 2 * LANES
    out = jax.ShapeDtypeStruct((tokens, gain.shape[1]), BF16)
    block = pl.BlockSpec((tokens, width), lambda step: (0, step))
    return pl.pallas_call(
        project_kernel,
        grid=(3,),
        out_shape=(out, out, out),
        in_specs=[
            pl.BlockSpec(cells.shape, lambda step: (0, 0, 0)),
            pl.BlockSpec(panel.shape, lambda step: (0, 0)),
            pl.BlockSpec((2, width), lambda step: (0, step)),
        ],
        out_specs=(block, block, block),
        scratch_shapes=[
            pltpu.VMEM((tokens, KEPT), BF16),
            pltpu.VMEM((tokens, LANES), F32),
        ],
        compiler_params=pltpu.CompilerParams(vmem_limit_bytes=32 * 1024 * 1024),
    )(cells, panel, gain)


def body(
    video,
    conv_weight,
    conv_bias,
    time_weight,
    time_bias,
    latent_weight,
    latent_bias,
    patch_weight,
    patch_bias,
    frame_pos,
    row_pos,
    col_pos,
    modulation,
    qkv_weight,
    qk_gain,
):
    panel, cells = exchange(
        video.reshape(-1, C),
        conv_weight,
        conv_bias.reshape(1, -1),
        time_weight,
        time_bias.reshape(1, -1),
        latent_weight,
        latent_bias.reshape(1, -1),
        patch_weight,
        patch_bias.reshape(1, -1),
        frame_pos,
        row_pos,
        col_pos,
        modulation,
        qkv_weight,
    )
    return project(cells, panel.reshape(-1, LANES), qk_gain, N_CP * 2 * CELLS)


def solution(mesh):
    return jax.shard_map(
        body,
        mesh=mesh,
        in_specs=(
            P("fsdp", None, "cp", None),
            P(),
            P(),
            P(),
            P(),
            P(),
            P(),
            P(),
            P(),
            P(),
            P(),
            P(),
            P(),
            P(None, "fsdp", "cp"),
            P(None, "cp"),
        ),
        out_specs=(P("fsdp", "cp"), P("fsdp", "cp"), P("fsdp", "cp")),
        check_vma=False,
    )
```

```python
import functools

import jax
import jax.numpy as jnp
from jax import lax
from jax.experimental import pallas as pl
from jax.experimental.pallas import tpu as pltpu
from jax.sharding import PartitionSpec as P

MESH = pl.DeviceIdType.MESH
F32 = jnp.float32
BF16 = jnp.bfloat16
HIGHEST = lax.Precision.HIGHEST

D = 6144
HD = 128
C = 512
LAT = 16
FR = 4
LANES = 128
GROUP = 16
N_FSDP = 32
N_CP = 4
WINDOWS = 4
ROWS = 12
COLS = 24
ROW_BLOCKS = 8
ROW_SPLIT = 2
COL_SPLIT = 4
PATCH = 3
CELLS = ROW_BLOCKS * PATCH * PATCH
WIDE = WINDOWS * COLS
PW_ROWS = 64
POS_ROWS = 48
TABLE_ROWS = PW_ROWS + 2 * POS_ROWS + GROUP
KEPT = PW_ROWS + TABLE_ROWS
GROUPS = TABLE_ROWS // GROUP
SHIFT_ROW = 11
HEAD_TILES = 18
HALF_TILES = HEAD_TILES // 2 * GROUPS
QUARTER = 25
SMALL = 4
RING = 4
NEAR = 8
CELL_ROWS = 80
CHUNK = 4 * 96
OWN = D // N_FSDP


def split_2(values):
    high = values.astype(BF16)
    low = (values - high.astype(F32)).astype(BF16)
    return high, low


def place(shape):
    return [lax.broadcasted_iota(jnp.int32, shape, axis) for axis in range(len(shape))]


def token_coefs(cells, fsdp, column):
    group, row_part, col_part = fsdp // 8, fsdp // 4 % 2, fsdp % 4
    cell, lane = place((CELLS, LANES))
    block, inner = cell // 9, cell % 9
    row = block * 6 + row_part * PATCH + inner // PATCH
    col = column * 12 + col_part * PATCH + inner % PATCH
    base = (lane == row) | (lane == POS_ROWS + col)
    base = base | ((lane >= 2 * POS_ROWS + 8) & (lane < 2 * POS_ROWS + SHIFT_ROW))
    coefs = []
    for late in range(2):
        hot = base | (lane == 2 * POS_ROWS + group * 2 + late)
        kept = (lane // PW_ROWS) == late
        coefs.append(
            jnp.concatenate(
                [jnp.where(kept, cells, 0.0), jnp.where(hot, 1.0, 0.0)[:, : KEPT - LANES]],
                axis=1,
            )
        )
    return jnp.concatenate(coefs, axis=0).astype(BF16)


def exchange_kernel(
    video_far,
    conv_far,
    conv_bias_far,
    time_far,
    time_bias_far,
    latent_weight_far,
    latent_bias_far,
    patch_weight_far,
    patch_bias_far,
    frame_pos_far,
    row_pos_far,
    col_pos_far,
    modulation_far,
    weight_far,
    panel_out,
    cells_out,
    gram_out,
    tables,
    video_in,
    conv_in,
    time_in,
    weight,
    conv_bias,
    time_bias,
    latent_weight,
    latent_bias,
    patch_bias,
    frame_pos,
    modulation,
    centers,
    left_side,
    parts,
    ring_in,
    blocks,
    near_in,
    pieces,
    gathered,
    folded,
    kernels,
    q0,
    q1,
    q2,
    direct,
    edge_out,
    edge_in,
    padded,
    spread_out,
    messages,
    latents_in,
    sums,
    cells,
    token_out,
    local_sems,
    ring_sems,
    near_sems,
    spread_sems,
    panel_sems,
    edge_send,
    edge_recv,
    tile_sems,
    cell_sems,
):
    me = lax.axis_index("fsdp")
    column = lax.axis_index("cp")
    barrier = pltpu.get_barrier_semaphore()
    z_at, x_at, y_at = me // 8, me // 4 % 2, me % 4

    def ring_peer(half, step):
        if half == 0:
            return (z_at + step) % RING * 8 + me % 8
        return me // 4 * 4 + (y_at + step) % RING

    def near_at(half):
        return me % 8 if half == 0 else z_at * 2 + x_at

    def near_peer(half, target):
        if half == 0:
            return me // 8 * 8 + target
        return target // 2 * 8 + target % 2 * 4 + y_at

    ring_at = (z_at, y_at)

    def wait_bytes(view, sem):
        pltpu.make_async_copy(view, view, sem).wait()

    def greet(step, carry):
        pl.semaphore_signal(
            barrier, inc=1, device_id={"fsdp": (me + step) % N_FSDP}, device_id_type=MESH
        )
        return carry

    lax.fori_loop(1, N_FSDP, greet, 0)
    for step in range(1, N_CP):
        pl.semaphore_signal(
            barrier, inc=1, device_id={"cp": (column + step) % N_CP}, device_id_type=MESH
        )
    pairs = [
        (patch_weight_far, tables.at[pl.ds(PW_ROWS, PW_ROWS)]),
        (row_pos_far, tables.at[pl.ds(2 * PW_ROWS, POS_ROWS)]),
        (col_pos_far, tables.at[pl.ds(2 * PW_ROWS + POS_ROWS, POS_ROWS)]),
        (frame_pos_far, frame_pos),
        (patch_bias_far, patch_bias),
        (modulation_far, modulation),
        (weight_far, weight),
        (latent_weight_far, latent_weight),
        (conv_bias_far, conv_bias),
        (time_bias_far, time_bias),
        (latent_bias_far, latent_bias),
        (time_far, time_in),
        (conv_far, conv_in),
        (video_far, video_in),
        (patch_weight_far, tables.at[pl.ds(0, PW_ROWS)]),
    ]
    loads = [
        pltpu.make_async_copy(source, target, local_sems.at[at])
        for at, (source, target) in enumerate(pairs)
    ]
    for load in loads:
        load.start()

    for load in loads[:7]:
        load.wait()
    bias = patch_bias[...]
    bias_high = bias.astype(BF16).astype(F32)
    bias_mid = (bias - bias_high).astype(BF16).astype(F32)
    bias_low = bias - bias_high - bias_mid
    eight = lax.broadcasted_iota(jnp.int32, (8, D), 0)
    tail = jnp.where(
        eight == 0,
        bias_high,
        jnp.where(eight == 1, bias_mid, jnp.where(eight == 2, bias_low, 0.0)),
    )
    tables[pl.ds(KEPT - GROUP, GROUP), :] = jnp.concatenate(
        [frame_pos[...].astype(F32), tail], axis=0
    ).astype(BF16)
    start = pl.multiple_of((me // 2) * (2 * OWN), 2 * OWN)
    odd = me % 2 == 1
    own_mod = modulation[:, pl.ds(start, 2 * OWN)]
    own_scale = 1.0 + own_mod[0:1]
    own_shift = own_mod[1:2]

    def scaled(group, carry):
        at = pl.multiple_of(PW_ROWS + group * GROUP, GROUP)
        whole = tables[pl.ds(at, GROUP), :].astype(F32)
        center = jnp.sum(whole, axis=1, keepdims=True) * (1.0 / D)
        centers[pl.ds(at, GROUP), :] = jnp.broadcast_to(center, (GROUP, LANES))
        block = tables[pl.ds(at, GROUP), pl.ds(start, 2 * OWN)].astype(F32)
        block = (block - center) * own_scale
        row = lax.broadcasted_iota(jnp.int32, block.shape, 0)
        block = jnp.where((row == SHIFT_ROW) & (group == GROUPS - 1), own_shift, block)
        block = jnp.where(odd, block[:, OWN:], block[:, :OWN])
        high, low = split_2(block)
        to = pl.multiple_of(group * GROUP, GROUP)
        left_side[pl.ds(to, GROUP), :] = high
        left_side[pl.ds(TABLE_ROWS + to, GROUP), :] = low
        return carry

    lax.fori_loop(0, GROUPS, scaled, 0)
    for which in range(3):
        for pair in range(3):
            part = jnp.dot(
                left_side[...],
                weight[which, :, pair * 256 : (pair + 1) * 256],
                preferred_element_type=F32,
            )
            part = part[:TABLE_ROWS] + part[TABLE_ROWS:]
            for half in range(2):
                tile = which * 6 + pair * 2 + half
                at = tile % 9 * GROUPS
                parts[tile // 9, pl.ds(at, GROUPS)] = (
                    part[:, half * LANES : (half + 1) * LANES]
                    .astype(BF16)
                    .reshape(GROUPS, GROUP, LANES)
                )
    parts[:, HALF_TILES:] = jnp.zeros((2, 1, GROUP, LANES), BF16)
    pl.semaphore_wait(barrier, N_FSDP - 1 + N_CP - 1)

    ring_copies = []
    for step in (2, 1, 3):
        for half in range(2):
            target = (ring_at[half] + step) % RING
            ring_copies.append(
                pltpu.make_async_remote_copy(
                    src_ref=parts.at[half, pl.ds(target * QUARTER, QUARTER)],
                    dst_ref=ring_in.at[half, RING - 1 - step],
                    send_sem=ring_sems.at[half],
                    recv_sem=ring_sems.at[2 + half],
                    device_id={"fsdp": ring_peer(half, step)},
                    device_id_type=MESH,
                )
            )
    for copy in ring_copies:
        copy.start()

    frame = (me + N_FSDP - 4) % N_FSDP // ROW_BLOCKS
    channel, lane = place((LAT, LANES))
    for load in loads[7:11]:
        load.wait()
    latent_in = latent_weight[...]

    def spread(keep):
        return lax.dot_general(
            latent_in,
            jnp.where(keep, 1.0, 0.0).astype(BF16),
            (((0,), (0,)), ((), ())),
            preferred_element_type=F32,
        ).astype(BF16)

    early_index = jnp.minimum(frame + 1, 2)
    late_index = jnp.maximum(frame - 1, 0)
    early_keep = (frame <= 1) & (lane == channel)
    late_keep = (frame >= 1) & (lane == PW_ROWS + channel)
    loads[11].wait()
    both = jnp.dot(time_in[early_index], spread(early_keep), preferred_element_type=F32)
    both = both + jnp.dot(time_in[late_index], spread(late_keep), preferred_element_type=F32)
    high, low = split_2(both)
    folded[:, :LANES] = high
    folded[:, LANES:] = low
    bias_row = jnp.dot(conv_bias[...], both, precision=HIGHEST, preferred_element_type=F32)
    loads[12].wait()

    def fold(col_shift, carry):
        total = None
        for row_shift in range(3):
            through = jnp.dot(
                conv_in[row_shift, col_shift], folded[...], preferred_element_type=F32
            )
            through = through[:, :LANES] + through[:, LANES:]
            if row_shift:
                through = pltpu.roll(through, row_shift * LAT, 1)
            total = through if total is None else total + through
        high, low = split_2(total)
        kernels[col_shift, :, :LANES] = high
        kernels[col_shift, :, LANES:] = low
        return carry

    lax.fori_loop(0, 3, fold, 0)
    loads[13].wait()

    def convolve(row, carry):
        at = pl.multiple_of(row * CHUNK, CHUNK)
        raw = video_in[pl.ds(at, CHUNK), :]
        wide = raw.astype(F32)
        active = (wide / (1.0 + jnp.exp(-wide))).astype(BF16)
        for col_shift, kept in enumerate((q0, q1, q2)):
            through = jnp.dot(active, kernels[col_shift], preferred_element_type=F32)
            kept[pl.ds(at, CHUNK), :] = through[:, :LANES] + through[:, LANES:]
        plain = jnp.dot(raw, folded[...], preferred_element_type=F32)
        direct[pl.ds(at, CHUNK), :] = plain[:, :LANES] + plain[:, LANES:] + bias_row
        return carry

    lax.fori_loop(0, ROWS * WIDE // CHUNK, convolve, 0)
    lines = ROWS * WINDOWS
    edge_out[0] = q0[pl.ds(COLS - 1, lines, stride=COLS), :]
    edge_out[1] = q2[pl.ds(0, lines, stride=COLS), :]
    edges = [
        pltpu.make_async_remote_copy(
            src_ref=edge_out.at[side],
            dst_ref=edge_in.at[side],
            send_sem=edge_send.at[side],
            recv_sem=edge_recv.at[side],
            device_id={"cp": (column + step) % N_CP},
            device_id_type=MESH,
        )
        for side, step in ((0, 1), (1, N_CP - 1))
    ]
    for edge in edges:
        edge.start()
    near_copies = []
    for half in range(2):
        wait_bytes(ring_in.at[half], ring_sems.at[2 + half])
        total = parts[half, pl.ds(ring_at[half] * QUARTER, QUARTER)].astype(F32)
        for other in range(RING - 1):
            total = total + ring_in[half, other].astype(F32)
        blocks[half, pl.ds(0, QUARTER)] = total.astype(BF16)
        spare = NEAR * SMALL - QUARTER
        blocks[half, pl.ds(QUARTER, spare)] = jnp.zeros((spare, GROUP, LANES), BF16)
    for step in range(NEAR - 1, 0, -1):
        for half in range(2):
            target = (near_at(half) + step) % NEAR
            near_copies.append(
                pltpu.make_async_remote_copy(
                    src_ref=blocks.at[half, pl.ds(target * SMALL, SMALL)],
                    dst_ref=near_in.at[half, NEAR - 1 - step],
                    send_sem=near_sems.at[half],
                    recv_sem=near_sems.at[2 + half],
                    device_id={"fsdp": near_peer(half, target)},
                    device_id_type=MESH,
                )
            )
    for copy in near_copies:
        copy.start()
    empty = jnp.zeros((2 * WIDE, LANES), F32)
    padded[pl.ds(0, 2 * WIDE), :] = empty
    padded[pl.ds((ROWS + 2) * WIDE, 2 * WIDE), :] = empty
    pixel = lax.broadcasted_iota(jnp.int32, (WIDE, LANES), 0) % COLS

    def columns(row, carry):
        at = pl.multiple_of(row * WIDE, WIDE)
        here = pl.ds(at, WIDE)
        total = q1[here, :]
        total = total + jnp.where(pixel == 0, 0.0, pltpu.roll(q0[here, :], 1, 0))
        total = total + jnp.where(pixel == COLS - 1, 0.0, pltpu.roll(q2[here, :], WIDE - 1, 0))
        padded[pl.ds(pl.multiple_of(at + 2 * WIDE, WIDE), WIDE), :] = total
        return carry

    lax.fori_loop(0, ROWS, columns, 0)
    for edge in edges:
        edge.wait()
    first = pl.ds(2 * WIDE, lines, stride=COLS)
    last = pl.ds(2 * WIDE + COLS - 1, lines, stride=COLS)
    padded[first, :] = padded[first, :] + jnp.where(column > 0, edge_in[0], 0.0)
    padded[last, :] = padded[last, :] + jnp.where(column < N_CP - 1, edge_in[1], 0.0)
    own_lanes = lax.broadcasted_iota(jnp.int32, (WIDE, LANES), 1) % PW_ROWS < LAT

    def packed(row, parity):
        total = padded[pl.ds((row + 1) * WIDE, WIDE), :]
        total = total + pltpu.roll(
            padded[pl.ds((row + 2) * WIDE, WIDE), :], LANES - LAT, 1
        )
        total = total + pltpu.roll(
            padded[pl.ds((row + 3) * WIDE, WIDE), :], LANES - 2 * LAT, 1
        )
        if 0 <= row < ROWS:
            total = total + direct[pl.ds(row * WIDE, WIDE), :]
        spread_out[...] = jnp.where(own_lanes, total, 0.0)
        result = None
        for side in range(2):
            taken = spread_out[pl.ds(side, WIDE // 2, stride=2), :]
            shift = 2 * LAT * parity + LAT * side
            taken = pltpu.roll(taken, shift, 1) if shift else taken
            result = taken if result is None else result + taken
        return result

    def post(values, row_part, at):
        for window in range(WINDOWS):
            for part in range(COL_SPLIT):
                begin = window * COLS // 2 + part * PATCH
                messages[window * 8 + row_part * 4 + part, at : at + PATCH, :] = values[
                    begin : begin + PATCH
                ]

    messages[...] = jnp.zeros(messages.shape, F32)
    for pair in range(ROWS // 2):
        values = packed(2 * pair, 0) + packed(2 * pair + 1, 1)
        post(values, pair // PATCH, pair % PATCH * PATCH)
    post(packed(ROWS, 0), 0, PATCH * PATCH)
    post(packed(-1, 1), 1, PATCH * PATCH)
    slot = (me + N_FSDP - 4) % N_FSDP

    def tile_copy(step):
        target = (me + step) % N_FSDP
        return pltpu.make_async_remote_copy(
            src_ref=messages.at[target],
            dst_ref=latents_in.at[slot],
            send_sem=tile_sems.at[0],
            recv_sem=tile_sems.at[1],
            device_id={"fsdp": target},
            device_id_type=MESH,
        )

    def send_tile(step, carry):
        tile_copy(step).start()
        return carry

    lax.fori_loop(1, N_FSDP, send_tile, 0)
    latents_in[slot] = messages[me]

    spread_copies = []
    for half in range(2):
        wait_bytes(near_in.at[half], near_sems.at[2 + half])
        total = blocks[half, pl.ds(near_at(half) * SMALL, SMALL)].astype(F32)
        for other in range(NEAR - 1):
            total = total + near_in[half, other].astype(F32)
        pieces[half] = total.astype(BF16)
        gathered[half, pl.ds(near_at(half) * SMALL, SMALL)] = pieces[half]
    for step in range(NEAR - 1, 0, -1):
        for half in range(2):
            spread_copies.append(
                pltpu.make_async_remote_copy(
                    src_ref=pieces.at[half],
                    dst_ref=gathered.at[half, pl.ds(near_at(half) * SMALL, SMALL)],
                    send_sem=spread_sems.at[half],
                    recv_sem=spread_sems.at[2 + half],
                    device_id={"fsdp": near_peer(half, (near_at(half) + step) % NEAR)},
                    device_id_type=MESH,
                )
            )
    for copy in spread_copies:
        copy.start()

    loads[14].wait()
    centers[pl.ds(0, PW_ROWS), :] = centers[pl.ds(PW_ROWS, PW_ROWS), :]
    gram_out[...] = jnp.zeros((KEPT, KEPT), F32)
    both_last = (((1,), (1,)), ((), ()))

    def product(step, carry):
        here = pl.ds(pl.multiple_of(step * 1024, 1024), 1024)
        high, low = split_2(tables[:, here].astype(F32) - centers[:, :1])
        total = lax.dot_general(high, high, both_last, preferred_element_type=F32)
        cross = lax.dot_general(high, low, both_last, preferred_element_type=F32)
        gram_out[...] += (total + 2.0 * cross) * (1.0 / D)
        return carry

    lax.fori_loop(0, D // 1024, product, 0)
    panel_copies = []
    for half in range(2):
        wait_bytes(gathered.at[half, pl.ds(0, (NEAR - 1) * SMALL)], spread_sems.at[2 + half])
        at = half * RING * QUARTER + ring_at[half] * QUARTER
        for step in (2, 1, 3):
            panel_copies.append(
                pltpu.make_async_remote_copy(
                    src_ref=gathered.at[half, pl.ds(0, QUARTER)],
                    dst_ref=panel_out.at[pl.ds(at, QUARTER)],
                    send_sem=panel_sems.at[half],
                    recv_sem=panel_sems.at[2 + half],
                    device_id={"fsdp": ring_peer(half, step)},
                    device_id_type=MESH,
                )
            )
        for copy in panel_copies[-3:]:
            copy.start()
        panel_out[pl.ds(at, QUARTER)] = gathered[half, pl.ds(0, QUARTER)]

    spread_all = spread(lane % LAT == channel).astype(F32)
    offset = jnp.dot(time_bias[...], spread_all, precision=HIGHEST, preferred_element_type=F32)
    offset = offset + jnp.dot(
        latent_bias[...],
        jnp.where(lane % LAT == channel, 1.0, 0.0),
        precision=HIGHEST,
        preferred_element_type=F32,
    )
    wait_bytes(latents_in.at[pl.ds(0, N_FSDP - 1)], tile_sems.at[1])
    for block in range(ROW_BLOCKS):
        total = latents_in[block]
        for other in range(1, FR):
            total = total + latents_in[other * ROW_BLOCKS + block]
        sums[block] = total
    row_part = me // 4 % 2
    upper = jnp.where(row_part == 0, 1.0, 0.0)
    lower = 1.0 - upper
    nine = PATCH * PATCH
    for block in range(ROW_BLOCKS):
        cells[pl.ds(block * nine, nine), :] = sums[block, 0:nine, :]
        if block > 0:
            here = pl.ds(block * nine, PATCH)
            cells[here, :] = cells[here, :] + sums[block - 1, nine : nine + PATCH, :] * upper
        if block < ROW_BLOCKS - 1:
            here = pl.ds(block * nine + 2 * PATCH, PATCH)
            cells[here, :] = cells[here, :] + sums[block + 1, nine : nine + PATCH, :] * lower
    cells[pl.ds(CELLS, CELL_ROWS - CELLS), :] = jnp.zeros((CELL_ROWS - CELLS, LANES), F32)
    token_out[...] = (cells[...] + offset).astype(BF16)
    copies = [
        pltpu.make_async_remote_copy(
            src_ref=token_out,
            dst_ref=cells_out.at[column],
            send_sem=cell_sems.at[0],
            recv_sem=cell_sems.at[1],
            device_id={"cp": (column + step) % N_CP},
            device_id_type=MESH,
        )
        for step in range(1, N_CP)
    ]
    for copy in copies:
        copy.start()
    cells_out[column] = token_out[...]
    others = cells_out.at[pl.ds(0, N_CP - 1)]
    wait_bytes(others, cell_sems.at[1])
    wait_bytes(others, cell_sems.at[0])
    wait_bytes(latents_in.at[pl.ds(0, N_FSDP - 1)], tile_sems.at[0])
    for half in range(2):
        wait_bytes(ring_in.at[half], ring_sems.at[half])
        wait_bytes(near_in.at[half], near_sems.at[half])
        wait_bytes(gathered.at[half, pl.ds(0, (NEAR - 1) * SMALL)], spread_sems.at[half])
        sent = panel_out.at[pl.ds(0, (RING - 1) * QUARTER)]
        wait_bytes(sent, panel_sems.at[half])
        wait_bytes(sent, panel_sems.at[2 + half])


def exchange(*args):
    whole = pl.BlockSpec(memory_space=pltpu.VMEM)
    apart = pl.BlockSpec(memory_space=pltpu.HBM)
    pixels = ROWS * WIDE
    return pl.pallas_call(
        exchange_kernel,
        out_shape=(
            jax.ShapeDtypeStruct((2 * RING * QUARTER, GROUP, LANES), BF16),
            jax.ShapeDtypeStruct((N_CP, CELL_ROWS, LANES), BF16),
            jax.ShapeDtypeStruct((KEPT, KEPT), F32),
        ),
        in_specs=[apart] * len(args),
        out_specs=(whole, whole, whole),
        scratch_shapes=[
            pltpu.VMEM((KEPT, D), BF16),
            pltpu.VMEM((pixels, C), BF16),
            pltpu.VMEM((3, 3, C, C), BF16),
            pltpu.VMEM((3, C, C), BF16),
            pltpu.VMEM((3, OWN, 6 * LANES), BF16),
            pltpu.VMEM((1, C), F32),
            pltpu.VMEM((1, C), F32),
            pltpu.VMEM((LAT, C), BF16),
            pltpu.VMEM((1, LAT), F32),
            pltpu.VMEM((1, D), F32),
            pltpu.VMEM((8, D), BF16),
            pltpu.VMEM((2, D), F32),
            pltpu.VMEM((KEPT, LANES), F32),
            pltpu.VMEM((2 * TABLE_ROWS, OWN), BF16),
            pltpu.VMEM((2, RING * QUARTER, GROUP, LANES), BF16),
            pltpu.VMEM((2, RING - 1, QUARTER, GROUP, LANES), BF16),
            pltpu.VMEM((2, NEAR * SMALL, GROUP, LANES), BF16),
            pltpu.VMEM((2, NEAR - 1, SMALL, GROUP, LANES), BF16),
            pltpu.VMEM((2, SMALL, GROUP, LANES), BF16),
            pltpu.VMEM((2, NEAR * SMALL, GROUP, LANES), BF16),
            pltpu.VMEM((C, 2 * LANES), BF16),
            pltpu.VMEM((3, C, 2 * LANES), BF16),
            pltpu.VMEM((pixels, LANES), F32),
            pltpu.VMEM((pixels, LANES), F32),
            pltpu.VMEM((pixels, LANES), F32),
            pltpu.VMEM((pixels, LANES), F32),
            pltpu.VMEM((2, ROWS * WINDOWS, LANES), F32),
            pltpu.VMEM((2, ROWS * WINDOWS, LANES), F32),
            pltpu.VMEM(((ROWS + 4) * WIDE, LANES), F32),
            pltpu.VMEM((WIDE, LANES), F32),
            pltpu.VMEM((N_FSDP, GROUP, LANES), F32),
            pltpu.VMEM((N_FSDP, GROUP, LANES), F32),
            pltpu.VMEM((ROW_BLOCKS, GROUP, LANES), F32),
            pltpu.VMEM((CELL_ROWS, LANES), F32),
            pltpu.VMEM((CELL_ROWS, LANES), BF16),
            pltpu.SemaphoreType.DMA((15,)),
            pltpu.SemaphoreType.DMA((4,)),
            pltpu.SemaphoreType.DMA((4,)),
            pltpu.SemaphoreType.DMA((4,)),
            pltpu.SemaphoreType.DMA((4,)),
            pltpu.SemaphoreType.DMA((2,)),
            pltpu.SemaphoreType.DMA((2,)),
            pltpu.SemaphoreType.DMA((2,)),
            pltpu.SemaphoreType.DMA((2,)),
        ],
        compiler_params=pltpu.CompilerParams(
            collective_id=0, has_side_effects=True, vmem_limit_bytes=48 * 1024 * 1024
        ),
    )(*[pltpu.with_memory_space_constraint(arg, pltpu.HBM) for arg in args])


def project_kernel(cells, panel, gram, gain, query, keys, values, coefs, scales):
    me = lax.axis_index("fsdp")
    step = pl.program_id(0)
    count = 2 * CELLS

    @pl.when(step == 0)
    def _():
        high, low = split_2(gram[...])
        for column in range(N_CP):
            here = pl.ds(column * count, count)
            own = token_coefs(cells[column].astype(F32)[:CELLS], me, column)
            coefs[here, :] = own
            through = jnp.dot(own, high, preferred_element_type=F32)
            through = through + jnp.dot(own, low, preferred_element_type=F32)
            power = jnp.sum(through * own.astype(F32), axis=1, keepdims=True)
            scale = lax.rsqrt(jnp.maximum(power, 0.0) + 1e-06)
            scales[here, :] = jnp.broadcast_to(scale, (count, LANES))

    for which, out in enumerate((query, keys, values)):
        sides = []
        for half in range(2):
            tile = which * 6 + step * 2 + half
            at = tile * TABLE_ROWS + jnp.where(tile >= HEAD_TILES // 2, GROUP, 0)
            rows = panel[pl.ds(pl.multiple_of(at, GROUP), TABLE_ROWS), :]
            sides.append(rows)
        both = jnp.concatenate(sides, axis=1)
        stacked = jnp.concatenate([both[:PW_ROWS], both], axis=0)
        shift_at = TABLE_ROWS - GROUP
        shift = both[shift_at:].astype(F32)[SHIFT_ROW : SHIFT_ROW + 1]
        for column in range(N_CP):
            here = pl.ds(column * count, count)
            projected = jnp.dot(coefs[here, :], stacked, preferred_element_type=F32)
            scale = scales[here, :]
            for half in range(2):
                side = slice(half * LANES, (half + 1) * LANES)
                part = projected[:, side] * scale + shift[:, side]
                if which < 2:
                    power = jnp.sum(part * part, axis=1, keepdims=True) * (1.0 / HD)
                    part = part * lax.rsqrt(power + 1e-06) * gain[which : which + 1, side]
                out[here, side] = part.astype(BF16)


def project(cells, panel, gram, gain, tokens):
    width = 2 * LANES
    out = jax.ShapeDtypeStruct((tokens, gain.shape[1]), BF16)
    block = pl.BlockSpec((tokens, width), lambda step: (0, step))
    return pl.pallas_call(
        project_kernel,
        grid=(3,),
        out_shape=(out, out, out),
        in_specs=[
            pl.BlockSpec(cells.shape, lambda step: (0, 0, 0)),
            pl.BlockSpec(panel.shape, lambda step: (0, 0)),
            pl.BlockSpec(gram.shape, lambda step: (0, 0)),
            pl.BlockSpec((2, width), lambda step: (0, step)),
        ],
        out_specs=(block, block, block),
        scratch_shapes=[
            pltpu.VMEM((tokens, KEPT), BF16),
            pltpu.VMEM((tokens, LANES), F32),
        ],
        compiler_params=pltpu.CompilerParams(vmem_limit_bytes=32 * 1024 * 1024),
    )(cells, panel, gram, gain)


def body(
    video,
    conv_weight,
    conv_bias,
    time_weight,
    time_bias,
    latent_weight,
    latent_bias,
    patch_weight,
    patch_bias,
    frame_pos,
    row_pos,
    col_pos,
    modulation,
    qkv_weight,
    qk_gain,
):
    panel, cells, gram = exchange(
        video.reshape(-1, C),
        conv_weight,
        conv_bias.reshape(1, -1),
        time_weight,
        time_bias.reshape(1, -1),
        latent_weight.T,
        latent_bias.reshape(1, -1),
        patch_weight,
        patch_bias.reshape(1, -1),
        frame_pos,
        row_pos,
        col_pos,
        modulation,
        qkv_weight,
    )
    return project(cells, panel.reshape(-1, LANES), gram, qk_gain, N_CP * 2 * CELLS)


def solution(mesh):
    return jax.shard_map(
        body,
        mesh=mesh,
        in_specs=(
            P("fsdp", None, "cp", None),
            P(),
            P(),
            P(),
            P(),
            P(),
            P(),
            P(),
            P(),
            P(),
            P(),
            P(),
            P(),
            P(None, "fsdp", "cp"),
            P(None, "cp"),
        ),
        out_specs=(P("fsdp", "cp"), P("fsdp", "cp"), P("fsdp", "cp")),
        check_vma=False,
    )
```

```python
import functools

import jax
import jax.numpy as jnp
from jax import lax
from jax.experimental import pallas as pl
from jax.experimental.pallas import tpu as pltpu
from jax.sharding import PartitionSpec as P

MESH = pl.DeviceIdType.MESH
F32 = jnp.float32
BF16 = jnp.bfloat16
HIGHEST = lax.Precision.HIGHEST

D = 6144
HD = 128
C = 512
LAT = 16
FR = 4
LANES = 128
GROUP = 16
N_FSDP = 32
N_CP = 4
WINDOWS = 4
ROWS = 12
COLS = 24
ROW_BLOCKS = 8
ROW_SPLIT = 2
COL_SPLIT = 4
PATCH = 3
CELLS = ROW_BLOCKS * PATCH * PATCH
WIDE = WINDOWS * COLS
PW_ROWS = 64
POS_ROWS = 48
TABLE_ROWS = PW_ROWS + 2 * POS_ROWS + GROUP
KEPT = PW_ROWS + TABLE_ROWS
GROUPS = TABLE_ROWS // GROUP
SHIFT_ROW = 11
HEAD_TILES = 18
HALF_TILES = HEAD_TILES // 2 * GROUPS
QUARTER = 25
SMALL = 4
RING = 4
NEAR = 8
CELL_ROWS = 80
CHUNK = 4 * 96
OWN = D // N_FSDP


def split_2(values):
    high = values.astype(BF16)
    low = (values - high.astype(F32)).astype(BF16)
    return high, low


def place(shape):
    return [lax.broadcasted_iota(jnp.int32, shape, axis) for axis in range(len(shape))]


def token_coefs(cells, fsdp, column):
    group, row_part, col_part = fsdp // 8, fsdp // 4 % 2, fsdp % 4
    cell, lane = place((CELLS, LANES))
    block, inner = cell // 9, cell % 9
    row = block * 6 + row_part * PATCH + inner // PATCH
    col = column * 12 + col_part * PATCH + inner % PATCH
    base = (lane == row) | (lane == POS_ROWS + col)
    base = base | ((lane >= 2 * POS_ROWS + 8) & (lane < 2 * POS_ROWS + SHIFT_ROW))
    coefs = []
    for late in range(2):
        hot = base | (lane == 2 * POS_ROWS + group * 2 + late)
        kept = (lane // PW_ROWS) == late
        coefs.append(
            jnp.concatenate(
                [jnp.where(kept, cells, 0.0), jnp.where(hot, 1.0, 0.0)[:, : KEPT - LANES]],
                axis=1,
            )
        )
    return jnp.concatenate(coefs, axis=0).astype(BF16)


def exchange_kernel(
    video_far,
    conv_far,
    conv_bias_far,
    time_far,
    time_bias_far,
    latent_weight_far,
    latent_bias_far,
    patch_weight_far,
    patch_bias_far,
    frame_pos_far,
    row_pos_far,
    col_pos_far,
    modulation_far,
    weight_far,
    gain_far,
    query_out,
    keys_out,
    values_out,
    panel_out,
    cells_out,
    gram_out,
    coefs,
    scales,
    gain,
    tables,
    video_in,
    conv_in,
    time_in,
    weight,
    conv_bias,
    time_bias,
    latent_weight,
    latent_bias,
    patch_bias,
    frame_pos,
    modulation,
    centers,
    left_side,
    parts,
    ring_in,
    blocks,
    near_in,
    pieces,
    gathered,
    folded,
    kernels,
    q0,
    q1,
    q2,
    direct,
    edge_out,
    edge_in,
    padded,
    spread_out,
    staged,
    messages,
    latents_in,
    sums,
    cells,
    token_out,
    local_sems,
    ring_sems,
    near_sems,
    spread_sems,
    panel_sems,
    edge_send,
    edge_recv,
    tile_sems,
    cell_sems,
):
    me = lax.axis_index("fsdp")
    column = lax.axis_index("cp")
    barrier = pltpu.get_barrier_semaphore()
    z_at, x_at, y_at = me // 8, me // 4 % 2, me % 4

    def ring_peer(half, step):
        if half == 0:
            return (z_at + step) % RING * 8 + me % 8
        return me // 4 * 4 + (y_at + step) % RING

    def near_at(half):
        return me % 8 if half == 0 else z_at * 2 + x_at

    def near_peer(half, target):
        if half == 0:
            return me // 8 * 8 + target
        return target // 2 * 8 + target % 2 * 4 + y_at

    ring_at = (z_at, y_at)

    def wait_bytes(view, sem):
        pltpu.make_async_copy(view, view, sem).wait()

    pairs = [
        (patch_weight_far, tables.at[pl.ds(PW_ROWS, PW_ROWS)]),
        (row_pos_far, tables.at[pl.ds(2 * PW_ROWS, POS_ROWS)]),
        (col_pos_far, tables.at[pl.ds(2 * PW_ROWS + POS_ROWS, POS_ROWS)]),
        (frame_pos_far, frame_pos),
        (patch_bias_far, patch_bias),
        (modulation_far, modulation),
        (weight_far, weight),
        (latent_weight_far, latent_weight),
        (conv_bias_far, conv_bias),
        (time_bias_far, time_bias),
        (latent_bias_far, latent_bias),
        (gain_far, gain),
        (time_far, time_in),
        (conv_far, conv_in),
        (video_far, video_in),
        (patch_weight_far, tables.at[pl.ds(0, PW_ROWS)]),
    ]
    loads = [
        pltpu.make_async_copy(source, target, local_sems.at[at])
        for at, (source, target) in enumerate(pairs)
    ]
    for load in loads:
        load.start()

    def greet(step, carry):
        pl.semaphore_signal(
            barrier, inc=1, device_id={"fsdp": (me + step) % N_FSDP}, device_id_type=MESH
        )
        return carry

    lax.fori_loop(1, N_FSDP, greet, 0)
    for step in range(1, N_CP):
        pl.semaphore_signal(
            barrier, inc=1, device_id={"cp": (column + step) % N_CP}, device_id_type=MESH
        )
    for load in loads[:7]:
        load.wait()
    bias = patch_bias[...]
    bias_high = bias.astype(BF16).astype(F32)
    bias_mid = (bias - bias_high).astype(BF16).astype(F32)
    bias_low = bias - bias_high - bias_mid
    eight = lax.broadcasted_iota(jnp.int32, (8, D), 0)
    tail = jnp.where(
        eight == 0,
        bias_high,
        jnp.where(eight == 1, bias_mid, jnp.where(eight == 2, bias_low, 0.0)),
    )
    tables[pl.ds(KEPT - GROUP, GROUP), :] = jnp.concatenate(
        [frame_pos[...].astype(F32), tail], axis=0
    ).astype(BF16)
    start = pl.multiple_of((me // 2) * (2 * OWN), 2 * OWN)
    odd = me % 2 == 1
    own_mod = modulation[:, pl.ds(start, 2 * OWN)]
    own_scale = 1.0 + own_mod[0:1]
    own_shift = own_mod[1:2]

    for group in range(GROUPS):
        at = PW_ROWS + group * GROUP
        whole = tables[pl.ds(at, GROUP), :].astype(F32)
        center = jnp.sum(whole, axis=1, keepdims=True) * (1.0 / D)
        centers[pl.ds(at, GROUP), :] = jnp.broadcast_to(center, (GROUP, LANES))
        block = tables[pl.ds(at, GROUP), pl.ds(start, 2 * OWN)].astype(F32)
        block = (block - center) * own_scale
        if group == GROUPS - 1:
            row = lax.broadcasted_iota(jnp.int32, block.shape, 0)
            block = jnp.where(row == SHIFT_ROW, own_shift, block)
        block = jnp.where(odd, block[:, OWN:], block[:, :OWN])
        high, low = split_2(block)
        left_side[pl.ds(group * GROUP, GROUP), :] = high
        left_side[pl.ds(TABLE_ROWS + group * GROUP, GROUP), :] = low
    for which in range(3):
        for pair in range(3):
            part = jnp.dot(
                left_side[...],
                weight[which, :, pair * 256 : (pair + 1) * 256],
                preferred_element_type=F32,
            )
            part = part[:TABLE_ROWS] + part[TABLE_ROWS:]
            for half in range(2):
                tile = which * 6 + pair * 2 + half
                at = tile % 9 * GROUPS
                parts[tile // 9, pl.ds(at, GROUPS)] = (
                    part[:, half * LANES : (half + 1) * LANES]
                    .astype(BF16)
                    .reshape(GROUPS, GROUP, LANES)
                )
    parts[:, HALF_TILES:] = jnp.zeros((2, 1, GROUP, LANES), BF16)
    pl.semaphore_wait(barrier, N_FSDP - 1 + N_CP - 1)

    ring_copies = []
    for step in (2, 1, 3):
        for half in range(2):
            target = (ring_at[half] + step) % RING
            ring_copies.append(
                pltpu.make_async_remote_copy(
                    src_ref=parts.at[half, pl.ds(target * QUARTER, QUARTER)],
                    dst_ref=ring_in.at[half, RING - 1 - step],
                    send_sem=ring_sems.at[half],
                    recv_sem=ring_sems.at[2 + half],
                    device_id={"fsdp": ring_peer(half, step)},
                    device_id_type=MESH,
                )
            )
    for copy in ring_copies:
        copy.start()

    frame = (me + N_FSDP - 4) % N_FSDP // ROW_BLOCKS
    channel, lane = place((LAT, LANES))
    for load in loads[7:12]:
        load.wait()
    latent_in = latent_weight[...]

    def spread(keep):
        return lax.dot_general(
            latent_in,
            jnp.where(keep, 1.0, 0.0).astype(BF16),
            (((0,), (0,)), ((), ())),
            preferred_element_type=F32,
        ).astype(BF16)

    early_index = jnp.minimum(frame + 1, 2)
    late_index = jnp.maximum(frame - 1, 0)
    early_keep = (frame <= 1) & (lane == channel)
    late_keep = (frame >= 1) & (lane == PW_ROWS + channel)
    loads[12].wait()
    both = jnp.dot(time_in[early_index], spread(early_keep), preferred_element_type=F32)
    both = both + jnp.dot(time_in[late_index], spread(late_keep), preferred_element_type=F32)
    high, low = split_2(both)
    folded[:, :LANES] = high
    folded[:, LANES:] = low
    bias_row = jnp.dot(conv_bias[...], both, precision=HIGHEST, preferred_element_type=F32)
    loads[13].wait()

    def fold(col_shift, carry):
        total = None
        for row_shift in range(3):
            through = jnp.dot(
                conv_in[row_shift, col_shift], folded[...], preferred_element_type=F32
            )
            through = through[:, :LANES] + through[:, LANES:]
            if row_shift:
                through = pltpu.roll(through, row_shift * LAT, 1)
            total = through if total is None else total + through
        high, low = split_2(total)
        kernels[col_shift, :, :LANES] = high
        kernels[col_shift, :, LANES:] = low
        return carry

    lax.fori_loop(0, 3, fold, 0)
    loads[14].wait()

    def convolve(row, carry):
        at = pl.multiple_of(row * CHUNK, CHUNK)
        raw = video_in[pl.ds(at, CHUNK), :]
        wide = raw.astype(F32)
        active = (wide / (1.0 + jnp.exp(-wide))).astype(BF16)
        for col_shift, kept in enumerate((q0, q1, q2)):
            through = jnp.dot(active, kernels[col_shift], preferred_element_type=F32)
            kept[pl.ds(at, CHUNK), :] = through[:, :LANES] + through[:, LANES:]
        plain = jnp.dot(raw, folded[...], preferred_element_type=F32)
        direct[pl.ds(at, CHUNK), :] = plain[:, :LANES] + plain[:, LANES:] + bias_row
        return carry

    lax.fori_loop(0, ROWS * WIDE // CHUNK, convolve, 0)
    lines = ROWS * WINDOWS
    edge_out[0] = q0[pl.ds(COLS - 1, lines, stride=COLS), :]
    edge_out[1] = q2[pl.ds(0, lines, stride=COLS), :]
    edges = [
        pltpu.make_async_remote_copy(
            src_ref=edge_out.at[side],
            dst_ref=edge_in.at[side],
            send_sem=edge_send.at[side],
            recv_sem=edge_recv.at[side],
            device_id={"cp": (column + step) % N_CP},
            device_id_type=MESH,
        )
        for side, step in ((0, 1), (1, N_CP - 1))
    ]
    for edge in edges:
        edge.start()
    for half in range(2):
        wait_bytes(ring_in.at[half], ring_sems.at[2 + half])
        total = parts[half, pl.ds(ring_at[half] * QUARTER, QUARTER)].astype(F32)
        for other in range(RING - 1):
            total = total + ring_in[half, other].astype(F32)
        blocks[half, pl.ds(0, QUARTER)] = total.astype(BF16)
        spare = NEAR * SMALL - QUARTER
        blocks[half, pl.ds(QUARTER, spare)] = jnp.zeros((spare, GROUP, LANES), BF16)
        for step in range(NEAR - 1, 0, -1):
            target = (near_at(half) + step) % NEAR
            pltpu.make_async_remote_copy(
                src_ref=blocks.at[half, pl.ds(target * SMALL, SMALL)],
                dst_ref=near_in.at[half, NEAR - 1 - step],
                send_sem=near_sems.at[half],
                recv_sem=near_sems.at[2 + half],
                device_id={"fsdp": near_peer(half, target)},
                device_id_type=MESH,
            ).start()
    empty = jnp.zeros((2 * WIDE, LANES), F32)
    padded[pl.ds(0, 2 * WIDE), :] = empty
    padded[pl.ds((ROWS + 2) * WIDE, 2 * WIDE), :] = empty
    pixel = lax.broadcasted_iota(jnp.int32, (WIDE, LANES), 0) % COLS

    def columns(row, carry):
        at = pl.multiple_of(row * WIDE, WIDE)
        here = pl.ds(at, WIDE)
        total = q1[here, :]
        total = total + jnp.where(pixel == 0, 0.0, pltpu.roll(q0[here, :], 1, 0))
        total = total + jnp.where(pixel == COLS - 1, 0.0, pltpu.roll(q2[here, :], WIDE - 1, 0))
        padded[pl.ds(pl.multiple_of(at + 2 * WIDE, WIDE), WIDE), :] = total
        return carry

    lax.fori_loop(0, ROWS, columns, 0)
    for edge in edges:
        edge.wait()
    first = pl.ds(2 * WIDE, lines, stride=COLS)
    last = pl.ds(2 * WIDE + COLS - 1, lines, stride=COLS)
    padded[first, :] = padded[first, :] + jnp.where(column > 0, edge_in[0], 0.0)
    padded[last, :] = padded[last, :] + jnp.where(column < N_CP - 1, edge_in[1], 0.0)
    own_lanes = lax.broadcasted_iota(jnp.int32, (WIDE, LANES), 1) % PW_ROWS < LAT

    def packed(row, parity):
        total = padded[pl.ds((row + 1) * WIDE, WIDE), :]
        total = total + pltpu.roll(
            padded[pl.ds((row + 2) * WIDE, WIDE), :], LANES - LAT, 1
        )
        total = total + pltpu.roll(
            padded[pl.ds((row + 3) * WIDE, WIDE), :], LANES - 2 * LAT, 1
        )
        if 0 <= row < ROWS:
            total = total + direct[pl.ds(row * WIDE, WIDE), :]
        spread_out[...] = jnp.where(own_lanes, total, 0.0)
        result = None
        for side in range(2):
            taken = spread_out[pl.ds(side, WIDE // 2, stride=2), :]
            shift = 2 * LAT * parity + LAT * side
            taken = pltpu.roll(taken, shift, 1) if shift else taken
            result = taken if result is None else result + taken
        return result

    def post(values, row_part, at):
        for window in range(WINDOWS):
            for part in range(COL_SPLIT):
                begin = window * COLS // 2 + part * PATCH
                staged[window * 8 + row_part * 4 + part, at : at + PATCH, :] = values[
                    begin : begin + PATCH
                ]

    staged[...] = jnp.zeros(staged.shape, F32)
    for pair in range(ROWS // 2):
        values = packed(2 * pair, 0) + packed(2 * pair + 1, 1)
        post(values, pair // PATCH, pair % PATCH * PATCH)
    post(packed(ROWS, 0), 0, PATCH * PATCH)
    post(packed(-1, 1), 1, PATCH * PATCH)
    messages[...] = staged[...].astype(BF16)
    slot = (me + N_FSDP - 4) % N_FSDP

    def tile_copy(step):
        target = (me + step) % N_FSDP
        return pltpu.make_async_remote_copy(
            src_ref=messages.at[target],
            dst_ref=latents_in.at[slot],
            send_sem=tile_sems.at[0],
            recv_sem=tile_sems.at[1],
            device_id={"fsdp": target},
            device_id_type=MESH,
        )

    def send_tile(step, carry):
        tile_copy(step).start()
        return carry

    lax.fori_loop(1, N_FSDP, send_tile, 0)
    latents_in[slot] = messages[me]

    for half in range(2):
        wait_bytes(near_in.at[half], near_sems.at[2 + half])
        total = blocks[half, pl.ds(near_at(half) * SMALL, SMALL)].astype(F32)
        for other in range(NEAR - 1):
            total = total + near_in[half, other].astype(F32)
        pieces[half] = total.astype(BF16)
        gathered[half, pl.ds(near_at(half) * SMALL, SMALL)] = pieces[half]
        for step in range(NEAR - 1, 0, -1):
            pltpu.make_async_remote_copy(
                src_ref=pieces.at[half],
                dst_ref=gathered.at[half, pl.ds(near_at(half) * SMALL, SMALL)],
                send_sem=spread_sems.at[half],
                recv_sem=spread_sems.at[2 + half],
                device_id={"fsdp": near_peer(half, (near_at(half) + step) % NEAR)},
                device_id_type=MESH,
            ).start()

    loads[15].wait()
    centers[pl.ds(0, PW_ROWS), :] = centers[pl.ds(PW_ROWS, PW_ROWS), :]
    gram_out[...] = jnp.zeros((KEPT, KEPT), F32)
    both_last = (((1,), (1,)), ((), ()))

    def product(step, carry):
        here = pl.ds(pl.multiple_of(step * 1024, 1024), 1024)
        high, low = split_2(tables[:, here].astype(F32) - centers[:, :1])
        total = lax.dot_general(high, high, both_last, preferred_element_type=F32)
        cross = lax.dot_general(high, low, both_last, preferred_element_type=F32)
        gram_out[...] += (total + 2.0 * cross) * (1.0 / D)
        return carry

    lax.fori_loop(0, D // 1024, product, 0)
    gram_high, gram_low = split_2(gram_out[...])
    panel_copies = []
    for half in range(2):
        wait_bytes(gathered.at[half, pl.ds(0, (NEAR - 1) * SMALL)], spread_sems.at[2 + half])
        at = half * RING * QUARTER + ring_at[half] * QUARTER
        for step in (2, 1, 3):
            panel_copies.append(
                pltpu.make_async_remote_copy(
                    src_ref=gathered.at[half, pl.ds(0, QUARTER)],
                    dst_ref=panel_out.at[pl.ds(at, QUARTER)],
                    send_sem=panel_sems.at[half],
                    recv_sem=panel_sems.at[2 + half],
                    device_id={"fsdp": ring_peer(half, step)},
                    device_id_type=MESH,
                )
            )
        for copy in panel_copies[-3:]:
            copy.start()
        panel_out[pl.ds(at, QUARTER)] = gathered[half, pl.ds(0, QUARTER)]

    spread_all = spread(lane % LAT == channel).astype(F32)
    offset = jnp.dot(time_bias[...], spread_all, precision=HIGHEST, preferred_element_type=F32)
    offset = offset + jnp.dot(
        latent_bias[...],
        jnp.where(lane % LAT == channel, 1.0, 0.0),
        precision=HIGHEST,
        preferred_element_type=F32,
    )
    wait_bytes(latents_in.at[pl.ds(0, N_FSDP - 1)], tile_sems.at[1])
    for block in range(ROW_BLOCKS):
        total = latents_in[block].astype(F32)
        for other in range(1, FR):
            total = total + latents_in[other * ROW_BLOCKS + block].astype(F32)
        sums[block] = total
    row_part = me // 4 % 2
    upper = jnp.where(row_part == 0, 1.0, 0.0)
    lower = 1.0 - upper
    nine = PATCH * PATCH
    for block in range(ROW_BLOCKS):
        cells[pl.ds(block * nine, nine), :] = sums[block, 0:nine, :]
        if block > 0:
            here = pl.ds(block * nine, PATCH)
            cells[here, :] = cells[here, :] + sums[block - 1, nine : nine + PATCH, :] * upper
        if block < ROW_BLOCKS - 1:
            here = pl.ds(block * nine + 2 * PATCH, PATCH)
            cells[here, :] = cells[here, :] + sums[block + 1, nine : nine + PATCH, :] * lower
    cells[pl.ds(CELLS, CELL_ROWS - CELLS), :] = jnp.zeros((CELL_ROWS - CELLS, LANES), F32)
    token_out[...] = (cells[...] + offset).astype(BF16)
    copies = [
        pltpu.make_async_remote_copy(
            src_ref=token_out,
            dst_ref=cells_out.at[column],
            send_sem=cell_sems.at[0],
            recv_sem=cell_sems.at[1],
            device_id={"cp": (column + step) % N_CP},
            device_id_type=MESH,
        )
        for step in range(1, N_CP)
    ]
    for copy in copies:
        copy.start()
    cells_out[column] = token_out[...]
    others = cells_out.at[pl.ds(0, N_CP - 1)]
    wait_bytes(others, cell_sems.at[1])
    count = 2 * CELLS
    for group in range(N_CP):
        here = pl.ds(group * count, count)
        own = token_coefs(cells_out[group].astype(F32)[:CELLS], me, group)
        coefs[here, :] = own
        through = jnp.dot(own, gram_high, preferred_element_type=F32)
        through = through + jnp.dot(own, gram_low, preferred_element_type=F32)
        power = jnp.sum(through * own.astype(F32), axis=1, keepdims=True)
        scale = lax.rsqrt(jnp.maximum(power, 0.0) + 1e-06)
        scales[here, :] = jnp.broadcast_to(scale, (count, LANES))
    sent = panel_out.at[pl.ds(0, (RING - 1) * QUARTER)]
    for half, steps in enumerate(((0, 2, 4, 6, 8, 9), (9, 10, 12, 14, 16, 18))):
        wait_bytes(sent, panel_sems.at[2 + half])
        for begin, end in zip(steps[:-1], steps[1:]):
            sides = []
            for head in range(begin, end):
                rows = panel_out[pl.ds(half + head * GROUPS, GROUPS)]
                sides.append(rows.reshape(TABLE_ROWS, LANES))
            both = jnp.concatenate(sides, axis=1)
            stacked = jnp.concatenate([both[:PW_ROWS], both], axis=0)
            tail_rows = both[TABLE_ROWS - GROUP :].astype(F32)
            shift = tail_rows[SHIFT_ROW : SHIFT_ROW + 1]
            for group in range(N_CP):
                here = pl.ds(group * count, count)
                projected = jnp.dot(coefs[here, :], stacked, preferred_element_type=F32)
                for head in range(begin, end):
                    from_lane = (head - begin) * LANES
                    side = slice(from_lane, from_lane + LANES)
                    which, to = head // 6, head % 6 * LANES
                    part = projected[:, side] * scales[here, :] + shift[:, side]
                    if which < 2:
                        power = jnp.sum(part * part, axis=1, keepdims=True) * (1.0 / HD)
                        part = part * lax.rsqrt(power + 1e-06)
                        part = part * gain[which : which + 1, to : to + LANES]
                    out = (query_out, keys_out, values_out)[which]
                    out[here, to : to + LANES] = part.astype(BF16)
    wait_bytes(others, cell_sems.at[0])
    wait_bytes(latents_in.at[pl.ds(0, N_FSDP - 1)], tile_sems.at[0])
    for half in range(2):
        wait_bytes(ring_in.at[half], ring_sems.at[half])
        wait_bytes(near_in.at[half], near_sems.at[half])
        wait_bytes(gathered.at[half, pl.ds(0, (NEAR - 1) * SMALL)], spread_sems.at[half])
        wait_bytes(sent, panel_sems.at[half])


def exchange(*args):
    whole = pl.BlockSpec(memory_space=pltpu.VMEM)
    apart = pl.BlockSpec(memory_space=pltpu.HBM)
    pixels = ROWS * WIDE
    tokens = N_CP * 2 * CELLS
    out = jax.ShapeDtypeStruct((tokens, 6 * LANES), BF16)
    return pl.pallas_call(
        exchange_kernel,
        out_shape=(out, out, out),
        in_specs=[apart] * len(args),
        out_specs=(whole, whole, whole),
        scratch_shapes=[
            pltpu.VMEM((2 * RING * QUARTER, GROUP, LANES), BF16),
            pltpu.VMEM((N_CP, CELL_ROWS, LANES), BF16),
            pltpu.VMEM((KEPT, KEPT), F32),
            pltpu.VMEM((tokens, KEPT), BF16),
            pltpu.VMEM((tokens, LANES), F32),
            pltpu.VMEM((2, 6 * LANES), F32),
            pltpu.VMEM((KEPT, D), BF16),
            pltpu.VMEM((pixels, C), BF16),
            pltpu.VMEM((3, 3, C, C), BF16),
            pltpu.VMEM((3, C, C), BF16),
            pltpu.VMEM((3, OWN, 6 * LANES), BF16),
            pltpu.VMEM((1, C), F32),
            pltpu.VMEM((1, C), F32),
            pltpu.VMEM((LAT, C), BF16),
            pltpu.VMEM((1, LAT), F32),
            pltpu.VMEM((1, D), F32),
            pltpu.VMEM((8, D), BF16),
            pltpu.VMEM((2, D), F32),
            pltpu.VMEM((KEPT, LANES), F32),
            pltpu.VMEM((2 * TABLE_ROWS, OWN), BF16),
            pltpu.VMEM((2, RING * QUARTER, GROUP, LANES), BF16),
            pltpu.VMEM((2, RING - 1, QUARTER, GROUP, LANES), BF16),
            pltpu.VMEM((2, NEAR * SMALL, GROUP, LANES), BF16),
            pltpu.VMEM((2, NEAR - 1, SMALL, GROUP, LANES), BF16),
            pltpu.VMEM((2, SMALL, GROUP, LANES), BF16),
            pltpu.VMEM((2, NEAR * SMALL, GROUP, LANES), BF16),
            pltpu.VMEM((C, 2 * LANES), BF16),
            pltpu.VMEM((3, C, 2 * LANES), BF16),
            pltpu.VMEM((pixels, LANES), F32),
            pltpu.VMEM((pixels, LANES), F32),
            pltpu.VMEM((pixels, LANES), F32),
            pltpu.VMEM((pixels, LANES), F32),
            pltpu.VMEM((2, ROWS * WINDOWS, LANES), F32),
            pltpu.VMEM((2, ROWS * WINDOWS, LANES), F32),
            pltpu.VMEM(((ROWS + 4) * WIDE, LANES), F32),
            pltpu.VMEM((WIDE, LANES), F32),
            pltpu.VMEM((N_FSDP, GROUP, LANES), F32),
            pltpu.VMEM((N_FSDP, GROUP, LANES), BF16),
            pltpu.VMEM((N_FSDP, GROUP, LANES), BF16),
            pltpu.VMEM((ROW_BLOCKS, GROUP, LANES), F32),
            pltpu.VMEM((CELL_ROWS, LANES), F32),
            pltpu.VMEM((CELL_ROWS, LANES), BF16),
            pltpu.SemaphoreType.DMA((16,)),
            pltpu.SemaphoreType.DMA((4,)),
            pltpu.SemaphoreType.DMA((4,)),
            pltpu.SemaphoreType.DMA((4,)),
            pltpu.SemaphoreType.DMA((4,)),
            pltpu.SemaphoreType.DMA((2,)),
            pltpu.SemaphoreType.DMA((2,)),
            pltpu.SemaphoreType.DMA((2,)),
            pltpu.SemaphoreType.DMA((2,)),
        ],
        compiler_params=pltpu.CompilerParams(
            collective_id=0, has_side_effects=True, vmem_limit_bytes=48 * 1024 * 1024
        ),
    )(*[pltpu.with_memory_space_constraint(arg, pltpu.HBM) for arg in args])


def body(
    video,
    conv_weight,
    conv_bias,
    time_weight,
    time_bias,
    latent_weight,
    latent_bias,
    patch_weight,
    patch_bias,
    frame_pos,
    row_pos,
    col_pos,
    modulation,
    qkv_weight,
    qk_gain,
):
    results = exchange(
        video.reshape(-1, C),
        conv_weight,
        conv_bias.reshape(1, -1),
        time_weight,
        time_bias.reshape(1, -1),
        latent_weight.T,
        latent_bias.reshape(1, -1),
        patch_weight,
        patch_bias.reshape(1, -1),
        frame_pos,
        row_pos,
        col_pos,
        modulation,
        qkv_weight,
        qk_gain,
    )
    return results


def solution(mesh):
    return jax.shard_map(
        body,
        mesh=mesh,
        in_specs=(
            P("fsdp", None, "cp", None),
            P(),
            P(),
            P(),
            P(),
            P(),
            P(),
            P(),
            P(),
            P(),
            P(),
            P(),
            P(),
            P(None, "fsdp", "cp"),
            P(None, "cp"),
        ),
        out_specs=(P("fsdp", "cp"), P("fsdp", "cp"), P("fsdp", "cp")),
        check_vma=False,
    )
```

```python
import functools

import jax
import jax.numpy as jnp
from jax import lax
from jax.experimental import pallas as pl
from jax.experimental.pallas import tpu as pltpu
from jax.sharding import PartitionSpec as P

MESH = pl.DeviceIdType.MESH
F32 = jnp.float32
BF16 = jnp.bfloat16
HIGHEST = lax.Precision.HIGHEST

D = 6144
HD = 128
C = 512
LAT = 16
FR = 4
LANES = 128
GROUP = 16
N_FSDP = 32
N_CP = 4
WINDOWS = 4
ROWS = 12
COLS = 24
ROW_BLOCKS = 8
ROW_SPLIT = 2
COL_SPLIT = 4
PATCH = 3
CELLS = ROW_BLOCKS * PATCH * PATCH
WIDE = WINDOWS * COLS
PW_ROWS = 64
POS_ROWS = 48
TABLE_ROWS = PW_ROWS + 2 * POS_ROWS + GROUP
KEPT = PW_ROWS + TABLE_ROWS
GROUPS = TABLE_ROWS // GROUP
SHIFT_ROW = 11
HEAD_TILES = 18
HALF_TILES = HEAD_TILES // 2 * GROUPS
QUARTER = 25
SMALL = 4
RING = 4
NEAR = 8
CELL_ROWS = 80
CHUNK = 4 * 96
OWN = D // N_FSDP


def split_2(values):
    high = values.astype(BF16)
    low = (values - high.astype(F32)).astype(BF16)
    return high, low


def place(shape):
    return [lax.broadcasted_iota(jnp.int32, shape, axis) for axis in range(len(shape))]


def token_coefs(cells, fsdp, column):
    group, row_part, col_part = fsdp // 8, fsdp // 4 % 2, fsdp % 4
    cell, lane = place((CELLS, LANES))
    block, inner = cell // 9, cell % 9
    row = block * 6 + row_part * PATCH + inner // PATCH
    col = column * 12 + col_part * PATCH + inner % PATCH
    base = (lane == row) | (lane == POS_ROWS + col)
    base = base | ((lane >= 2 * POS_ROWS + 8) & (lane < 2 * POS_ROWS + SHIFT_ROW))
    coefs = []
    for late in range(2):
        hot = base | (lane == 2 * POS_ROWS + group * 2 + late)
        kept = (lane // PW_ROWS) == late
        coefs.append(
            jnp.concatenate(
                [jnp.where(kept, cells, 0.0), jnp.where(hot, 1.0, 0.0)[:, : KEPT - LANES]],
                axis=1,
            )
        )
    return jnp.concatenate(coefs, axis=0).astype(BF16)


def exchange_kernel(
    video_far,
    conv_far,
    conv_bias_far,
    time_far,
    time_bias_far,
    latent_weight_far,
    latent_bias_far,
    patch_weight_far,
    patch_bias_far,
    frame_pos_far,
    row_pos_far,
    col_pos_far,
    modulation_far,
    weight_far,
    panel_out,
    coefs,
    scales,
    cells_out,
    gram_out,
    tables,
    video_in,
    conv_in,
    time_in,
    weight,
    conv_bias,
    time_bias,
    latent_weight,
    latent_bias,
    patch_bias,
    frame_pos,
    modulation,
    centers,
    left_side,
    parts,
    ring_in,
    blocks,
    near_in,
    pieces,
    gathered,
    folded,
    kernels,
    q0,
    q1,
    q2,
    direct,
    edge_out,
    edge_in,
    padded,
    spread_out,
    staged,
    messages,
    latents_in,
    sums,
    cells,
    token_out,
    local_sems,
    ring_sems,
    near_sems,
    spread_sems,
    panel_sems,
    edge_send,
    edge_recv,
    tile_sems,
    cell_sems,
):
    me = lax.axis_index("fsdp")
    column = lax.axis_index("cp")
    barrier = pltpu.get_barrier_semaphore()
    z_at, x_at, y_at = me // 8, me // 4 % 2, me % 4

    def ring_peer(half, step):
        if half == 0:
            return (z_at + step) % RING * 8 + me % 8
        return me // 4 * 4 + (y_at + step) % RING

    def near_at(half):
        return me % 8 if half == 0 else z_at * 2 + x_at

    def near_peer(half, step):
        x_to = (x_at + step[0]) % 2
        if half == 0:
            ring_to = (y_at + step[1]) % RING
            return x_to * RING + ring_to, z_at * 8 + x_to * 4 + ring_to
        ring_to = (z_at + step[1]) % RING
        return ring_to * 2 + x_to, ring_to * 8 + x_to * 4 + y_at

    near_steps = ((1, 2), (1, 1), (1, 3), (0, 2), (1, 0), (0, 1), (0, 3))

    ring_at = (z_at, y_at)

    def wait_bytes(view, sem):
        pltpu.make_async_copy(view, view, sem).wait()

    pairs = [
        (patch_weight_far, tables.at[pl.ds(PW_ROWS, PW_ROWS)]),
        (row_pos_far, tables.at[pl.ds(2 * PW_ROWS, POS_ROWS)]),
        (col_pos_far, tables.at[pl.ds(2 * PW_ROWS + POS_ROWS, POS_ROWS)]),
        (frame_pos_far, frame_pos),
        (patch_bias_far, patch_bias),
        (modulation_far, modulation),
        (weight_far, weight),
        (latent_weight_far, latent_weight),
        (conv_bias_far, conv_bias),
        (time_bias_far, time_bias),
        (latent_bias_far, latent_bias),
        (time_far, time_in),
        (conv_far, conv_in),
        (video_far, video_in),
        (patch_weight_far, tables.at[pl.ds(0, PW_ROWS)]),
    ]
    loads = [
        pltpu.make_async_copy(source, target, local_sems.at[at])
        for at, (source, target) in enumerate(pairs)
    ]
    for load in loads:
        load.start()

    def greet(step, carry):
        pl.semaphore_signal(
            barrier, inc=1, device_id={"fsdp": (me + step) % N_FSDP}, device_id_type=MESH
        )
        return carry

    lax.fori_loop(1, N_FSDP, greet, 0)
    for step in range(1, N_CP):
        pl.semaphore_signal(
            barrier, inc=1, device_id={"cp": (column + step) % N_CP}, device_id_type=MESH
        )
    for load in loads[:7]:
        load.wait()
    bias = patch_bias[...]
    bias_high = bias.astype(BF16).astype(F32)
    bias_mid = (bias - bias_high).astype(BF16).astype(F32)
    bias_low = bias - bias_high - bias_mid
    eight = lax.broadcasted_iota(jnp.int32, (8, D), 0)
    tail = jnp.where(
        eight == 0,
        bias_high,
        jnp.where(eight == 1, bias_mid, jnp.where(eight == 2, bias_low, 0.0)),
    )
    tables[pl.ds(KEPT - GROUP, GROUP), :] = jnp.concatenate(
        [frame_pos[...].astype(F32), tail], axis=0
    ).astype(BF16)
    start = pl.multiple_of((me // 2) * (2 * OWN), 2 * OWN)
    odd = me % 2 == 1
    own_mod = modulation[:, pl.ds(start, 2 * OWN)]
    own_scale = 1.0 + own_mod[0:1]
    own_shift = own_mod[1:2]

    for group in range(GROUPS):
        at = PW_ROWS + group * GROUP
        whole = tables[pl.ds(at, GROUP), :].astype(F32)
        center = jnp.sum(whole, axis=1, keepdims=True) * (1.0 / D)
        centers[pl.ds(at, GROUP), :] = jnp.broadcast_to(center, (GROUP, LANES))
        block = tables[pl.ds(at, GROUP), pl.ds(start, 2 * OWN)].astype(F32)
        block = (block - center) * own_scale
        if group == GROUPS - 1:
            row = lax.broadcasted_iota(jnp.int32, block.shape, 0)
            block = jnp.where(row == SHIFT_ROW, own_shift, block)
        block = jnp.where(odd, block[:, OWN:], block[:, :OWN])
        high, low = split_2(block)
        left_side[pl.ds(group * GROUP, GROUP), :] = high
        left_side[pl.ds(TABLE_ROWS + group * GROUP, GROUP), :] = low
    for which in range(3):
        for pair in range(3):
            part = jnp.dot(
                left_side[...],
                weight[which, :, pair * 256 : (pair + 1) * 256],
                preferred_element_type=F32,
            )
            part = part[:TABLE_ROWS] + part[TABLE_ROWS:]
            for half in range(2):
                tile = which * 6 + pair * 2 + half
                at = tile % 9 * GROUPS
                parts[tile // 9, pl.ds(at, GROUPS)] = (
                    part[:, half * LANES : (half + 1) * LANES]
                    .astype(BF16)
                    .reshape(GROUPS, GROUP, LANES)
                )
    parts[:, HALF_TILES:] = jnp.zeros((2, 1, GROUP, LANES), BF16)
    pl.semaphore_wait(barrier, N_FSDP - 1 + N_CP - 1)

    ring_copies = []
    for step in (2, 1, 3):
        for half in range(2):
            target = (ring_at[half] + step) % RING
            ring_copies.append(
                pltpu.make_async_remote_copy(
                    src_ref=parts.at[half, pl.ds(target * QUARTER, QUARTER)],
                    dst_ref=ring_in.at[half, RING - 1 - step],
                    send_sem=ring_sems.at[half],
                    recv_sem=ring_sems.at[2 + half],
                    device_id={"fsdp": ring_peer(half, step)},
                    device_id_type=MESH,
                )
            )
    for copy in ring_copies:
        copy.start()

    frame = (me + N_FSDP - 4) % N_FSDP // ROW_BLOCKS
    channel, lane = place((LAT, LANES))
    for load in loads[7:11]:
        load.wait()
    latent_in = latent_weight[...]

    def spread(keep):
        return lax.dot_general(
            latent_in,
            jnp.where(keep, 1.0, 0.0).astype(BF16),
            (((0,), (0,)), ((), ())),
            preferred_element_type=F32,
        ).astype(BF16)

    early_index = jnp.minimum(frame + 1, 2)
    late_index = jnp.maximum(frame - 1, 0)
    early_keep = (frame <= 1) & (lane == channel)
    late_keep = (frame >= 1) & (lane == PW_ROWS + channel)
    loads[11].wait()
    both = jnp.dot(time_in[early_index], spread(early_keep), preferred_element_type=F32)
    both = both + jnp.dot(time_in[late_index], spread(late_keep), preferred_element_type=F32)
    high, low = split_2(both)
    folded[:, :LANES] = high
    folded[:, LANES:] = low
    bias_row = jnp.dot(conv_bias[...], both, precision=HIGHEST, preferred_element_type=F32)
    loads[12].wait()

    def fold(col_shift, carry):
        total = None
        for row_shift in range(3):
            through = jnp.dot(
                conv_in[row_shift, col_shift], folded[...], preferred_element_type=F32
            )
            through = through[:, :LANES] + through[:, LANES:]
            if row_shift:
                through = pltpu.roll(through, row_shift * LAT, 1)
            total = through if total is None else total + through
        high, low = split_2(total)
        kernels[col_shift, :, :LANES] = high
        kernels[col_shift, :, LANES:] = low
        return carry

    lax.fori_loop(0, 3, fold, 0)
    loads[13].wait()

    def convolve(row, carry):
        at = pl.multiple_of(row * CHUNK, CHUNK)
        raw = video_in[pl.ds(at, CHUNK), :]
        wide = raw.astype(F32)
        active = (wide / (1.0 + jnp.exp(-wide))).astype(BF16)
        for col_shift, kept in enumerate((q0, q1, q2)):
            through = jnp.dot(active, kernels[col_shift], preferred_element_type=F32)
            kept[pl.ds(at, CHUNK), :] = through[:, :LANES] + through[:, LANES:]
        plain = jnp.dot(raw, folded[...], preferred_element_type=F32)
        direct[pl.ds(at, CHUNK), :] = plain[:, :LANES] + plain[:, LANES:] + bias_row
        return carry

    lax.fori_loop(0, ROWS * WIDE // CHUNK, convolve, 0)
    lines = ROWS * WINDOWS
    edge_out[0] = q0[pl.ds(COLS - 1, lines, stride=COLS), :]
    edge_out[1] = q2[pl.ds(0, lines, stride=COLS), :]
    edges = [
        pltpu.make_async_remote_copy(
            src_ref=edge_out.at[side],
            dst_ref=edge_in.at[side],
            send_sem=edge_send.at[side],
            recv_sem=edge_recv.at[side],
            device_id={"cp": (column + step) % N_CP},
            device_id_type=MESH,
        )
        for side, step in ((0, 1), (1, N_CP - 1))
    ]
    for edge in edges:
        edge.start()
    for half in range(2):
        wait_bytes(ring_in.at[half], ring_sems.at[2 + half])
        total = parts[half, pl.ds(ring_at[half] * QUARTER, QUARTER)].astype(F32)
        for other in range(RING - 1):
            total = total + ring_in[half, other].astype(F32)
        blocks[half, pl.ds(0, QUARTER)] = total.astype(BF16)
        spare = NEAR * SMALL - QUARTER
        blocks[half, pl.ds(QUARTER, spare)] = jnp.zeros((spare, GROUP, LANES), BF16)
        for slot, step in enumerate(near_steps):
            target, peer = near_peer(half, step)
            pltpu.make_async_remote_copy(
                src_ref=blocks.at[half, pl.ds(target * SMALL, SMALL)],
                dst_ref=near_in.at[half, slot],
                send_sem=near_sems.at[half],
                recv_sem=near_sems.at[2 + half],
                device_id={"fsdp": peer},
                device_id_type=MESH,
            ).start()
    empty = jnp.zeros((2 * WIDE, LANES), F32)
    padded[pl.ds(0, 2 * WIDE), :] = empty
    padded[pl.ds((ROWS + 2) * WIDE, 2 * WIDE), :] = empty
    pixel = lax.broadcasted_iota(jnp.int32, (WIDE, LANES), 0) % COLS

    def columns(row, carry):
        at = pl.multiple_of(row * WIDE, WIDE)
        here = pl.ds(at, WIDE)
        total = q1[here, :]
        total = total + jnp.where(pixel == 0, 0.0, pltpu.roll(q0[here, :], 1, 0))
        total = total + jnp.where(pixel == COLS - 1, 0.0, pltpu.roll(q2[here, :], WIDE - 1, 0))
        padded[pl.ds(pl.multiple_of(at + 2 * WIDE, WIDE), WIDE), :] = total
        return carry

    lax.fori_loop(0, ROWS, columns, 0)
    for edge in edges:
        edge.wait()
    first = pl.ds(2 * WIDE, lines, stride=COLS)
    last = pl.ds(2 * WIDE + COLS - 1, lines, stride=COLS)
    padded[first, :] = padded[first, :] + jnp.where(column > 0, edge_in[0], 0.0)
    padded[last, :] = padded[last, :] + jnp.where(column < N_CP - 1, edge_in[1], 0.0)
    own_lanes = lax.broadcasted_iota(jnp.int32, (WIDE, LANES), 1) % PW_ROWS < LAT

    def packed(row, parity):
        total = padded[pl.ds((row + 1) * WIDE, WIDE), :]
        total = total + pltpu.roll(
            padded[pl.ds((row + 2) * WIDE, WIDE), :], LANES - LAT, 1
        )
        total = total + pltpu.roll(
            padded[pl.ds((row + 3) * WIDE, WIDE), :], LANES - 2 * LAT, 1
        )
        if 0 <= row < ROWS:
            total = total + direct[pl.ds(row * WIDE, WIDE), :]
        spread_out[...] = jnp.where(own_lanes, total, 0.0)
        result = None
        for side in range(2):
            taken = spread_out[pl.ds(side, WIDE // 2, stride=2), :]
            shift = 2 * LAT * parity + LAT * side
            taken = pltpu.roll(taken, shift, 1) if shift else taken
            result = taken if result is None else result + taken
        return result

    def post(values, row_part, at):
        for window in range(WINDOWS):
            for part in range(COL_SPLIT):
                begin = window * COLS // 2 + part * PATCH
                staged[window * 8 + row_part * 4 + part, at : at + PATCH, :] = values[
                    begin : begin + PATCH
                ]

    staged[...] = jnp.zeros(staged.shape, F32)
    for pair in range(ROWS // 2):
        values = packed(2 * pair, 0) + packed(2 * pair + 1, 1)
        post(values, pair // PATCH, pair % PATCH * PATCH)
    post(packed(ROWS, 0), 0, PATCH * PATCH)
    post(packed(-1, 1), 1, PATCH * PATCH)
    messages[...] = staged[...].astype(BF16)
    slot = (me + N_FSDP - 4) % N_FSDP

    def tile_copy(step):
        target = (me + step) % N_FSDP
        return pltpu.make_async_remote_copy(
            src_ref=messages.at[target],
            dst_ref=latents_in.at[slot],
            send_sem=tile_sems.at[0],
            recv_sem=tile_sems.at[1],
            device_id={"fsdp": target},
            device_id_type=MESH,
        )

    def send_tile(step, carry):
        tile_copy(step).start()
        return carry

    lax.fori_loop(1, N_FSDP, send_tile, 0)
    latents_in[slot] = messages[me]

    for half in range(2):
        wait_bytes(near_in.at[half], near_sems.at[2 + half])
        total = blocks[half, pl.ds(near_at(half) * SMALL, SMALL)].astype(F32)
        for other in range(NEAR - 1):
            total = total + near_in[half, other].astype(F32)
        pieces[half] = total.astype(BF16)
        gathered[half, pl.ds(near_at(half) * SMALL, SMALL)] = pieces[half]
        for step in near_steps:
            pltpu.make_async_remote_copy(
                src_ref=pieces.at[half],
                dst_ref=gathered.at[half, pl.ds(near_at(half) * SMALL, SMALL)],
                send_sem=spread_sems.at[half],
                recv_sem=spread_sems.at[2 + half],
                device_id={"fsdp": near_peer(half, step)[1]},
                device_id_type=MESH,
            ).start()

    loads[14].wait()
    centers[pl.ds(0, PW_ROWS), :] = centers[pl.ds(PW_ROWS, PW_ROWS), :]
    gram_out[...] = jnp.zeros((KEPT, KEPT), F32)
    both_last = (((1,), (1,)), ((), ()))

    def product(step, carry):
        here = pl.ds(pl.multiple_of(step * 1024, 1024), 1024)
        high, low = split_2(tables[:, here].astype(F32) - centers[:, :1])
        total = lax.dot_general(high, high, both_last, preferred_element_type=F32)
        cross = lax.dot_general(high, low, both_last, preferred_element_type=F32)
        gram_out[...] += (total + 2.0 * cross) * (1.0 / D)
        return carry

    lax.fori_loop(0, D // 1024, product, 0)
    gram_high, gram_low = split_2(gram_out[...])
    panel_copies = []
    for half in range(2):
        wait_bytes(gathered.at[half, pl.ds(0, (NEAR - 1) * SMALL)], spread_sems.at[2 + half])
        at = half * RING * QUARTER + ring_at[half] * QUARTER
        for step in (2, 1, 3):
            panel_copies.append(
                pltpu.make_async_remote_copy(
                    src_ref=gathered.at[half, pl.ds(0, QUARTER)],
                    dst_ref=panel_out.at[pl.ds(at, QUARTER)],
                    send_sem=panel_sems.at[half],
                    recv_sem=panel_sems.at[2 + half],
                    device_id={"fsdp": ring_peer(half, step)},
                    device_id_type=MESH,
                )
            )
        for copy in panel_copies[-3:]:
            copy.start()
    for half in range(2):
        at = half * RING * QUARTER + ring_at[half] * QUARTER
        panel_out[pl.ds(at, QUARTER)] = gathered[half, pl.ds(0, QUARTER)]

    spread_all = spread(lane % LAT == channel).astype(F32)
    offset = jnp.dot(time_bias[...], spread_all, precision=HIGHEST, preferred_element_type=F32)
    offset = offset + jnp.dot(
        latent_bias[...],
        jnp.where(lane % LAT == channel, 1.0, 0.0),
        precision=HIGHEST,
        preferred_element_type=F32,
    )
    wait_bytes(latents_in.at[pl.ds(0, N_FSDP - 1)], tile_sems.at[1])
    for block in range(ROW_BLOCKS):
        total = latents_in[block].astype(F32)
        for other in range(1, FR):
            total = total + latents_in[other * ROW_BLOCKS + block].astype(F32)
        sums[block] = total
    row_part = me // 4 % 2
    upper = jnp.where(row_part == 0, 1.0, 0.0)
    lower = 1.0 - upper
    nine = PATCH * PATCH
    for block in range(ROW_BLOCKS):
        cells[pl.ds(block * nine, nine), :] = sums[block, 0:nine, :]
        if block > 0:
            here = pl.ds(block * nine, PATCH)
            cells[here, :] = cells[here, :] + sums[block - 1, nine : nine + PATCH, :] * upper
        if block < ROW_BLOCKS - 1:
            here = pl.ds(block * nine + 2 * PATCH, PATCH)
            cells[here, :] = cells[here, :] + sums[block + 1, nine : nine + PATCH, :] * lower
    cells[pl.ds(CELLS, CELL_ROWS - CELLS), :] = jnp.zeros((CELL_ROWS - CELLS, LANES), F32)
    token_out[...] = (cells[...] + offset).astype(BF16)
    copies = [
        pltpu.make_async_remote_copy(
            src_ref=token_out,
            dst_ref=cells_out.at[column],
            send_sem=cell_sems.at[0],
            recv_sem=cell_sems.at[1],
            device_id={"cp": (column + step) % N_CP},
            device_id_type=MESH,
        )
        for step in range(1, N_CP)
    ]
    for copy in copies:
        copy.start()
    cells_out[column] = token_out[...]
    others = cells_out.at[pl.ds(0, N_CP - 1)]
    wait_bytes(others, cell_sems.at[1])
    count = 2 * CELLS
    for group in range(N_CP):
        here = pl.ds(group * count, count)
        own = token_coefs(cells_out[group].astype(F32)[:CELLS], me, group)
        coefs[here, :] = own
        through = jnp.dot(own, gram_high, preferred_element_type=F32)
        through = through + jnp.dot(own, gram_low, preferred_element_type=F32)
        power = jnp.sum(through * own.astype(F32), axis=1, keepdims=True)
        scale = lax.rsqrt(jnp.maximum(power, 0.0) + 1e-06)
        scales[here, :] = jnp.broadcast_to(scale, (count, LANES))
    sent = panel_out.at[pl.ds(0, (RING - 1) * QUARTER)]
    for half in range(2):
        wait_bytes(sent, panel_sems.at[2 + half])
    wait_bytes(others, cell_sems.at[0])
    wait_bytes(latents_in.at[pl.ds(0, N_FSDP - 1)], tile_sems.at[0])
    for half in range(2):
        wait_bytes(ring_in.at[half], ring_sems.at[half])
        wait_bytes(near_in.at[half], near_sems.at[half])
        wait_bytes(gathered.at[half, pl.ds(0, (NEAR - 1) * SMALL)], spread_sems.at[half])
        wait_bytes(sent, panel_sems.at[half])


def exchange(*args):
    whole = pl.BlockSpec(memory_space=pltpu.VMEM)
    apart = pl.BlockSpec(memory_space=pltpu.HBM)
    pixels = ROWS * WIDE
    tokens = N_CP * 2 * CELLS
    return pl.pallas_call(
        exchange_kernel,
        out_shape=(
            jax.ShapeDtypeStruct((2 * RING * QUARTER, GROUP, LANES), BF16),
            jax.ShapeDtypeStruct((tokens, KEPT), BF16),
            jax.ShapeDtypeStruct((tokens, LANES), F32),
        ),
        in_specs=[apart] * len(args),
        out_specs=(whole, whole, whole),
        scratch_shapes=[
            pltpu.VMEM((N_CP, CELL_ROWS, LANES), BF16),
            pltpu.VMEM((KEPT, KEPT), F32),
            pltpu.VMEM((KEPT, D), BF16),
            pltpu.VMEM((pixels, C), BF16),
            pltpu.VMEM((3, 3, C, C), BF16),
            pltpu.VMEM((3, C, C), BF16),
            pltpu.VMEM((3, OWN, 6 * LANES), BF16),
            pltpu.VMEM((1, C), F32),
            pltpu.VMEM((1, C), F32),
            pltpu.VMEM((LAT, C), BF16),
            pltpu.VMEM((1, LAT), F32),
            pltpu.VMEM((1, D), F32),
            pltpu.VMEM((8, D), BF16),
            pltpu.VMEM((2, D), F32),
            pltpu.VMEM((KEPT, LANES), F32),
            pltpu.VMEM((2 * TABLE_ROWS, OWN), BF16),
            pltpu.VMEM((2, RING * QUARTER, GROUP, LANES), BF16),
            pltpu.VMEM((2, RING - 1, QUARTER, GROUP, LANES), BF16),
            pltpu.VMEM((2, NEAR * SMALL, GROUP, LANES), BF16),
            pltpu.VMEM((2, NEAR - 1, SMALL, GROUP, LANES), BF16),
            pltpu.VMEM((2, SMALL, GROUP, LANES), BF16),
            pltpu.VMEM((2, NEAR * SMALL, GROUP, LANES), BF16),
            pltpu.VMEM((C, 2 * LANES), BF16),
            pltpu.VMEM((3, C, 2 * LANES), BF16),
            pltpu.VMEM((pixels, LANES), F32),
            pltpu.VMEM((pixels, LANES), F32),
            pltpu.VMEM((pixels, LANES), F32),
            pltpu.VMEM((pixels, LANES), F32),
            pltpu.VMEM((2, ROWS * WINDOWS, LANES), F32),
            pltpu.VMEM((2, ROWS * WINDOWS, LANES), F32),
            pltpu.VMEM(((ROWS + 4) * WIDE, LANES), F32),
            pltpu.VMEM((WIDE, LANES), F32),
            pltpu.VMEM((N_FSDP, GROUP, LANES), F32),
            pltpu.VMEM((N_FSDP, GROUP, LANES), BF16),
            pltpu.VMEM((N_FSDP, GROUP, LANES), BF16),
            pltpu.VMEM((ROW_BLOCKS, GROUP, LANES), F32),
            pltpu.VMEM((CELL_ROWS, LANES), F32),
            pltpu.VMEM((CELL_ROWS, LANES), BF16),
            pltpu.SemaphoreType.DMA((15,)),
            pltpu.SemaphoreType.DMA((4,)),
            pltpu.SemaphoreType.DMA((4,)),
            pltpu.SemaphoreType.DMA((4,)),
            pltpu.SemaphoreType.DMA((4,)),
            pltpu.SemaphoreType.DMA((2,)),
            pltpu.SemaphoreType.DMA((2,)),
            pltpu.SemaphoreType.DMA((2,)),
            pltpu.SemaphoreType.DMA((2,)),
        ],
        compiler_params=pltpu.CompilerParams(
            collective_id=0, has_side_effects=True, vmem_limit_bytes=48 * 1024 * 1024
        ),
    )(*[pltpu.with_memory_space_constraint(arg, pltpu.HBM) for arg in args])


def project_kernel(
    panel, coefs, scales, gain, query, keys, values, results, result_sems
):
    count = 2 * CELLS
    writes = []
    for which, out in enumerate((query, keys, values)):
        for pair in range(3):
            sides = []
            for head in range(which * 6 + pair * 2, which * 6 + pair * 2 + 2):
                rows = panel[pl.ds(head // (HEAD_TILES // 2) + head * GROUPS, GROUPS)]
                sides.append(rows.reshape(TABLE_ROWS, LANES))
            both = jnp.concatenate(sides, axis=1)
            stacked = jnp.concatenate([both[:PW_ROWS], both], axis=0)
            tail_rows = both[TABLE_ROWS - GROUP :].astype(F32)
            shift = tail_rows[SHIFT_ROW : SHIFT_ROW + 1]
            for group in range(N_CP):
                here = pl.ds(group * count, count)
                projected = jnp.dot(coefs[here, :], stacked, preferred_element_type=F32)
                for half in range(2):
                    side = slice(half * LANES, (half + 1) * LANES)
                    to = (pair * 2 + half) * LANES
                    part = projected[:, side] * scales[here, :] + shift[:, side]
                    if which < 2:
                        power = jnp.sum(part * part, axis=1, keepdims=True) * (1.0 / HD)
                        part = part * lax.rsqrt(power + 1e-06)
                        part = part * gain[which : which + 1, to : to + LANES]
                    results[which, here, to : to + LANES] = part.astype(BF16)
                if pair == 2:
                    write = pltpu.make_async_copy(
                        results.at[which, here], out.at[here], result_sems.at[which, group]
                    )
                    write.start()
                    writes.append(write)
    for write in writes:
        write.wait()


def project(panel, coefs, scales, gain):
    tokens = coefs.shape[0]
    out = jax.ShapeDtypeStruct((tokens, gain.shape[1]), BF16)
    return pl.pallas_call(
        project_kernel,
        out_shape=(out, out, out),
        in_specs=[pl.BlockSpec(memory_space=pltpu.VMEM)] * 4,
        out_specs=(pl.BlockSpec(memory_space=pltpu.HBM),) * 3,
        scratch_shapes=[
            pltpu.VMEM((3, tokens, gain.shape[1]), BF16),
            pltpu.SemaphoreType.DMA((3, N_CP)),
        ],
        compiler_params=pltpu.CompilerParams(vmem_limit_bytes=32 * 1024 * 1024),
    )(panel, coefs, scales, gain)


def body(
    video,
    conv_weight,
    conv_bias,
    time_weight,
    time_bias,
    latent_weight,
    latent_bias,
    patch_weight,
    patch_bias,
    frame_pos,
    row_pos,
    col_pos,
    modulation,
    qkv_weight,
    qk_gain,
):
    panel, coefs, scales = exchange(
        video.reshape(-1, C),
        conv_weight,
        conv_bias.reshape(1, -1),
        time_weight,
        time_bias.reshape(1, -1),
        latent_weight.T,
        latent_bias.reshape(1, -1),
        patch_weight,
        patch_bias.reshape(1, -1),
        frame_pos,
        row_pos,
        col_pos,
        modulation,
        qkv_weight,
    )
    return project(panel, coefs, scales, qk_gain)


def solution(mesh):
    return jax.shard_map(
        body,
        mesh=mesh,
        in_specs=(
            P("fsdp", None, "cp", None),
            P(),
            P(),
            P(),
            P(),
            P(),
            P(),
            P(),
            P(),
            P(),
            P(),
            P(),
            P(),
            P(None, "fsdp", "cp"),
            P(None, "cp"),
        ),
        out_specs=(P("fsdp", "cp"), P("fsdp", "cp"), P("fsdp", "cp")),
        check_vma=False,
    )
```

```python
import functools

import jax
import jax.numpy as jnp
from jax import lax
from jax.experimental import pallas as pl
from jax.experimental.pallas import tpu as pltpu
from jax.sharding import PartitionSpec as P

MESH = pl.DeviceIdType.MESH
F32 = jnp.float32
BF16 = jnp.bfloat16
HIGHEST = lax.Precision.HIGHEST

D = 6144
HD = 128
C = 512
LAT = 16
FR = 4
LANES = 128
GROUP = 16
N_FSDP = 32
N_CP = 4
WINDOWS = 4
ROWS = 12
COLS = 24
ROW_BLOCKS = 8
ROW_SPLIT = 2
COL_SPLIT = 4
PATCH = 3
CELLS = ROW_BLOCKS * PATCH * PATCH
WIDE = WINDOWS * COLS
PW_ROWS = 64
POS_ROWS = 48
TABLE_ROWS = PW_ROWS + 2 * POS_ROWS + GROUP
KEPT = PW_ROWS + TABLE_ROWS
GROUPS = TABLE_ROWS // GROUP
SHIFT_ROW = 11
HEAD_TILES = 18
HALF_TILES = HEAD_TILES // 2 * GROUPS
QUARTER = 25
SMALL = 3
RING = 4
NEAR = 8
LAST = NEAR * SMALL
CELL_ROWS = 80
CHUNK = 4 * 96
OWN = D // N_FSDP


def split_2(values):
    high = values.astype(BF16)
    low = (values - high.astype(F32)).astype(BF16)
    return high, low


def place(shape):
    return [lax.broadcasted_iota(jnp.int32, shape, axis) for axis in range(len(shape))]


def token_coefs(cells, fsdp, column):
    group, row_part, col_part = fsdp // 8, fsdp // 4 % 2, fsdp % 4
    cell, lane = place((CELLS, LANES))
    block, inner = cell // 9, cell % 9
    row = block * 6 + row_part * PATCH + inner // PATCH
    col = column * 12 + col_part * PATCH + inner % PATCH
    base = (lane == row) | (lane == POS_ROWS + col)
    base = base | ((lane >= 2 * POS_ROWS + 8) & (lane < 2 * POS_ROWS + SHIFT_ROW))
    coefs = []
    for late in range(2):
        hot = base | (lane == 2 * POS_ROWS + group * 2 + late)
        kept = (lane // PW_ROWS) == late
        coefs.append(
            jnp.concatenate(
                [jnp.where(kept, cells, 0.0), jnp.where(hot, 1.0, 0.0)[:, : KEPT - LANES]],
                axis=1,
            )
        )
    return jnp.concatenate(coefs, axis=0).astype(BF16)


def exchange_kernel(
    video_far,
    conv_far,
    conv_bias_far,
    time_far,
    time_bias_far,
    latent_weight_far,
    latent_bias_far,
    patch_weight_far,
    patch_bias_far,
    frame_pos_far,
    row_pos_far,
    col_pos_far,
    modulation_far,
    weight_far,
    panel_out,
    coefs,
    scales,
    cells_out,
    gram_out,
    tables,
    video_in,
    conv_in,
    time_in,
    weight,
    conv_bias,
    time_bias,
    latent_weight,
    latent_bias,
    patch_bias,
    frame_pos,
    modulation,
    centers,
    left_side,
    parts,
    ring_in,
    blocks,
    near_in,
    last_in,
    pieces,
    lasts,
    gathered,
    folded,
    kernels,
    q0,
    q1,
    q2,
    direct,
    edge_out,
    edge_in,
    padded,
    spread_out,
    staged,
    messages,
    latents_in,
    sums,
    cells,
    token_out,
    local_sems,
    ring_sems,
    near_sems,
    spread_sems,
    last_sems,
    panel_sems,
    edge_send,
    edge_recv,
    tile_sems,
    cell_sems,
):
    me = lax.axis_index("fsdp")
    column = lax.axis_index("cp")
    barrier = pltpu.get_barrier_semaphore()
    z_at, x_at, y_at = me // 8, me // 4 % 2, me % 4

    def ring_peer(half, step):
        if half == 0:
            return (z_at + step) % RING * 8 + me % 8
        return me // 4 * 4 + (y_at + step) % RING

    def near_at(half):
        return me % 8 if half == 0 else z_at * 2 + x_at

    def near_peer(half, step):
        x_to = (x_at + step[0]) % 2
        if half == 0:
            ring_to = (y_at + step[1]) % RING
            return x_to * RING + ring_to, z_at * 8 + x_to * 4 + ring_to
        ring_to = (z_at + step[1]) % RING
        return ring_to * 2 + x_to, ring_to * 8 + x_to * 4 + y_at

    near_steps = ((1, 2), (1, 1), (1, 3), (0, 2), (1, 0), (0, 1), (0, 3))

    ring_at = (z_at, y_at)

    def wait_bytes(view, sem):
        pltpu.make_async_copy(view, view, sem).wait()

    pairs = [
        (patch_weight_far, tables.at[pl.ds(PW_ROWS, PW_ROWS)]),
        (row_pos_far, tables.at[pl.ds(2 * PW_ROWS, POS_ROWS)]),
        (col_pos_far, tables.at[pl.ds(2 * PW_ROWS + POS_ROWS, POS_ROWS)]),
        (frame_pos_far, frame_pos),
        (patch_bias_far, patch_bias),
        (modulation_far, modulation),
        (weight_far, weight),
        (latent_weight_far, latent_weight),
        (conv_bias_far, conv_bias),
        (time_bias_far, time_bias),
        (latent_bias_far, latent_bias),
        (time_far, time_in),
        (conv_far, conv_in),
        (video_far, video_in),
        (patch_weight_far, tables.at[pl.ds(0, PW_ROWS)]),
    ]
    loads = [
        pltpu.make_async_copy(source, target, local_sems.at[at])
        for at, (source, target) in enumerate(pairs)
    ]
    for load in loads:
        load.start()

    def greet(step, carry):
        pl.semaphore_signal(
            barrier, inc=1, device_id={"fsdp": (me + step) % N_FSDP}, device_id_type=MESH
        )
        return carry

    lax.fori_loop(1, N_FSDP, greet, 0)
    for step in range(1, N_CP):
        pl.semaphore_signal(
            barrier, inc=1, device_id={"cp": (column + step) % N_CP}, device_id_type=MESH
        )
    for load in loads[:7]:
        load.wait()
    bias = patch_bias[...]
    bias_high = bias.astype(BF16).astype(F32)
    bias_mid = (bias - bias_high).astype(BF16).astype(F32)
    bias_low = bias - bias_high - bias_mid
    eight = lax.broadcasted_iota(jnp.int32, (8, D), 0)
    tail = jnp.where(
        eight == 0,
        bias_high,
        jnp.where(eight == 1, bias_mid, jnp.where(eight == 2, bias_low, 0.0)),
    )
    tables[pl.ds(KEPT - GROUP, GROUP), :] = jnp.concatenate(
        [frame_pos[...].astype(F32), tail], axis=0
    ).astype(BF16)
    start = pl.multiple_of((me // 2) * (2 * OWN), 2 * OWN)
    odd = me % 2 == 1
    own_mod = modulation[:, pl.ds(start, 2 * OWN)]
    own_scale = 1.0 + own_mod[0:1]
    own_shift = own_mod[1:2]

    for group in range(GROUPS):
        at = PW_ROWS + group * GROUP
        whole = tables[pl.ds(at, GROUP), :].astype(F32)
        center = jnp.sum(whole, axis=1, keepdims=True) * (1.0 / D)
        centers[pl.ds(at, GROUP), :] = jnp.broadcast_to(center, (GROUP, LANES))
        block = tables[pl.ds(at, GROUP), pl.ds(start, 2 * OWN)].astype(F32)
        block = (block - center) * own_scale
        if group == GROUPS - 1:
            row = lax.broadcasted_iota(jnp.int32, block.shape, 0)
            block = jnp.where(row == SHIFT_ROW, own_shift, block)
        block = jnp.where(odd, block[:, OWN:], block[:, :OWN])
        high, low = split_2(block)
        left_side[pl.ds(group * GROUP, GROUP), :] = high
        left_side[pl.ds(TABLE_ROWS + group * GROUP, GROUP), :] = low
    for which in range(3):
        for pair in range(3):
            part = jnp.dot(
                left_side[...],
                weight[which, :, pair * 256 : (pair + 1) * 256],
                preferred_element_type=F32,
            )
            part = part[:TABLE_ROWS] + part[TABLE_ROWS:]
            for half in range(2):
                tile = which * 6 + pair * 2 + half
                at = tile % 9 * GROUPS
                parts[tile // 9, pl.ds(at, GROUPS)] = (
                    part[:, half * LANES : (half + 1) * LANES]
                    .astype(BF16)
                    .reshape(GROUPS, GROUP, LANES)
                )
    parts[:, HALF_TILES:] = jnp.zeros((2, 1, GROUP, LANES), BF16)
    pl.semaphore_wait(barrier, N_FSDP - 1 + N_CP - 1)

    ring_copies = []
    for step in (2, 1, 3):
        for half in range(2):
            target = (ring_at[half] + step) % RING
            ring_copies.append(
                pltpu.make_async_remote_copy(
                    src_ref=parts.at[half, pl.ds(target * QUARTER, QUARTER)],
                    dst_ref=ring_in.at[half, RING - 1 - step],
                    send_sem=ring_sems.at[half],
                    recv_sem=ring_sems.at[2 + half],
                    device_id={"fsdp": ring_peer(half, step)},
                    device_id_type=MESH,
                )
            )
    for copy in ring_copies:
        copy.start()

    frame = (me + N_FSDP - 4) % N_FSDP // ROW_BLOCKS
    channel, lane = place((LAT, LANES))
    for load in loads[7:11]:
        load.wait()
    latent_in = latent_weight[...]

    def spread(keep):
        return lax.dot_general(
            latent_in,
            jnp.where(keep, 1.0, 0.0).astype(BF16),
            (((0,), (0,)), ((), ())),
            preferred_element_type=F32,
        ).astype(BF16)

    early_index = jnp.minimum(frame + 1, 2)
    late_index = jnp.maximum(frame - 1, 0)
    early_keep = (frame <= 1) & (lane == channel)
    late_keep = (frame >= 1) & (lane == PW_ROWS + channel)
    loads[11].wait()
    both = jnp.dot(time_in[early_index], spread(early_keep), preferred_element_type=F32)
    both = both + jnp.dot(time_in[late_index], spread(late_keep), preferred_element_type=F32)
    high, low = split_2(both)
    folded[:, :LANES] = high
    folded[:, LANES:] = low
    bias_row = jnp.dot(conv_bias[...], both, precision=HIGHEST, preferred_element_type=F32)
    loads[12].wait()

    def fold(col_shift, carry):
        total = None
        for row_shift in range(3):
            through = jnp.dot(
                conv_in[row_shift, col_shift], folded[...], preferred_element_type=F32
            )
            through = through[:, :LANES] + through[:, LANES:]
            if row_shift:
                through = pltpu.roll(through, row_shift * LAT, 1)
            total = through if total is None else total + through
        high, low = split_2(total)
        kernels[col_shift, :, :LANES] = high
        kernels[col_shift, :, LANES:] = low
        return carry

    lax.fori_loop(0, 3, fold, 0)
    loads[13].wait()

    def convolve(row, carry):
        at = pl.multiple_of(row * CHUNK, CHUNK)
        raw = video_in[pl.ds(at, CHUNK), :]
        wide = raw.astype(F32)
        active = (wide / (1.0 + jnp.exp(-wide))).astype(BF16)
        for col_shift, kept in enumerate((q0, q1, q2)):
            through = jnp.dot(active, kernels[col_shift], preferred_element_type=F32)
            kept[pl.ds(at, CHUNK), :] = through[:, :LANES] + through[:, LANES:]
        plain = jnp.dot(raw, folded[...], preferred_element_type=F32)
        direct[pl.ds(at, CHUNK), :] = plain[:, :LANES] + plain[:, LANES:] + bias_row
        return carry

    lax.fori_loop(0, ROWS * WIDE // CHUNK, convolve, 0)
    lines = ROWS * WINDOWS
    edge_out[0] = q0[pl.ds(COLS - 1, lines, stride=COLS), :]
    edge_out[1] = q2[pl.ds(0, lines, stride=COLS), :]
    edges = [
        pltpu.make_async_remote_copy(
            src_ref=edge_out.at[side],
            dst_ref=edge_in.at[side],
            send_sem=edge_send.at[side],
            recv_sem=edge_recv.at[side],
            device_id={"cp": (column + step) % N_CP},
            device_id_type=MESH,
        )
        for side, step in ((0, 1), (1, N_CP - 1))
    ]
    for edge in edges:
        edge.start()
    for half in range(2):
        wait_bytes(ring_in.at[half], ring_sems.at[2 + half])
        total = parts[half, pl.ds(ring_at[half] * QUARTER, QUARTER)].astype(F32)
        for other in range(RING - 1):
            total = total + ring_in[half, other].astype(F32)
        blocks[half] = total.astype(BF16)
        for slot, step in enumerate(near_steps):
            target, peer = near_peer(half, step)
            pltpu.make_async_remote_copy(
                src_ref=blocks.at[half, pl.ds(target * SMALL, SMALL)],
                dst_ref=near_in.at[half, slot],
                send_sem=near_sems.at[half],
                recv_sem=near_sems.at[2 + half],
                device_id={"fsdp": peer},
                device_id_type=MESH,
            ).start()

            @pl.when(target == 0)
            def _():
                pltpu.make_async_remote_copy(
                    src_ref=blocks.at[half, pl.ds(LAST, 1)],
                    dst_ref=last_in.at[half, slot],
                    send_sem=last_sems.at[half],
                    recv_sem=last_sems.at[2 + half],
                    device_id={"fsdp": peer},
                    device_id_type=MESH,
                ).start()

    empty = jnp.zeros((2 * WIDE, LANES), F32)
    padded[pl.ds(0, 2 * WIDE), :] = empty
    padded[pl.ds((ROWS + 2) * WIDE, 2 * WIDE), :] = empty
    pixel = lax.broadcasted_iota(jnp.int32, (WIDE, LANES), 0) % COLS

    def columns(row, carry):
        at = pl.multiple_of(row * WIDE, WIDE)
        here = pl.ds(at, WIDE)
        total = q1[here, :]
        total = total + jnp.where(pixel == 0, 0.0, pltpu.roll(q0[here, :], 1, 0))
        total = total + jnp.where(pixel == COLS - 1, 0.0, pltpu.roll(q2[here, :], WIDE - 1, 0))
        padded[pl.ds(pl.multiple_of(at + 2 * WIDE, WIDE), WIDE), :] = total
        return carry

    lax.fori_loop(0, ROWS, columns, 0)
    for edge in edges:
        edge.wait()
    first = pl.ds(2 * WIDE, lines, stride=COLS)
    last = pl.ds(2 * WIDE + COLS - 1, lines, stride=COLS)
    padded[first, :] = padded[first, :] + jnp.where(column > 0, edge_in[0], 0.0)
    padded[last, :] = padded[last, :] + jnp.where(column < N_CP - 1, edge_in[1], 0.0)
    own_lanes = lax.broadcasted_iota(jnp.int32, (WIDE, LANES), 1) % PW_ROWS < LAT

    def packed(row, parity):
        total = padded[pl.ds((row + 1) * WIDE, WIDE), :]
        total = total + pltpu.roll(
            padded[pl.ds((row + 2) * WIDE, WIDE), :], LANES - LAT, 1
        )
        total = total + pltpu.roll(
            padded[pl.ds((row + 3) * WIDE, WIDE), :], LANES - 2 * LAT, 1
        )
        if 0 <= row < ROWS:
            total = total + direct[pl.ds(row * WIDE, WIDE), :]
        spread_out[...] = jnp.where(own_lanes, total, 0.0)
        result = None
        for side in range(2):
            taken = spread_out[pl.ds(side, WIDE // 2, stride=2), :]
            shift = 2 * LAT * parity + LAT * side
            taken = pltpu.roll(taken, shift, 1) if shift else taken
            result = taken if result is None else result + taken
        return result

    def post(values, row_part, at):
        for window in range(WINDOWS):
            for part in range(COL_SPLIT):
                begin = window * COLS // 2 + part * PATCH
                staged[window * 8 + row_part * 4 + part, at : at + PATCH, :] = values[
                    begin : begin + PATCH
                ]

    staged[...] = jnp.zeros(staged.shape, F32)
    for pair in range(ROWS // 2):
        values = packed(2 * pair, 0) + packed(2 * pair + 1, 1)
        post(values, pair // PATCH, pair % PATCH * PATCH)
    post(packed(ROWS, 0), 0, PATCH * PATCH)
    post(packed(-1, 1), 1, PATCH * PATCH)
    messages[...] = staged[...].astype(BF16)
    slot = (me + N_FSDP - 4) % N_FSDP

    def tile_copy(step):
        target = (me + step) % N_FSDP
        return pltpu.make_async_remote_copy(
            src_ref=messages.at[target],
            dst_ref=latents_in.at[slot],
            send_sem=tile_sems.at[0],
            recv_sem=tile_sems.at[1],
            device_id={"fsdp": target},
            device_id_type=MESH,
        )

    def send_tile(step, carry):
        tile_copy(step).start()
        return carry

    lax.fori_loop(1, N_FSDP, send_tile, 0)
    latents_in[slot] = messages[me]

    for half in range(2):
        wait_bytes(near_in.at[half], near_sems.at[2 + half])
        total = blocks[half, pl.ds(near_at(half) * SMALL, SMALL)].astype(F32)
        for other in range(NEAR - 1):
            total = total + near_in[half, other].astype(F32)
        pieces[half] = total.astype(BF16)
        for step in near_steps:
            pltpu.make_async_remote_copy(
                src_ref=pieces.at[half],
                dst_ref=gathered.at[half, pl.ds(near_at(half) * SMALL, SMALL)],
                send_sem=spread_sems.at[half],
                recv_sem=spread_sems.at[2 + half],
                device_id={"fsdp": near_peer(half, step)[1]},
                device_id_type=MESH,
            ).start()
        gathered[half, pl.ds(near_at(half) * SMALL, SMALL)] = pieces[half]

        @pl.when(near_at(half) == 0)
        def _():
            wait_bytes(last_in.at[half], last_sems.at[2 + half])
            total = blocks[half, pl.ds(LAST, 1)].astype(F32)
            for other in range(NEAR - 1):
                total = total + last_in[half, other].astype(F32)
            lasts[half] = total.astype(BF16)
            for step in near_steps:
                pltpu.make_async_remote_copy(
                    src_ref=lasts.at[half],
                    dst_ref=gathered.at[half, pl.ds(LAST, 1)],
                    send_sem=last_sems.at[4 + half],
                    recv_sem=last_sems.at[6 + half],
                    device_id={"fsdp": near_peer(half, step)[1]},
                    device_id_type=MESH,
                ).start()
            gathered[half, pl.ds(LAST, 1)] = lasts[half]

    loads[14].wait()
    centers[pl.ds(0, PW_ROWS), :] = centers[pl.ds(PW_ROWS, PW_ROWS), :]
    gram_out[...] = jnp.zeros((KEPT, KEPT), F32)
    both_last = (((1,), (1,)), ((), ()))

    def product(step, carry):
        here = pl.ds(pl.multiple_of(step * 1024, 1024), 1024)
        high, low = split_2(tables[:, here].astype(F32) - centers[:, :1])
        total = lax.dot_general(high, high, both_last, preferred_element_type=F32)
        cross = lax.dot_general(high, low, both_last, preferred_element_type=F32)
        gram_out[...] += (total + 2.0 * cross) * (1.0 / D)
        return carry

    lax.fori_loop(0, D // 1024, product, 0)
    gram_high, gram_low = split_2(gram_out[...])
    panel_copies = []
    for half in range(2):
        wait_bytes(gathered.at[half, pl.ds(0, (NEAR - 1) * SMALL)], spread_sems.at[2 + half])

        @pl.when(near_at(half) != 0)
        def _():
            wait_bytes(gathered.at[half, pl.ds(LAST, 1)], last_sems.at[6 + half])

        at = half * RING * QUARTER + ring_at[half] * QUARTER
        for step in (2, 1, 3):
            panel_copies.append(
                pltpu.make_async_remote_copy(
                    src_ref=gathered.at[half, pl.ds(0, QUARTER)],
                    dst_ref=panel_out.at[pl.ds(at, QUARTER)],
                    send_sem=panel_sems.at[half],
                    recv_sem=panel_sems.at[2 + half],
                    device_id={"fsdp": ring_peer(half, step)},
                    device_id_type=MESH,
                )
            )
        for copy in panel_copies[-3:]:
            copy.start()
    for half in range(2):
        at = half * RING * QUARTER + ring_at[half] * QUARTER
        panel_out[pl.ds(at, QUARTER)] = gathered[half, pl.ds(0, QUARTER)]

    spread_all = spread(lane % LAT == channel).astype(F32)
    offset = jnp.dot(time_bias[...], spread_all, precision=HIGHEST, preferred_element_type=F32)
    offset = offset + jnp.dot(
        latent_bias[...],
        jnp.where(lane % LAT == channel, 1.0, 0.0),
        precision=HIGHEST,
        preferred_element_type=F32,
    )
    wait_bytes(latents_in.at[pl.ds(0, N_FSDP - 1)], tile_sems.at[1])
    for block in range(ROW_BLOCKS):
        total = latents_in[block].astype(F32)
        for other in range(1, FR):
            total = total + latents_in[other * ROW_BLOCKS + block].astype(F32)
        sums[block] = total
    row_part = me // 4 % 2
    upper = jnp.where(row_part == 0, 1.0, 0.0)
    lower = 1.0 - upper
    nine = PATCH * PATCH
    for block in range(ROW_BLOCKS):
        cells[pl.ds(block * nine, nine), :] = sums[block, 0:nine, :]
        if block > 0:
            here = pl.ds(block * nine, PATCH)
            cells[here, :] = cells[here, :] + sums[block - 1, nine : nine + PATCH, :] * upper
        if block < ROW_BLOCKS - 1:
            here = pl.ds(block * nine + 2 * PATCH, PATCH)
            cells[here, :] = cells[here, :] + sums[block + 1, nine : nine + PATCH, :] * lower
    cells[pl.ds(CELLS, CELL_ROWS - CELLS), :] = jnp.zeros((CELL_ROWS - CELLS, LANES), F32)
    token_out[...] = (cells[...] + offset).astype(BF16)
    copies = [
        pltpu.make_async_remote_copy(
            src_ref=token_out,
            dst_ref=cells_out.at[column],
            send_sem=cell_sems.at[0],
            recv_sem=cell_sems.at[1],
            device_id={"cp": (column + step) % N_CP},
            device_id_type=MESH,
        )
        for step in range(1, N_CP)
    ]
    for copy in copies:
        copy.start()
    cells_out[column] = token_out[...]
    others = cells_out.at[pl.ds(0, N_CP - 1)]
    wait_bytes(others, cell_sems.at[1])
    count = 2 * CELLS
    for group in range(N_CP):
        here = pl.ds(group * count, count)
        own = token_coefs(cells_out[group].astype(F32)[:CELLS], me, group)
        coefs[here, :] = own
        through = jnp.dot(own, gram_high, preferred_element_type=F32)
        through = through + jnp.dot(own, gram_low, preferred_element_type=F32)
        power = jnp.sum(through * own.astype(F32), axis=1, keepdims=True)
        scale = lax.rsqrt(jnp.maximum(power, 0.0) + 1e-06)
        scales[here, :] = jnp.broadcast_to(scale, (count, LANES))
    sent = panel_out.at[pl.ds(0, (RING - 1) * QUARTER)]
    for half in range(2):
        wait_bytes(sent, panel_sems.at[2 + half])
    wait_bytes(others, cell_sems.at[0])
    wait_bytes(latents_in.at[pl.ds(0, N_FSDP - 1)], tile_sems.at[0])
    for half in range(2):
        wait_bytes(ring_in.at[half], ring_sems.at[half])
        wait_bytes(near_in.at[half], near_sems.at[half])
        wait_bytes(gathered.at[half, pl.ds(0, (NEAR - 1) * SMALL)], spread_sems.at[half])
        wait_bytes(sent, panel_sems.at[half])

        @pl.when(near_at(half) == 0)
        def _():
            wait_bytes(last_in.at[half], last_sems.at[4 + half])

        @pl.when(near_at(half) != 0)
        def _():
            wait_bytes(last_in.at[half, 0], last_sems.at[half])


def exchange(*args):
    whole = pl.BlockSpec(memory_space=pltpu.VMEM)
    apart = pl.BlockSpec(memory_space=pltpu.HBM)
    pixels = ROWS * WIDE
    tokens = N_CP * 2 * CELLS
    return pl.pallas_call(
        exchange_kernel,
        out_shape=(
            jax.ShapeDtypeStruct((2 * RING * QUARTER, GROUP, LANES), BF16),
            jax.ShapeDtypeStruct((tokens, KEPT), BF16),
            jax.ShapeDtypeStruct((tokens, LANES), F32),
        ),
        in_specs=[apart] * len(args),
        out_specs=(whole, whole, whole),
        scratch_shapes=[
            pltpu.VMEM((N_CP, CELL_ROWS, LANES), BF16),
            pltpu.VMEM((KEPT, KEPT), F32),
            pltpu.VMEM((KEPT, D), BF16),
            pltpu.VMEM((pixels, C), BF16),
            pltpu.VMEM((3, 3, C, C), BF16),
            pltpu.VMEM((3, C, C), BF16),
            pltpu.VMEM((3, OWN, 6 * LANES), BF16),
            pltpu.VMEM((1, C), F32),
            pltpu.VMEM((1, C), F32),
            pltpu.VMEM((LAT, C), BF16),
            pltpu.VMEM((1, LAT), F32),
            pltpu.VMEM((1, D), F32),
            pltpu.VMEM((8, D), BF16),
            pltpu.VMEM((2, D), F32),
            pltpu.VMEM((KEPT, LANES), F32),
            pltpu.VMEM((2 * TABLE_ROWS, OWN), BF16),
            pltpu.VMEM((2, RING * QUARTER, GROUP, LANES), BF16),
            pltpu.VMEM((2, RING - 1, QUARTER, GROUP, LANES), BF16),
            pltpu.VMEM((2, QUARTER, GROUP, LANES), BF16),
            pltpu.VMEM((2, NEAR - 1, SMALL, GROUP, LANES), BF16),
            pltpu.VMEM((2, NEAR - 1, 1, GROUP, LANES), BF16),
            pltpu.VMEM((2, SMALL, GROUP, LANES), BF16),
            pltpu.VMEM((2, 1, GROUP, LANES), BF16),
            pltpu.VMEM((2, QUARTER, GROUP, LANES), BF16),
            pltpu.VMEM((C, 2 * LANES), BF16),
            pltpu.VMEM((3, C, 2 * LANES), BF16),
            pltpu.VMEM((pixels, LANES), F32),
            pltpu.VMEM((pixels, LANES), F32),
            pltpu.VMEM((pixels, LANES), F32),
            pltpu.VMEM((pixels, LANES), F32),
            pltpu.VMEM((2, ROWS * WINDOWS, LANES), F32),
            pltpu.VMEM((2, ROWS * WINDOWS, LANES), F32),
            pltpu.VMEM(((ROWS + 4) * WIDE, LANES), F32),
            pltpu.VMEM((WIDE, LANES), F32),
            pltpu.VMEM((N_FSDP, GROUP, LANES), F32),
            pltpu.VMEM((N_FSDP, GROUP, LANES), BF16),
            pltpu.VMEM((N_FSDP, GROUP, LANES), BF16),
            pltpu.VMEM((ROW_BLOCKS, GROUP, LANES), F32),
            pltpu.VMEM((CELL_ROWS, LANES), F32),
            pltpu.VMEM((CELL_ROWS, LANES), BF16),
            pltpu.SemaphoreType.DMA((15,)),
            pltpu.SemaphoreType.DMA((4,)),
            pltpu.SemaphoreType.DMA((4,)),
            pltpu.SemaphoreType.DMA((4,)),
            pltpu.SemaphoreType.DMA((8,)),
            pltpu.SemaphoreType.DMA((4,)),
            pltpu.SemaphoreType.DMA((2,)),
            pltpu.SemaphoreType.DMA((2,)),
            pltpu.SemaphoreType.DMA((2,)),
            pltpu.SemaphoreType.DMA((2,)),
        ],
        compiler_params=pltpu.CompilerParams(
            collective_id=0, has_side_effects=True, vmem_limit_bytes=48 * 1024 * 1024
        ),
    )(*[pltpu.with_memory_space_constraint(arg, pltpu.HBM) for arg in args])


def project_kernel(
    panel, coefs, scales, gain, query, keys, values, stacked, results, result_sems
):
    count = 2 * CELLS
    writes = []
    for which, out in ((2, values), (0, query), (1, keys)):
        pairs = []
        for pair in range(3):
            sides = []
            for head in range(which * 6 + pair * 2, which * 6 + pair * 2 + 2):
                rows = panel[pl.ds(head // (HEAD_TILES // 2) + head * GROUPS, GROUPS)]
                sides.append(rows.reshape(TABLE_ROWS, LANES))
            both = jnp.concatenate(sides, axis=1)
            stacked[pair, pl.ds(0, PW_ROWS)] = both[:PW_ROWS]
            stacked[pair, pl.ds(PW_ROWS, TABLE_ROWS)] = both
            tail_rows = both[TABLE_ROWS - GROUP :].astype(F32)
            pairs.append(tail_rows[SHIFT_ROW : SHIFT_ROW + 1])
        for group in range(N_CP):
            here = pl.ds(group * count, count)
            for pair, shift in enumerate(pairs):
                projected = jnp.dot(
                    coefs[here, :], stacked[pair], preferred_element_type=F32
                )
                for half in range(2):
                    side = slice(half * LANES, (half + 1) * LANES)
                    to = (pair * 2 + half) * LANES
                    part = projected[:, side] * scales[here, :] + shift[:, side]
                    if which < 2:
                        power = jnp.sum(part * part, axis=1, keepdims=True) * (1.0 / HD)
                        part = part * lax.rsqrt(power + 1e-06)
                        part = part * gain[which : which + 1, to : to + LANES]
                    results[which, here, to : to + LANES] = part.astype(BF16)
            write = pltpu.make_async_copy(
                results.at[which, here], out.at[here], result_sems.at[which, group]
            )
            write.start()
            writes.append(write)
    for write in writes:
        write.wait()


def project(panel, coefs, scales, gain):
    tokens = coefs.shape[0]
    out = jax.ShapeDtypeStruct((tokens, gain.shape[1]), BF16)
    return pl.pallas_call(
        project_kernel,
        out_shape=(out, out, out),
        in_specs=[pl.BlockSpec(memory_space=pltpu.VMEM)] * 4,
        out_specs=(pl.BlockSpec(memory_space=pltpu.HBM),) * 3,
        scratch_shapes=[
            pltpu.VMEM((3, KEPT, 2 * LANES), BF16),
            pltpu.VMEM((3, tokens, gain.shape[1]), BF16),
            pltpu.SemaphoreType.DMA((3, N_CP)),
        ],
        compiler_params=pltpu.CompilerParams(vmem_limit_bytes=32 * 1024 * 1024),
    )(panel, coefs, scales, gain)


def body(
    video,
    conv_weight,
    conv_bias,
    time_weight,
    time_bias,
    latent_weight,
    latent_bias,
    patch_weight,
    patch_bias,
    frame_pos,
    row_pos,
    col_pos,
    modulation,
    qkv_weight,
    qk_gain,
):
    panel, coefs, scales = exchange(
        video.reshape(-1, C),
        conv_weight,
        conv_bias.reshape(1, -1),
        time_weight,
        time_bias.reshape(1, -1),
        latent_weight.T,
        latent_bias.reshape(1, -1),
        patch_weight,
        patch_bias.reshape(1, -1),
        frame_pos,
        row_pos,
        col_pos,
        modulation,
        qkv_weight,
    )
    return project(panel, coefs, scales, qk_gain)


def solution(mesh):
    return jax.shard_map(
        body,
        mesh=mesh,
        in_specs=(
            P("fsdp", None, "cp", None),
            P(),
            P(),
            P(),
            P(),
            P(),
            P(),
            P(),
            P(),
            P(),
            P(),
            P(),
            P(),
            P(None, "fsdp", "cp"),
            P(None, "cp"),
        ),
        out_specs=(P("fsdp", "cp"), P("fsdp", "cp"), P("fsdp", "cp")),
        check_vma=False,
    )
```

```python
import functools

import jax
import jax.numpy as jnp
from jax import lax
from jax.experimental import pallas as pl
from jax.experimental.pallas import tpu as pltpu
from jax.sharding import PartitionSpec as P

MESH = pl.DeviceIdType.MESH
F32 = jnp.float32
BF16 = jnp.bfloat16
HIGHEST = lax.Precision.HIGHEST

D = 6144
HD = 128
C = 512
LAT = 16
FR = 4
LANES = 128
GROUP = 16
N_FSDP = 32
N_CP = 4
WINDOWS = 4
ROWS = 12
COLS = 24
ROW_BLOCKS = 8
ROW_SPLIT = 2
COL_SPLIT = 4
PATCH = 3
CELLS = ROW_BLOCKS * PATCH * PATCH
WIDE = WINDOWS * COLS
PW_ROWS = 64
POS_ROWS = 48
TABLE_ROWS = PW_ROWS + 2 * POS_ROWS + GROUP
KEPT = PW_ROWS + TABLE_ROWS
GROUPS = TABLE_ROWS // GROUP
SHIFT_ROW = 11
HEAD_TILES = 18
HALF_TILES = HEAD_TILES // 2 * GROUPS
QUARTER = 25
SMALL = 3
RING = 4
NEAR = 8
LAST = NEAR * SMALL
CELL_ROWS = 80
CHUNK = 4 * 96
OWN = D // N_FSDP


def split_2(values):
    high = values.astype(BF16)
    low = (values - high.astype(F32)).astype(BF16)
    return high, low


def place(shape):
    return [lax.broadcasted_iota(jnp.int32, shape, axis) for axis in range(len(shape))]


def token_coefs(cells, fsdp, column):
    group, row_part, col_part = fsdp // 8, fsdp // 4 % 2, fsdp % 4
    cell, lane = place((CELLS, LANES))
    block, inner = cell // 9, cell % 9
    row = block * 6 + row_part * PATCH + inner // PATCH
    col = column * 12 + col_part * PATCH + inner % PATCH
    base = (lane == row) | (lane == POS_ROWS + col)
    base = base | ((lane >= 2 * POS_ROWS + 8) & (lane < 2 * POS_ROWS + SHIFT_ROW))
    coefs = []
    for late in range(2):
        hot = base | (lane == 2 * POS_ROWS + group * 2 + late)
        kept = (lane // PW_ROWS) == late
        coefs.append(
            jnp.concatenate(
                [jnp.where(kept, cells, 0.0), jnp.where(hot, 1.0, 0.0)[:, : KEPT - LANES]],
                axis=1,
            )
        )
    return jnp.concatenate(coefs, axis=0).astype(BF16)


def exchange_kernel(
    video_far,
    conv_far,
    conv_bias_far,
    time_far,
    time_bias_far,
    latent_weight_far,
    latent_bias_far,
    patch_weight_far,
    patch_bias_far,
    frame_pos_far,
    row_pos_far,
    col_pos_far,
    modulation_far,
    weight_far,
    panel_out,
    coefs,
    scales,
    cells_out,
    gram_out,
    tables,
    video_in,
    conv_in,
    time_in,
    weight,
    conv_bias,
    time_bias,
    latent_weight,
    latent_bias,
    patch_bias,
    frame_pos,
    modulation,
    centers,
    left_side,
    parts,
    ring_in,
    blocks,
    near_in,
    last_in,
    pieces,
    lasts,
    gathered,
    folded,
    kernels,
    q0,
    q1,
    q2,
    direct,
    edge_out,
    edge_in,
    padded,
    spread_out,
    staged,
    messages,
    latents_in,
    sums,
    cells,
    token_out,
    local_sems,
    ring_sems,
    near_sems,
    spread_sems,
    last_sems,
    panel_sems,
    edge_send,
    edge_recv,
    tile_sems,
    cell_sems,
):
    me = lax.axis_index("fsdp")
    column = lax.axis_index("cp")
    barrier = pltpu.get_barrier_semaphore()
    z_at, x_at, y_at = lax.div(me, 8), lax.rem(lax.div(me, 4), 2), lax.rem(me, 4)
    plane_at = lax.rem(me, 8)

    def ring_peer(half, step):
        if half == 0:
            return lax.rem(z_at + step, RING) * 8 + plane_at
        return me - y_at + lax.rem(y_at + step, RING)

    def near_at(half):
        return plane_at if half == 0 else z_at * 2 + x_at

    def near_peer(half, step):
        x_to = 1 - x_at if step[0] else x_at
        if half == 0:
            ring_to = lax.rem(y_at + step[1], RING)
            return x_to * RING + ring_to, z_at * 8 + x_to * 4 + ring_to
        ring_to = lax.rem(z_at + step[1], RING)
        return ring_to * 2 + x_to, ring_to * 8 + x_to * 4 + y_at

    near_steps = ((1, 2), (1, 1), (1, 3), (0, 2), (1, 0), (0, 1), (0, 3))

    ring_at = (z_at, y_at)

    def wait_bytes(view, sem):
        pltpu.make_async_copy(view, view, sem).wait()

    pairs = [
        (patch_weight_far, tables.at[pl.ds(PW_ROWS, PW_ROWS)]),
        (row_pos_far, tables.at[pl.ds(2 * PW_ROWS, POS_ROWS)]),
        (col_pos_far, tables.at[pl.ds(2 * PW_ROWS + POS_ROWS, POS_ROWS)]),
        (frame_pos_far, frame_pos),
        (patch_bias_far, patch_bias),
        (modulation_far, modulation),
        (weight_far, weight),
        (latent_weight_far, latent_weight),
        (conv_bias_far, conv_bias),
        (time_bias_far, time_bias),
        (latent_bias_far, latent_bias),
        (time_far, time_in),
        (conv_far, conv_in),
        (video_far, video_in),
        (patch_weight_far, tables.at[pl.ds(0, PW_ROWS)]),
    ]
    loads = [
        pltpu.make_async_copy(source, target, local_sems.at[at])
        for at, (source, target) in enumerate(pairs)
    ]
    for load in loads:
        load.start()

    def greet(step, carry):
        pl.semaphore_signal(
            barrier,
            inc=1,
            device_id={"fsdp": lax.rem(me + step, N_FSDP)},
            device_id_type=MESH,
        )
        return carry

    lax.fori_loop(1, N_FSDP, greet, 0)
    for step in range(1, N_CP):
        pl.semaphore_signal(
            barrier, inc=1, device_id={"cp": (column + step) % N_CP}, device_id_type=MESH
        )
    for load in loads[:7]:
        load.wait()
    bias = patch_bias[...]
    bias_high = bias.astype(BF16).astype(F32)
    bias_mid = (bias - bias_high).astype(BF16).astype(F32)
    bias_low = bias - bias_high - bias_mid
    eight = lax.broadcasted_iota(jnp.int32, (8, D), 0)
    tail = jnp.where(
        eight == 0,
        bias_high,
        jnp.where(eight == 1, bias_mid, jnp.where(eight == 2, bias_low, 0.0)),
    )
    tables[pl.ds(KEPT - GROUP, GROUP), :] = jnp.concatenate(
        [frame_pos[...].astype(F32), tail], axis=0
    ).astype(BF16)
    start = pl.multiple_of((me // 2) * (2 * OWN), 2 * OWN)
    odd = me % 2 == 1
    own_mod = modulation[:, pl.ds(start, 2 * OWN)]
    own_scale = 1.0 + own_mod[0:1]
    own_shift = own_mod[1:2]

    for group in range(GROUPS):
        at = PW_ROWS + group * GROUP
        whole = tables[pl.ds(at, GROUP), :].astype(F32)
        center = jnp.sum(whole, axis=1, keepdims=True) * (1.0 / D)
        centers[pl.ds(at, GROUP), :] = jnp.broadcast_to(center, (GROUP, LANES))
        block = tables[pl.ds(at, GROUP), pl.ds(start, 2 * OWN)].astype(F32)
        block = (block - center) * own_scale
        if group == GROUPS - 1:
            row = lax.broadcasted_iota(jnp.int32, block.shape, 0)
            block = jnp.where(row == SHIFT_ROW, own_shift, block)
        block = jnp.where(odd, block[:, OWN:], block[:, :OWN])
        high, low = split_2(block)
        left_side[pl.ds(group * GROUP, GROUP), :] = high
        left_side[pl.ds(TABLE_ROWS + group * GROUP, GROUP), :] = low
    for which in range(3):
        for pair in range(3):
            part = jnp.dot(
                left_side[...],
                weight[which, :, pair * 256 : (pair + 1) * 256],
                preferred_element_type=F32,
            )
            part = part[:TABLE_ROWS] + part[TABLE_ROWS:]
            for half in range(2):
                tile = which * 6 + pair * 2 + half
                at = tile % 9 * GROUPS
                parts[tile // 9, pl.ds(at, GROUPS)] = (
                    part[:, half * LANES : (half + 1) * LANES]
                    .astype(BF16)
                    .reshape(GROUPS, GROUP, LANES)
                )
    parts[:, HALF_TILES:] = jnp.zeros((2, 1, GROUP, LANES), BF16)
    pl.semaphore_wait(barrier, N_FSDP - 1 + N_CP - 1)

    ring_copies = []
    for step in (2, 1, 3):
        for half in range(2):
            target = lax.rem(ring_at[half] + step, RING)
            ring_copies.append(
                pltpu.make_async_remote_copy(
                    src_ref=parts.at[half, pl.ds(target * QUARTER, QUARTER)],
                    dst_ref=ring_in.at[half, RING - 1 - step],
                    send_sem=ring_sems.at[half],
                    recv_sem=ring_sems.at[2 + half],
                    device_id={"fsdp": ring_peer(half, step)},
                    device_id_type=MESH,
                )
            )
    for copy in ring_copies:
        copy.start()

    frame = (me + N_FSDP - 4) % N_FSDP // ROW_BLOCKS
    channel, lane = place((LAT, LANES))
    for load in loads[7:11]:
        load.wait()
    latent_in = latent_weight[...]

    def spread(keep):
        return lax.dot_general(
            latent_in,
            jnp.where(keep, 1.0, 0.0).astype(BF16),
            (((0,), (0,)), ((), ())),
            preferred_element_type=F32,
        ).astype(BF16)

    early_index = jnp.minimum(frame + 1, 2)
    late_index = jnp.maximum(frame - 1, 0)
    early_keep = (frame <= 1) & (lane == channel)
    late_keep = (frame >= 1) & (lane == PW_ROWS + channel)
    loads[11].wait()
    both = jnp.dot(time_in[early_index], spread(early_keep), preferred_element_type=F32)
    both = both + jnp.dot(time_in[late_index], spread(late_keep), preferred_element_type=F32)
    high, low = split_2(both)
    folded[:, :LANES] = high
    folded[:, LANES:] = low
    bias_row = jnp.dot(conv_bias[...], both, precision=HIGHEST, preferred_element_type=F32)
    loads[12].wait()

    def fold(col_shift, carry):
        total = None
        for row_shift in range(3):
            through = jnp.dot(
                conv_in[row_shift, col_shift], folded[...], preferred_element_type=F32
            )
            through = through[:, :LANES] + through[:, LANES:]
            if row_shift:
                through = pltpu.roll(through, row_shift * LAT, 1)
            total = through if total is None else total + through
        high, low = split_2(total)
        kernels[col_shift, :, :LANES] = high
        kernels[col_shift, :, LANES:] = low
        return carry

    lax.fori_loop(0, 3, fold, 0)
    loads[13].wait()

    def convolve(row, carry):
        at = pl.multiple_of(row * CHUNK, CHUNK)
        raw = video_in[pl.ds(at, CHUNK), :]
        wide = raw.astype(F32)
        active = (wide / (1.0 + jnp.exp(-wide))).astype(BF16)
        for col_shift, kept in enumerate((q0, q1, q2)):
            through = jnp.dot(active, kernels[col_shift], preferred_element_type=F32)
            kept[pl.ds(at, CHUNK), :] = through[:, :LANES] + through[:, LANES:]
        plain = jnp.dot(raw, folded[...], preferred_element_type=F32)
        direct[pl.ds(at, CHUNK), :] = plain[:, :LANES] + plain[:, LANES:] + bias_row
        return carry

    lax.fori_loop(0, ROWS * WIDE // CHUNK, convolve, 0)
    lines = ROWS * WINDOWS
    edge_out[0] = q0[pl.ds(COLS - 1, lines, stride=COLS), :]
    edge_out[1] = q2[pl.ds(0, lines, stride=COLS), :]
    edges = [
        pltpu.make_async_remote_copy(
            src_ref=edge_out.at[side],
            dst_ref=edge_in.at[side],
            send_sem=edge_send.at[side],
            recv_sem=edge_recv.at[side],
            device_id={"cp": (column + step) % N_CP},
            device_id_type=MESH,
        )
        for side, step in ((0, 1), (1, N_CP - 1))
    ]
    for edge in edges:
        edge.start()
    for half in range(2):
        wait_bytes(ring_in.at[half], ring_sems.at[2 + half])
        total = parts[half, pl.ds(ring_at[half] * QUARTER, QUARTER)].astype(F32)
        for other in range(RING - 1):
            total = total + ring_in[half, other].astype(F32)
        blocks[half] = total.astype(BF16)
        for slot, step in enumerate(near_steps):
            target, peer = near_peer(half, step)
            pltpu.make_async_remote_copy(
                src_ref=blocks.at[half, pl.ds(target * SMALL, SMALL)],
                dst_ref=near_in.at[half, slot],
                send_sem=near_sems.at[half],
                recv_sem=near_sems.at[2 + half],
                device_id={"fsdp": peer},
                device_id_type=MESH,
            ).start()

            @pl.when(target == 0)
            def _():
                pltpu.make_async_remote_copy(
                    src_ref=blocks.at[half, pl.ds(LAST, 1)],
                    dst_ref=last_in.at[half, slot],
                    send_sem=last_sems.at[half],
                    recv_sem=last_sems.at[2 + half],
                    device_id={"fsdp": peer},
                    device_id_type=MESH,
                ).start()

    empty = jnp.zeros((2 * WIDE, LANES), F32)
    padded[pl.ds(0, 2 * WIDE), :] = empty
    padded[pl.ds((ROWS + 2) * WIDE, 2 * WIDE), :] = empty
    pixel = lax.broadcasted_iota(jnp.int32, (WIDE, LANES), 0) % COLS

    def columns(row, carry):
        at = pl.multiple_of(row * WIDE, WIDE)
        here = pl.ds(at, WIDE)
        total = q1[here, :]
        total = total + jnp.where(pixel == 0, 0.0, pltpu.roll(q0[here, :], 1, 0))
        total = total + jnp.where(pixel == COLS - 1, 0.0, pltpu.roll(q2[here, :], WIDE - 1, 0))
        padded[pl.ds(pl.multiple_of(at + 2 * WIDE, WIDE), WIDE), :] = total
        return carry

    lax.fori_loop(0, ROWS, columns, 0)
    for edge in edges:
        edge.wait()
    first = pl.ds(2 * WIDE, lines, stride=COLS)
    last = pl.ds(2 * WIDE + COLS - 1, lines, stride=COLS)
    padded[first, :] = padded[first, :] + jnp.where(column > 0, edge_in[0], 0.0)
    padded[last, :] = padded[last, :] + jnp.where(column < N_CP - 1, edge_in[1], 0.0)
    own_lanes = lax.broadcasted_iota(jnp.int32, (WIDE, LANES), 1) % PW_ROWS < LAT

    def packed(row, parity):
        total = padded[pl.ds((row + 1) * WIDE, WIDE), :]
        total = total + pltpu.roll(
            padded[pl.ds((row + 2) * WIDE, WIDE), :], LANES - LAT, 1
        )
        total = total + pltpu.roll(
            padded[pl.ds((row + 3) * WIDE, WIDE), :], LANES - 2 * LAT, 1
        )
        if 0 <= row < ROWS:
            total = total + direct[pl.ds(row * WIDE, WIDE), :]
        spread_out[pl.ds(0, WIDE), :] = jnp.where(own_lanes, total, 0.0)
        result = None
        for side in range(2):
            taken = spread_out[pl.ds(side, WIDE // 2, stride=2), :]
            shift = 2 * LAT * parity + LAT * side
            taken = pltpu.roll(taken, shift, 1) if shift else taken
            result = taken if result is None else result + taken
        return result

    def post(values, row_part, at):
        for window in range(WINDOWS):
            for part in range(COL_SPLIT):
                begin = window * COLS // 2 + part * PATCH
                staged[window * 8 + row_part * 4 + part, at : at + PATCH, :] = values[
                    begin : begin + PATCH
                ]

    staged[...] = jnp.zeros(staged.shape, F32)
    for pair in range(ROWS // 2):
        values = packed(2 * pair, 0) + packed(2 * pair + 1, 1)
        post(values, pair // PATCH, pair % PATCH * PATCH)
    post(packed(ROWS, 0), 0, PATCH * PATCH)
    post(packed(-1, 1), 1, PATCH * PATCH)
    messages[...] = staged[...].astype(BF16)
    slot = (me + N_FSDP - 4) % N_FSDP

    def tile_copy(step):
        target = lax.rem(me + step, N_FSDP)
        return pltpu.make_async_remote_copy(
            src_ref=messages.at[target],
            dst_ref=latents_in.at[slot],
            send_sem=tile_sems.at[0],
            recv_sem=tile_sems.at[1],
            device_id={"fsdp": target},
            device_id_type=MESH,
        )

    def send_tile(step, carry):
        tile_copy(step).start()
        return carry

    lax.fori_loop(1, N_FSDP, send_tile, 0)
    latents_in[slot] = messages[me]

    for half in range(2):
        wait_bytes(near_in.at[half], near_sems.at[2 + half])
        total = blocks[half, pl.ds(near_at(half) * SMALL, SMALL)].astype(F32)
        for other in range(NEAR - 1):
            total = total + near_in[half, other].astype(F32)
        pieces[half] = total.astype(BF16)
        for step in near_steps:
            pltpu.make_async_remote_copy(
                src_ref=pieces.at[half],
                dst_ref=gathered.at[half, pl.ds(near_at(half) * SMALL, SMALL)],
                send_sem=spread_sems.at[half],
                recv_sem=spread_sems.at[2 + half],
                device_id={"fsdp": near_peer(half, step)[1]},
                device_id_type=MESH,
            ).start()
        gathered[half, pl.ds(near_at(half) * SMALL, SMALL)] = pieces[half]

        @pl.when(near_at(half) == 0)
        def _():
            wait_bytes(last_in.at[half], last_sems.at[2 + half])
            total = blocks[half, pl.ds(LAST, 1)].astype(F32)
            for other in range(NEAR - 1):
                total = total + last_in[half, other].astype(F32)
            lasts[half] = total.astype(BF16)
            for step in near_steps:
                pltpu.make_async_remote_copy(
                    src_ref=lasts.at[half],
                    dst_ref=gathered.at[half, pl.ds(LAST, 1)],
                    send_sem=last_sems.at[4 + half],
                    recv_sem=last_sems.at[6 + half],
                    device_id={"fsdp": near_peer(half, step)[1]},
                    device_id_type=MESH,
                ).start()
            gathered[half, pl.ds(LAST, 1)] = lasts[half]

    loads[14].wait()
    centers[pl.ds(0, PW_ROWS), :] = centers[pl.ds(PW_ROWS, PW_ROWS), :]
    gram_out[...] = jnp.zeros((KEPT, KEPT), F32)
    both_last = (((1,), (1,)), ((), ()))

    def product(step, carry):
        here = pl.ds(pl.multiple_of(step * 1024, 1024), 1024)
        high, low = split_2(tables[:, here].astype(F32) - centers[:, :1])
        total = lax.dot_general(high, high, both_last, preferred_element_type=F32)
        cross = lax.dot_general(high, low, both_last, preferred_element_type=F32)
        gram_out[...] += (total + 2.0 * cross) * (1.0 / D)
        return carry

    lax.fori_loop(0, D // 1024, product, 0)
    gram_high, gram_low = split_2(gram_out[...])
    panel_copies = []
    for half in range(2):
        wait_bytes(gathered.at[half, pl.ds(0, (NEAR - 1) * SMALL)], spread_sems.at[2 + half])

        @pl.when(near_at(half) != 0)
        def _():
            wait_bytes(gathered.at[half, pl.ds(LAST, 1)], last_sems.at[6 + half])

        at = half * RING * QUARTER + ring_at[half] * QUARTER
        for step in (2, 1, 3):
            panel_copies.append(
                pltpu.make_async_remote_copy(
                    src_ref=gathered.at[half, pl.ds(0, QUARTER)],
                    dst_ref=panel_out.at[pl.ds(at, QUARTER)],
                    send_sem=panel_sems.at[half],
                    recv_sem=panel_sems.at[2 + half],
                    device_id={"fsdp": ring_peer(half, step)},
                    device_id_type=MESH,
                )
            )
        for copy in panel_copies[-3:]:
            copy.start()
    for half in range(2):
        at = half * RING * QUARTER + ring_at[half] * QUARTER
        panel_out[pl.ds(at, QUARTER)] = gathered[half, pl.ds(0, QUARTER)]

    spread_all = spread(lane % LAT == channel).astype(F32)
    offset = jnp.dot(time_bias[...], spread_all, precision=HIGHEST, preferred_element_type=F32)
    offset = offset + jnp.dot(
        latent_bias[...],
        jnp.where(lane % LAT == channel, 1.0, 0.0),
        precision=HIGHEST,
        preferred_element_type=F32,
    )
    wait_bytes(latents_in.at[pl.ds(0, N_FSDP - 1)], tile_sems.at[1])
    for block in range(ROW_BLOCKS):
        total = latents_in[block].astype(F32)
        for other in range(1, FR):
            total = total + latents_in[other * ROW_BLOCKS + block].astype(F32)
        sums[block] = total
    row_part = me // 4 % 2
    upper = jnp.where(row_part == 0, 1.0, 0.0)
    lower = 1.0 - upper
    nine = PATCH * PATCH
    for block in range(ROW_BLOCKS):
        cells[pl.ds(block * nine, nine), :] = sums[block, 0:nine, :]
        if block > 0:
            here = pl.ds(block * nine, PATCH)
            cells[here, :] = cells[here, :] + sums[block - 1, nine : nine + PATCH, :] * upper
        if block < ROW_BLOCKS - 1:
            here = pl.ds(block * nine + 2 * PATCH, PATCH)
            cells[here, :] = cells[here, :] + sums[block + 1, nine : nine + PATCH, :] * lower
    cells[pl.ds(CELLS, CELL_ROWS - CELLS), :] = jnp.zeros((CELL_ROWS - CELLS, LANES), F32)
    token_out[...] = (cells[...] + offset).astype(BF16)
    copies = [
        pltpu.make_async_remote_copy(
            src_ref=token_out,
            dst_ref=cells_out.at[column],
            send_sem=cell_sems.at[0],
            recv_sem=cell_sems.at[1],
            device_id={"cp": (column + step) % N_CP},
            device_id_type=MESH,
        )
        for step in range(1, N_CP)
    ]
    for copy in copies:
        copy.start()
    cells_out[column] = token_out[...]
    others = cells_out.at[pl.ds(0, N_CP - 1)]
    wait_bytes(others, cell_sems.at[1])
    count = 2 * CELLS
    for group in range(N_CP):
        here = pl.ds(group * count, count)
        own = token_coefs(cells_out[group].astype(F32)[:CELLS], me, group)
        coefs[here, :] = own
        through = jnp.dot(own, gram_high, preferred_element_type=F32)
        through = through + jnp.dot(own, gram_low, preferred_element_type=F32)
        power = jnp.sum(through * own.astype(F32), axis=1, keepdims=True)
        scale = lax.rsqrt(jnp.maximum(power, 0.0) + 1e-06)
        scales[here, :] = jnp.broadcast_to(scale, (count, LANES))
    sent = panel_out.at[pl.ds(0, (RING - 1) * QUARTER)]
    for half in range(2):
        wait_bytes(sent, panel_sems.at[2 + half])
    wait_bytes(others, cell_sems.at[0])
    wait_bytes(latents_in.at[pl.ds(0, N_FSDP - 1)], tile_sems.at[0])
    for half in range(2):
        wait_bytes(ring_in.at[half], ring_sems.at[half])
        wait_bytes(near_in.at[half], near_sems.at[half])
        wait_bytes(gathered.at[half, pl.ds(0, (NEAR - 1) * SMALL)], spread_sems.at[half])
        wait_bytes(sent, panel_sems.at[half])

        @pl.when(near_at(half) == 0)
        def _():
            wait_bytes(last_in.at[half], last_sems.at[4 + half])

        @pl.when(near_at(half) != 0)
        def _():
            wait_bytes(last_in.at[half, 0], last_sems.at[half])


def exchange(*args):
    whole = pl.BlockSpec(memory_space=pltpu.VMEM)
    apart = pl.BlockSpec(memory_space=pltpu.HBM)
    pixels = ROWS * WIDE
    tokens = N_CP * 2 * CELLS
    return pl.pallas_call(
        exchange_kernel,
        out_shape=(
            jax.ShapeDtypeStruct((2 * RING * QUARTER, GROUP, LANES), BF16),
            jax.ShapeDtypeStruct((tokens, KEPT), BF16),
            jax.ShapeDtypeStruct((tokens, LANES), F32),
        ),
        in_specs=[apart] * len(args),
        out_specs=(whole, whole, whole),
        scratch_shapes=[
            pltpu.VMEM((N_CP, CELL_ROWS, LANES), BF16),
            pltpu.VMEM((KEPT, KEPT), F32),
            pltpu.VMEM((KEPT, D), BF16),
            pltpu.VMEM((pixels, C), BF16),
            pltpu.VMEM((3, 3, C, C), BF16),
            pltpu.VMEM((3, C, C), BF16),
            pltpu.VMEM((3, OWN, 6 * LANES), BF16),
            pltpu.VMEM((1, C), F32),
            pltpu.VMEM((1, C), F32),
            pltpu.VMEM((LAT, C), BF16),
            pltpu.VMEM((1, LAT), F32),
            pltpu.VMEM((1, D), F32),
            pltpu.VMEM((8, D), BF16),
            pltpu.VMEM((2, D), F32),
            pltpu.VMEM((KEPT, LANES), F32),
            pltpu.VMEM((2 * TABLE_ROWS, OWN), BF16),
            pltpu.VMEM((2, RING * QUARTER, GROUP, LANES), BF16),
            pltpu.VMEM((2, RING - 1, QUARTER, GROUP, LANES), BF16),
            pltpu.VMEM((2, QUARTER, GROUP, LANES), BF16),
            pltpu.VMEM((2, NEAR - 1, SMALL, GROUP, LANES), BF16),
            pltpu.VMEM((2, NEAR - 1, 1, GROUP, LANES), BF16),
            pltpu.VMEM((2, SMALL, GROUP, LANES), BF16),
            pltpu.VMEM((2, 1, GROUP, LANES), BF16),
            pltpu.VMEM((2, QUARTER, GROUP, LANES), BF16),
            pltpu.VMEM((C, 2 * LANES), BF16),
            pltpu.VMEM((3, C, 2 * LANES), BF16),
            pltpu.VMEM((pixels + COLS, LANES), F32),
            pltpu.VMEM((pixels + COLS, LANES), F32),
            pltpu.VMEM((pixels + COLS, LANES), F32),
            pltpu.VMEM((pixels + COLS, LANES), F32),
            pltpu.VMEM((2, ROWS * WINDOWS, LANES), F32),
            pltpu.VMEM((2, ROWS * WINDOWS, LANES), F32),
            pltpu.VMEM(((ROWS + 4) * WIDE, LANES), F32),
            pltpu.VMEM((WIDE + 8, LANES), F32),
            pltpu.VMEM((N_FSDP, GROUP, LANES), F32),
            pltpu.VMEM((N_FSDP, GROUP, LANES), BF16),
            pltpu.VMEM((N_FSDP, GROUP, LANES), BF16),
            pltpu.VMEM((ROW_BLOCKS, GROUP, LANES), F32),
            pltpu.VMEM((CELL_ROWS, LANES), F32),
            pltpu.VMEM((CELL_ROWS, LANES), BF16),
            pltpu.SemaphoreType.DMA((15,)),
            pltpu.SemaphoreType.DMA((4,)),
            pltpu.SemaphoreType.DMA((4,)),
            pltpu.SemaphoreType.DMA((4,)),
            pltpu.SemaphoreType.DMA((8,)),
            pltpu.SemaphoreType.DMA((4,)),
            pltpu.SemaphoreType.DMA((2,)),
            pltpu.SemaphoreType.DMA((2,)),
            pltpu.SemaphoreType.DMA((2,)),
            pltpu.SemaphoreType.DMA((2,)),
        ],
        compiler_params=pltpu.CompilerParams(
            collective_id=0, has_side_effects=True, vmem_limit_bytes=48 * 1024 * 1024
        ),
    )(*[pltpu.with_memory_space_constraint(arg, pltpu.HBM) for arg in args])


def project_kernel(
    panel, coefs, scales, gain, query, keys, values, stacked, results, result_sems
):
    count = 2 * CELLS
    writes = []
    for which, out in ((2, values), (0, query), (1, keys)):
        pairs = []
        for pair in range(3):
            sides = []
            for head in range(which * 6 + pair * 2, which * 6 + pair * 2 + 2):
                rows = panel[pl.ds(head // (HEAD_TILES // 2) + head * GROUPS, GROUPS)]
                sides.append(rows.reshape(TABLE_ROWS, LANES))
            both = jnp.concatenate(sides, axis=1)
            stacked[pair, pl.ds(0, PW_ROWS)] = both[:PW_ROWS]
            stacked[pair, pl.ds(PW_ROWS, TABLE_ROWS)] = both
            tail_rows = both[TABLE_ROWS - GROUP :].astype(F32)
            pairs.append(tail_rows[SHIFT_ROW : SHIFT_ROW + 1])
        for group in range(N_CP):
            here = pl.ds(group * count, count)
            for pair, shift in enumerate(pairs):
                projected = jnp.dot(
                    coefs[here, :], stacked[pair], preferred_element_type=F32
                )
                for half in range(2):
                    side = slice(half * LANES, (half + 1) * LANES)
                    to = (pair * 2 + half) * LANES
                    part = projected[:, side] * scales[here, :] + shift[:, side]
                    if which < 2:
                        power = jnp.sum(part * part, axis=1, keepdims=True) * (1.0 / HD)
                        part = part * lax.rsqrt(power + 1e-06)
                        part = part * gain[which : which + 1, to : to + LANES]
                    results[which, here, to : to + LANES] = part.astype(BF16)
            write = pltpu.make_async_copy(
                results.at[which, here], out.at[here], result_sems.at[which, group]
            )
            write.start()
            writes.append(write)
    for write in writes:
        write.wait()


def project(panel, coefs, scales, gain):
    tokens = coefs.shape[0]
    out = jax.ShapeDtypeStruct((tokens, gain.shape[1]), BF16)
    return pl.pallas_call(
        project_kernel,
        out_shape=(out, out, out),
        in_specs=[pl.BlockSpec(memory_space=pltpu.VMEM)] * 4,
        out_specs=(pl.BlockSpec(memory_space=pltpu.HBM),) * 3,
        scratch_shapes=[
            pltpu.VMEM((3, KEPT, 2 * LANES), BF16),
            pltpu.VMEM((3, tokens, gain.shape[1]), BF16),
            pltpu.SemaphoreType.DMA((3, N_CP)),
        ],
        compiler_params=pltpu.CompilerParams(vmem_limit_bytes=32 * 1024 * 1024),
    )(panel, coefs, scales, gain)


def body(
    video,
    conv_weight,
    conv_bias,
    time_weight,
    time_bias,
    latent_weight,
    latent_bias,
    patch_weight,
    patch_bias,
    frame_pos,
    row_pos,
    col_pos,
    modulation,
    qkv_weight,
    qk_gain,
):
    panel, coefs, scales = exchange(
        video.reshape(-1, C),
        conv_weight,
        conv_bias.reshape(1, -1),
        time_weight,
        time_bias.reshape(1, -1),
        latent_weight.T,
        latent_bias.reshape(1, -1),
        patch_weight,
        patch_bias.reshape(1, -1),
        frame_pos,
        row_pos,
        col_pos,
        modulation,
        qkv_weight,
    )
    return project(panel, coefs, scales, qk_gain)


def solution(mesh):
    return jax.shard_map(
        body,
        mesh=mesh,
        in_specs=(
            P("fsdp", None, "cp", None),
            P(),
            P(),
            P(),
            P(),
            P(),
            P(),
            P(),
            P(),
            P(),
            P(),
            P(),
            P(),
            P(None, "fsdp", "cp"),
            P(None, "cp"),
        ),
        out_specs=(P("fsdp", "cp"), P("fsdp", "cp"), P("fsdp", "cp")),
        check_vma=False,
    )
```

```python
import functools

import jax
import jax.numpy as jnp
from jax import lax
from jax.experimental import pallas as pl
from jax.experimental.pallas import tpu as pltpu
from jax.sharding import PartitionSpec as P

MESH = pl.DeviceIdType.MESH
F32 = jnp.float32
BF16 = jnp.bfloat16
HIGHEST = lax.Precision.HIGHEST

D = 6144
HD = 128
C = 512
LAT = 16
FR = 4
LANES = 128
GROUP = 16
N_FSDP = 32
N_CP = 4
WINDOWS = 4
ROWS = 12
COLS = 24
ROW_BLOCKS = 8
ROW_SPLIT = 2
COL_SPLIT = 4
PATCH = 3
CELLS = ROW_BLOCKS * PATCH * PATCH
WIDE = WINDOWS * COLS
PW_ROWS = 64
POS_ROWS = 48
TABLE_ROWS = PW_ROWS + 2 * POS_ROWS + GROUP
KEPT = PW_ROWS + TABLE_ROWS
GROUPS = TABLE_ROWS // GROUP
SHIFT_ROW = 11
HEAD_TILES = 18
HALF_TILES = HEAD_TILES // 2 * GROUPS
QUARTER = 25
SMALL = 3
RING = 4
NEAR = 8
LAST = NEAR * SMALL
CELL_ROWS = 80
CHUNK = 4 * 96
OWN = D // N_FSDP


def split_2(values):
    high = values.astype(BF16)
    low = (values - high.astype(F32)).astype(BF16)
    return high, low


def place(shape):
    return [lax.broadcasted_iota(jnp.int32, shape, axis) for axis in range(len(shape))]


def token_coefs(cells, fsdp, column):
    group, row_part, col_part = fsdp // 8, fsdp // 4 % 2, fsdp % 4
    cell, lane = place((CELLS, LANES))
    block, inner = cell // 9, cell % 9
    row = block * 6 + row_part * PATCH + inner // PATCH
    col = column * 12 + col_part * PATCH + inner % PATCH
    base = (lane == row) | (lane == POS_ROWS + col)
    base = base | ((lane >= 2 * POS_ROWS + 8) & (lane < 2 * POS_ROWS + SHIFT_ROW))
    coefs = []
    for late in range(2):
        hot = base | (lane == 2 * POS_ROWS + group * 2 + late)
        kept = (lane // PW_ROWS) == late
        coefs.append(
            jnp.concatenate(
                [jnp.where(kept, cells, 0.0), jnp.where(hot, 1.0, 0.0)[:, : KEPT - LANES]],
                axis=1,
            )
        )
    return jnp.concatenate(coefs, axis=0).astype(BF16)


def exchange_kernel(
    video_far,
    conv_far,
    conv_bias_far,
    time_far,
    time_bias_far,
    latent_weight_far,
    latent_bias_far,
    patch_weight_far,
    patch_bias_far,
    frame_pos_far,
    row_pos_far,
    col_pos_far,
    modulation_far,
    weight_far,
    panel_out,
    coefs,
    scales,
    cells_out,
    gram_out,
    tables,
    video_in,
    conv_in,
    time_in,
    weight,
    conv_bias,
    time_bias,
    latent_weight,
    latent_bias,
    patch_bias,
    frame_pos,
    modulation,
    centers,
    left_side,
    parts,
    ring_in,
    blocks,
    near_in,
    last_in,
    pieces,
    lasts,
    gathered,
    folded,
    kernels,
    q0,
    q1,
    q2,
    direct,
    edge_out,
    edge_in,
    padded,
    spread_out,
    staged,
    messages,
    latents_in,
    sums,
    cells,
    token_out,
    local_sems,
    ring_sems,
    near_sems,
    spread_sems,
    last_sems,
    panel_sems,
    edge_send,
    edge_recv,
    tile_sems,
    cell_sems,
):
    me = lax.axis_index("fsdp")
    column = lax.axis_index("cp")
    barrier = pltpu.get_barrier_semaphore()
    z_at, x_at, y_at = lax.div(me, 8), lax.rem(lax.div(me, 4), 2), lax.rem(me, 4)
    plane_at = lax.rem(me, 8)

    def ring_peer(half, step):
        if half == 0:
            return lax.rem(z_at + step, RING) * 8 + plane_at
        return me - y_at + lax.rem(y_at + step, RING)

    def near_at(half):
        return plane_at if half == 0 else z_at * 2 + x_at

    def near_peer(half, step):
        x_to = 1 - x_at if step[0] else x_at
        if half == 0:
            ring_to = lax.rem(y_at + step[1], RING)
            return x_to * RING + ring_to, z_at * 8 + x_to * 4 + ring_to
        ring_to = lax.rem(z_at + step[1], RING)
        return ring_to * 2 + x_to, ring_to * 8 + x_to * 4 + y_at

    near_steps = ((1, 2), (1, 1), (1, 3), (0, 2), (1, 0), (0, 1), (0, 3))

    ring_at = (z_at, y_at)

    def wait_bytes(view, sem):
        pltpu.make_async_copy(view, view, sem).wait()

    pairs = [
        (patch_weight_far, tables.at[pl.ds(PW_ROWS, PW_ROWS)]),
        (row_pos_far, tables.at[pl.ds(2 * PW_ROWS, POS_ROWS)]),
        (col_pos_far, tables.at[pl.ds(2 * PW_ROWS + POS_ROWS, POS_ROWS)]),
        (frame_pos_far, frame_pos),
        (patch_bias_far, patch_bias),
        (modulation_far, modulation),
        (weight_far, weight),
        (latent_weight_far, latent_weight),
        (conv_bias_far, conv_bias),
        (time_bias_far, time_bias),
        (latent_bias_far, latent_bias),
        (time_far, time_in),
        (conv_far, conv_in),
        (video_far, video_in),
        (patch_weight_far, tables.at[pl.ds(0, PW_ROWS)]),
    ]
    loads = [
        pltpu.make_async_copy(source, target, local_sems.at[at])
        for at, (source, target) in enumerate(pairs)
    ]
    for load in loads:
        load.start()

    def greet(step, carry):
        pl.semaphore_signal(
            barrier,
            inc=1,
            device_id={"fsdp": lax.rem(me + step, N_FSDP)},
            device_id_type=MESH,
        )
        return carry

    lax.fori_loop(1, N_FSDP, greet, 0)
    for step in range(1, N_CP):
        pl.semaphore_signal(
            barrier, inc=1, device_id={"cp": (column + step) % N_CP}, device_id_type=MESH
        )
    for load in loads[3:6]:
        load.wait()
    bias = patch_bias[...]
    bias_high = bias.astype(BF16).astype(F32)
    bias_mid = (bias - bias_high).astype(BF16).astype(F32)
    bias_low = bias - bias_high - bias_mid
    eight = lax.broadcasted_iota(jnp.int32, (8, D), 0)
    tail = jnp.where(
        eight == 0,
        bias_high,
        jnp.where(eight == 1, bias_mid, jnp.where(eight == 2, bias_low, 0.0)),
    )
    tables[pl.ds(KEPT - GROUP, GROUP), :] = jnp.concatenate(
        [frame_pos[...].astype(F32), tail], axis=0
    ).astype(BF16)
    start = pl.multiple_of((me // 2) * (2 * OWN), 2 * OWN)
    odd = me % 2 == 1
    own_mod = modulation[:, pl.ds(start, 2 * OWN)]
    own_scale = 1.0 + own_mod[0:1]
    own_shift = own_mod[1:2]

    for group in range(GROUPS):
        at = PW_ROWS + group * GROUP
        if group in (0, 4, 7):
            loads[(0, 4, 7).index(group)].wait()
        whole = tables[pl.ds(at, GROUP), :].astype(F32)
        center = jnp.sum(whole, axis=1, keepdims=True) * (1.0 / D)
        centers[pl.ds(at, GROUP), :] = jnp.broadcast_to(center, (GROUP, LANES))
        block = tables[pl.ds(at, GROUP), pl.ds(start, 2 * OWN)].astype(F32)
        block = (block - center) * own_scale
        if group == GROUPS - 1:
            row = lax.broadcasted_iota(jnp.int32, block.shape, 0)
            block = jnp.where(row == SHIFT_ROW, own_shift, block)
        block = jnp.where(odd, block[:, OWN:], block[:, :OWN])
        high, low = split_2(block)
        left_side[pl.ds(group * GROUP, GROUP), :] = high
        left_side[pl.ds(TABLE_ROWS + group * GROUP, GROUP), :] = low
    loads[6].wait()
    for which in range(3):
        for pair in range(3):
            part = jnp.dot(
                left_side[...],
                weight[which, :, pair * 256 : (pair + 1) * 256],
                preferred_element_type=F32,
            )
            part = part[:TABLE_ROWS] + part[TABLE_ROWS:]
            for half in range(2):
                tile = which * 6 + pair * 2 + half
                at = tile % 9 * GROUPS
                parts[tile // 9, pl.ds(at, GROUPS)] = (
                    part[:, half * LANES : (half + 1) * LANES]
                    .astype(BF16)
                    .reshape(GROUPS, GROUP, LANES)
                )
    parts[:, HALF_TILES:] = jnp.zeros((2, 1, GROUP, LANES), BF16)
    pl.semaphore_wait(barrier, N_FSDP - 1 + N_CP - 1)

    ring_copies = []
    for step in (2, 1, 3):
        for half in range(2):
            target = lax.rem(ring_at[half] + step, RING)
            ring_copies.append(
                pltpu.make_async_remote_copy(
                    src_ref=parts.at[half, pl.ds(target * QUARTER, QUARTER)],
                    dst_ref=ring_in.at[half, RING - 1 - step],
                    send_sem=ring_sems.at[half],
                    recv_sem=ring_sems.at[2 + half],
                    device_id={"fsdp": ring_peer(half, step)},
                    device_id_type=MESH,
                )
            )
    for copy in ring_copies:
        copy.start()

    frame = (me + N_FSDP - 4) % N_FSDP // ROW_BLOCKS
    channel, lane = place((LAT, LANES))
    for load in loads[7:11]:
        load.wait()
    latent_in = latent_weight[...]

    def spread(keep):
        return lax.dot_general(
            latent_in,
            jnp.where(keep, 1.0, 0.0).astype(BF16),
            (((0,), (0,)), ((), ())),
            preferred_element_type=F32,
        ).astype(BF16)

    early_index = jnp.minimum(frame + 1, 2)
    late_index = jnp.maximum(frame - 1, 0)
    early_keep = (frame <= 1) & (lane == channel)
    late_keep = (frame >= 1) & (lane == PW_ROWS + channel)
    loads[11].wait()
    both = jnp.dot(time_in[early_index], spread(early_keep), preferred_element_type=F32)
    both = both + jnp.dot(time_in[late_index], spread(late_keep), preferred_element_type=F32)
    high, low = split_2(both)
    folded[:, :LANES] = high
    folded[:, LANES:] = low
    bias_row = jnp.dot(conv_bias[...], both, precision=HIGHEST, preferred_element_type=F32)
    loads[12].wait()

    def fold(col_shift, carry):
        total = None
        for row_shift in range(3):
            through = jnp.dot(
                conv_in[row_shift, col_shift], folded[...], preferred_element_type=F32
            )
            through = through[:, :LANES] + through[:, LANES:]
            if row_shift:
                through = pltpu.roll(through, row_shift * LAT, 1)
            total = through if total is None else total + through
        high, low = split_2(total)
        kernels[col_shift, :, :LANES] = high
        kernels[col_shift, :, LANES:] = low
        return carry

    lax.fori_loop(0, 3, fold, 0)
    loads[13].wait()

    def convolve(row, carry):
        at = pl.multiple_of(row * CHUNK, CHUNK)
        raw = video_in[pl.ds(at, CHUNK), :]
        wide = raw.astype(F32)
        active = (wide / (1.0 + jnp.exp(-wide))).astype(BF16)
        for col_shift, kept in enumerate((q0, q1, q2)):
            through = jnp.dot(active, kernels[col_shift], preferred_element_type=F32)
            kept[pl.ds(at, CHUNK), :] = through[:, :LANES] + through[:, LANES:]
        plain = jnp.dot(raw, folded[...], preferred_element_type=F32)
        direct[pl.ds(at, CHUNK), :] = plain[:, :LANES] + plain[:, LANES:] + bias_row
        return carry

    lax.fori_loop(0, ROWS * WIDE // CHUNK, convolve, 0)
    lines = ROWS * WINDOWS
    edge_out[0] = q0[pl.ds(COLS - 1, lines, stride=COLS), :]
    edge_out[1] = q2[pl.ds(0, lines, stride=COLS), :]
    edges = [
        pltpu.make_async_remote_copy(
            src_ref=edge_out.at[side],
            dst_ref=edge_in.at[side],
            send_sem=edge_send.at[side],
            recv_sem=edge_recv.at[side],
            device_id={"cp": (column + step) % N_CP},
            device_id_type=MESH,
        )
        for side, step in ((0, 1), (1, N_CP - 1))
    ]
    for edge in edges:
        edge.start()
    for half in range(2):
        wait_bytes(ring_in.at[half], ring_sems.at[2 + half])
        total = parts[half, pl.ds(ring_at[half] * QUARTER, QUARTER)].astype(F32)
        for other in range(RING - 1):
            total = total + ring_in[half, other].astype(F32)
        blocks[half] = total.astype(BF16)
        for slot, step in enumerate(near_steps):
            target, peer = near_peer(half, step)
            pltpu.make_async_remote_copy(
                src_ref=blocks.at[half, pl.ds(target * SMALL, SMALL)],
                dst_ref=near_in.at[half, slot],
                send_sem=near_sems.at[half],
                recv_sem=near_sems.at[2 + half],
                device_id={"fsdp": peer},
                device_id_type=MESH,
            ).start()

            @pl.when(target == 0)
            def _():
                pltpu.make_async_remote_copy(
                    src_ref=blocks.at[half, pl.ds(LAST, 1)],
                    dst_ref=last_in.at[half, slot],
                    send_sem=last_sems.at[half],
                    recv_sem=last_sems.at[2 + half],
                    device_id={"fsdp": peer},
                    device_id_type=MESH,
                ).start()

    empty = jnp.zeros((2 * WIDE, LANES), F32)
    padded[pl.ds(0, 2 * WIDE), :] = empty
    padded[pl.ds((ROWS + 2) * WIDE, 2 * WIDE), :] = empty
    pixel = lax.broadcasted_iota(jnp.int32, (WIDE, LANES), 0) % COLS

    def columns(row, carry):
        at = pl.multiple_of(row * WIDE, WIDE)
        here = pl.ds(at, WIDE)
        total = q1[here, :]
        total = total + jnp.where(pixel == 0, 0.0, pltpu.roll(q0[here, :], 1, 0))
        total = total + jnp.where(pixel == COLS - 1, 0.0, pltpu.roll(q2[here, :], WIDE - 1, 0))
        padded[pl.ds(pl.multiple_of(at + 2 * WIDE, WIDE), WIDE), :] = total
        return carry

    lax.fori_loop(0, ROWS, columns, 0)
    for edge in edges:
        edge.wait()
    first = pl.ds(2 * WIDE, lines, stride=COLS)
    last = pl.ds(2 * WIDE + COLS - 1, lines, stride=COLS)
    padded[first, :] = padded[first, :] + jnp.where(column > 0, edge_in[0], 0.0)
    padded[last, :] = padded[last, :] + jnp.where(column < N_CP - 1, edge_in[1], 0.0)
    own_lanes = lax.broadcasted_iota(jnp.int32, (WIDE, LANES), 1) % PW_ROWS < LAT

    def packed(row, parity):
        total = padded[pl.ds((row + 1) * WIDE, WIDE), :]
        total = total + pltpu.roll(
            padded[pl.ds((row + 2) * WIDE, WIDE), :], LANES - LAT, 1
        )
        total = total + pltpu.roll(
            padded[pl.ds((row + 3) * WIDE, WIDE), :], LANES - 2 * LAT, 1
        )
        if 0 <= row < ROWS:
            total = total + direct[pl.ds(row * WIDE, WIDE), :]
        spread_out[pl.ds(0, WIDE), :] = jnp.where(own_lanes, total, 0.0)
        result = None
        for side in range(2):
            taken = spread_out[pl.ds(side, WIDE // 2, stride=2), :]
            shift = 2 * LAT * parity + LAT * side
            taken = pltpu.roll(taken, shift, 1) if shift else taken
            result = taken if result is None else result + taken
        return result

    def post(values, row_part, at):
        for window in range(WINDOWS):
            for part in range(COL_SPLIT):
                begin = window * COLS // 2 + part * PATCH
                staged[window * 8 + row_part * 4 + part, at : at + PATCH, :] = values[
                    begin : begin + PATCH
                ]

    staged[...] = jnp.zeros(staged.shape, F32)
    for pair in range(ROWS // 2):
        values = packed(2 * pair, 0) + packed(2 * pair + 1, 1)
        post(values, pair // PATCH, pair % PATCH * PATCH)
    post(packed(ROWS, 0), 0, PATCH * PATCH)
    post(packed(-1, 1), 1, PATCH * PATCH)
    messages[...] = staged[...].astype(BF16)
    slot = (me + N_FSDP - 4) % N_FSDP

    def tile_copy(step):
        target = lax.rem(me + step, N_FSDP)
        return pltpu.make_async_remote_copy(
            src_ref=messages.at[target],
            dst_ref=latents_in.at[slot],
            send_sem=tile_sems.at[0],
            recv_sem=tile_sems.at[1],
            device_id={"fsdp": target},
            device_id_type=MESH,
        )

    def send_tile(step, carry):
        tile_copy(step).start()
        return carry

    lax.fori_loop(1, N_FSDP, send_tile, 0)
    latents_in[slot] = messages[me]

    for half in range(2):
        wait_bytes(near_in.at[half], near_sems.at[2 + half])
        total = blocks[half, pl.ds(near_at(half) * SMALL, SMALL)].astype(F32)
        for other in range(NEAR - 1):
            total = total + near_in[half, other].astype(F32)
        pieces[half] = total.astype(BF16)
        for step in near_steps:
            pltpu.make_async_remote_copy(
                src_ref=pieces.at[half],
                dst_ref=gathered.at[half, pl.ds(near_at(half) * SMALL, SMALL)],
                send_sem=spread_sems.at[half],
                recv_sem=spread_sems.at[2 + half],
                device_id={"fsdp": near_peer(half, step)[1]},
                device_id_type=MESH,
            ).start()
        gathered[half, pl.ds(near_at(half) * SMALL, SMALL)] = pieces[half]

        @pl.when(near_at(half) == 0)
        def _():
            wait_bytes(last_in.at[half], last_sems.at[2 + half])
            total = blocks[half, pl.ds(LAST, 1)].astype(F32)
            for other in range(NEAR - 1):
                total = total + last_in[half, other].astype(F32)
            lasts[half] = total.astype(BF16)
            for step in near_steps:
                pltpu.make_async_remote_copy(
                    src_ref=lasts.at[half],
                    dst_ref=gathered.at[half, pl.ds(LAST, 1)],
                    send_sem=last_sems.at[4 + half],
                    recv_sem=last_sems.at[6 + half],
                    device_id={"fsdp": near_peer(half, step)[1]},
                    device_id_type=MESH,
                ).start()
            gathered[half, pl.ds(LAST, 1)] = lasts[half]

    loads[14].wait()
    centers[pl.ds(0, PW_ROWS), :] = centers[pl.ds(PW_ROWS, PW_ROWS), :]
    gram_out[...] = jnp.zeros((KEPT, KEPT), F32)
    both_last = (((1,), (1,)), ((), ()))

    def product(step, carry):
        here = pl.ds(pl.multiple_of(step * 1024, 1024), 1024)
        high, low = split_2(tables[:, here].astype(F32) - centers[:, :1])
        total = lax.dot_general(high, high, both_last, preferred_element_type=F32)
        cross = lax.dot_general(high, low, both_last, preferred_element_type=F32)
        gram_out[...] += (total + 2.0 * cross) * (1.0 / D)
        return carry

    lax.fori_loop(0, D // 1024, product, 0)
    gram_high, gram_low = split_2(gram_out[...])
    panel_copies = []
    for half in range(2):
        wait_bytes(gathered.at[half, pl.ds(0, (NEAR - 1) * SMALL)], spread_sems.at[2 + half])

        @pl.when(near_at(half) != 0)
        def _():
            wait_bytes(gathered.at[half, pl.ds(LAST, 1)], last_sems.at[6 + half])

        at = half * RING * QUARTER + ring_at[half] * QUARTER
        for step in (2, 1, 3):
            panel_copies.append(
                pltpu.make_async_remote_copy(
                    src_ref=gathered.at[half, pl.ds(0, QUARTER)],
                    dst_ref=panel_out.at[pl.ds(at, QUARTER)],
                    send_sem=panel_sems.at[half],
                    recv_sem=panel_sems.at[2 + half],
                    device_id={"fsdp": ring_peer(half, step)},
                    device_id_type=MESH,
                )
            )
        for copy in panel_copies[-3:]:
            copy.start()
    for half in range(2):
        at = half * RING * QUARTER + ring_at[half] * QUARTER
        panel_out[pl.ds(at, QUARTER)] = gathered[half, pl.ds(0, QUARTER)]

    spread_all = spread(lane % LAT == channel).astype(F32)
    offset = jnp.dot(time_bias[...], spread_all, precision=HIGHEST, preferred_element_type=F32)
    offset = offset + jnp.dot(
        latent_bias[...],
        jnp.where(lane % LAT == channel, 1.0, 0.0),
        precision=HIGHEST,
        preferred_element_type=F32,
    )
    wait_bytes(latents_in.at[pl.ds(0, N_FSDP - 1)], tile_sems.at[1])
    for block in range(ROW_BLOCKS):
        total = latents_in[block].astype(F32)
        for other in range(1, FR):
            total = total + latents_in[other * ROW_BLOCKS + block].astype(F32)
        sums[block] = total
    row_part = me // 4 % 2
    upper = jnp.where(row_part == 0, 1.0, 0.0)
    lower = 1.0 - upper
    nine = PATCH * PATCH
    for block in range(ROW_BLOCKS):
        cells[pl.ds(block * nine, nine), :] = sums[block, 0:nine, :]
        if block > 0:
            here = pl.ds(block * nine, PATCH)
            cells[here, :] = cells[here, :] + sums[block - 1, nine : nine + PATCH, :] * upper
        if block < ROW_BLOCKS - 1:
            here = pl.ds(block * nine + 2 * PATCH, PATCH)
            cells[here, :] = cells[here, :] + sums[block + 1, nine : nine + PATCH, :] * lower
    cells[pl.ds(CELLS, CELL_ROWS - CELLS), :] = jnp.zeros((CELL_ROWS - CELLS, LANES), F32)
    token_out[...] = (cells[...] + offset).astype(BF16)
    copies = [
        pltpu.make_async_remote_copy(
            src_ref=token_out,
            dst_ref=cells_out.at[column],
            send_sem=cell_sems.at[0],
            recv_sem=cell_sems.at[1],
            device_id={"cp": (column + step) % N_CP},
            device_id_type=MESH,
        )
        for step in range(1, N_CP)
    ]
    for copy in copies:
        copy.start()
    cells_out[column] = token_out[...]
    others = cells_out.at[pl.ds(0, N_CP - 1)]
    wait_bytes(others, cell_sems.at[1])
    count = 2 * CELLS
    for group in range(N_CP):
        here = pl.ds(group * count, count)
        own = token_coefs(cells_out[group].astype(F32)[:CELLS], me, group)
        coefs[here, :] = own
        through = jnp.dot(own, gram_high, preferred_element_type=F32)
        through = through + jnp.dot(own, gram_low, preferred_element_type=F32)
        power = jnp.sum(through * own.astype(F32), axis=1, keepdims=True)
        scale = lax.rsqrt(jnp.maximum(power, 0.0) + 1e-06)
        scales[here, :] = jnp.broadcast_to(scale, (count, LANES))
    sent = panel_out.at[pl.ds(0, (RING - 1) * QUARTER)]
    for half in range(2):
        wait_bytes(sent, panel_sems.at[2 + half])
    wait_bytes(others, cell_sems.at[0])
    wait_bytes(latents_in.at[pl.ds(0, N_FSDP - 1)], tile_sems.at[0])
    for half in range(2):
        wait_bytes(ring_in.at[half], ring_sems.at[half])
        wait_bytes(near_in.at[half], near_sems.at[half])
        wait_bytes(gathered.at[half, pl.ds(0, (NEAR - 1) * SMALL)], spread_sems.at[half])
        wait_bytes(sent, panel_sems.at[half])

        @pl.when(near_at(half) == 0)
        def _():
            wait_bytes(last_in.at[half], last_sems.at[4 + half])

        @pl.when(near_at(half) != 0)
        def _():
            wait_bytes(last_in.at[half, 0], last_sems.at[half])


def exchange(*args):
    whole = pl.BlockSpec(memory_space=pltpu.VMEM)
    apart = pl.BlockSpec(memory_space=pltpu.HBM)
    pixels = ROWS * WIDE
    tokens = N_CP * 2 * CELLS
    return pl.pallas_call(
        exchange_kernel,
        out_shape=(
            jax.ShapeDtypeStruct((2 * RING * QUARTER, GROUP, LANES), BF16),
            jax.ShapeDtypeStruct((tokens, KEPT), BF16),
            jax.ShapeDtypeStruct((tokens, LANES), F32),
        ),
        in_specs=[apart] * len(args),
        out_specs=(whole, whole, whole),
        scratch_shapes=[
            pltpu.VMEM((N_CP, CELL_ROWS, LANES), BF16),
            pltpu.VMEM((KEPT, KEPT), F32),
            pltpu.VMEM((KEPT, D), BF16),
            pltpu.VMEM((pixels, C), BF16),
            pltpu.VMEM((3, 3, C, C), BF16),
            pltpu.VMEM((3, C, C), BF16),
            pltpu.VMEM((3, OWN, 6 * LANES), BF16),
            pltpu.VMEM((1, C), F32),
            pltpu.VMEM((1, C), F32),
            pltpu.VMEM((LAT, C), BF16),
            pltpu.VMEM((1, LAT), F32),
            pltpu.VMEM((1, D), F32),
            pltpu.VMEM((8, D), BF16),
            pltpu.VMEM((2, D), F32),
            pltpu.VMEM((KEPT, LANES), F32),
            pltpu.VMEM((2 * TABLE_ROWS, OWN), BF16),
            pltpu.VMEM((2, RING * QUARTER, GROUP, LANES), BF16),
            pltpu.VMEM((2, RING - 1, QUARTER, GROUP, LANES), BF16),
            pltpu.VMEM((2, QUARTER, GROUP, LANES), BF16),
            pltpu.VMEM((2, NEAR - 1, SMALL, GROUP, LANES), BF16),
            pltpu.VMEM((2, NEAR - 1, 1, GROUP, LANES), BF16),
            pltpu.VMEM((2, SMALL, GROUP, LANES), BF16),
            pltpu.VMEM((2, 1, GROUP, LANES), BF16),
            pltpu.VMEM((2, QUARTER, GROUP, LANES), BF16),
            pltpu.VMEM((C, 2 * LANES), BF16),
            pltpu.VMEM((3, C, 2 * LANES), BF16),
            pltpu.VMEM((pixels + COLS, LANES), F32),
            pltpu.VMEM((pixels + COLS, LANES), F32),
            pltpu.VMEM((pixels + COLS, LANES), F32),
            pltpu.VMEM((pixels + COLS, LANES), F32),
            pltpu.VMEM((2, ROWS * WINDOWS, LANES), F32),
            pltpu.VMEM((2, ROWS * WINDOWS, LANES), F32),
            pltpu.VMEM(((ROWS + 4) * WIDE, LANES), F32),
            pltpu.VMEM((WIDE + 8, LANES), F32),
            pltpu.VMEM((N_FSDP, GROUP, LANES), F32),
            pltpu.VMEM((N_FSDP, GROUP, LANES), BF16),
            pltpu.VMEM((N_FSDP, GROUP, LANES), BF16),
            pltpu.VMEM((ROW_BLOCKS, GROUP, LANES), F32),
            pltpu.VMEM((CELL_ROWS, LANES), F32),
            pltpu.VMEM((CELL_ROWS, LANES), BF16),
            pltpu.SemaphoreType.DMA((15,)),
            pltpu.SemaphoreType.DMA((4,)),
            pltpu.SemaphoreType.DMA((4,)),
            pltpu.SemaphoreType.DMA((4,)),
            pltpu.SemaphoreType.DMA((8,)),
            pltpu.SemaphoreType.DMA((4,)),
            pltpu.SemaphoreType.DMA((2,)),
            pltpu.SemaphoreType.DMA((2,)),
            pltpu.SemaphoreType.DMA((2,)),
            pltpu.SemaphoreType.DMA((2,)),
        ],
        compiler_params=pltpu.CompilerParams(
            collective_id=0, has_side_effects=True, vmem_limit_bytes=48 * 1024 * 1024
        ),
    )(*[pltpu.with_memory_space_constraint(arg, pltpu.HBM) for arg in args])


def project_kernel(
    panel, coefs, scales, gain, query, keys, values, stacked, results, result_sems
):
    count = 2 * CELLS
    writes = []
    for which, out in ((2, values), (0, query), (1, keys)):
        pairs = []
        for pair in range(3):
            sides = []
            for head in range(which * 6 + pair * 2, which * 6 + pair * 2 + 2):
                rows = panel[pl.ds(head // (HEAD_TILES // 2) + head * GROUPS, GROUPS)]
                sides.append(rows.reshape(TABLE_ROWS, LANES))
            both = jnp.concatenate(sides, axis=1)
            stacked[pair, pl.ds(0, PW_ROWS)] = both[:PW_ROWS]
            stacked[pair, pl.ds(PW_ROWS, TABLE_ROWS)] = both
            tail_rows = both[TABLE_ROWS - GROUP :].astype(F32)
            pairs.append(tail_rows[SHIFT_ROW : SHIFT_ROW + 1])
        for group in range(N_CP):
            here = pl.ds(group * count, count)
            for pair, shift in enumerate(pairs):
                projected = jnp.dot(
                    coefs[here, :], stacked[pair], preferred_element_type=F32
                )
                for half in range(2):
                    side = slice(half * LANES, (half + 1) * LANES)
                    to = (pair * 2 + half) * LANES
                    part = projected[:, side] * scales[here, :] + shift[:, side]
                    if which < 2:
                        power = jnp.sum(part * part, axis=1, keepdims=True) * (1.0 / HD)
                        part = part * lax.rsqrt(power + 1e-06)
                        part = part * gain[which : which + 1, to : to + LANES]
                    results[which, here, to : to + LANES] = part.astype(BF16)
            write = pltpu.make_async_copy(
                results.at[which, here], out.at[here], result_sems.at[which, group]
            )
            write.start()
            writes.append(write)
    for write in writes:
        write.wait()


def project(panel, coefs, scales, gain):
    tokens = coefs.shape[0]
    out = jax.ShapeDtypeStruct((tokens, gain.shape[1]), BF16)
    return pl.pallas_call(
        project_kernel,
        out_shape=(out, out, out),
        in_specs=[pl.BlockSpec(memory_space=pltpu.VMEM)] * 4,
        out_specs=(pl.BlockSpec(memory_space=pltpu.HBM),) * 3,
        scratch_shapes=[
            pltpu.VMEM((3, KEPT, 2 * LANES), BF16),
            pltpu.VMEM((3, tokens, gain.shape[1]), BF16),
            pltpu.SemaphoreType.DMA((3, N_CP)),
        ],
        compiler_params=pltpu.CompilerParams(vmem_limit_bytes=32 * 1024 * 1024),
    )(panel, coefs, scales, gain)


def body(
    video,
    conv_weight,
    conv_bias,
    time_weight,
    time_bias,
    latent_weight,
    latent_bias,
    patch_weight,
    patch_bias,
    frame_pos,
    row_pos,
    col_pos,
    modulation,
    qkv_weight,
    qk_gain,
):
    panel, coefs, scales = exchange(
        video.reshape(-1, C),
        conv_weight,
        conv_bias.reshape(1, -1),
        time_weight,
        time_bias.reshape(1, -1),
        latent_weight.T,
        latent_bias.reshape(1, -1),
        patch_weight,
        patch_bias.reshape(1, -1),
        frame_pos,
        row_pos,
        col_pos,
        modulation,
        qkv_weight,
    )
    return project(panel, coefs, scales, qk_gain)


def solution(mesh):
    return jax.shard_map(
        body,
        mesh=mesh,
        in_specs=(
            P("fsdp", None, "cp", None),
            P(),
            P(),
            P(),
            P(),
            P(),
            P(),
            P(),
            P(),
            P(),
            P(),
            P(),
            P(),
            P(None, "fsdp", "cp"),
            P(None, "cp"),
        ),
        out_specs=(P("fsdp", "cp"), P("fsdp", "cp"), P("fsdp", "cp")),
        check_vma=False,
    )
```
